128 devices in a mesh: dp: 8 (over x_lo, y), fsdp: 16 (over x_hi, z, core).
Axes of the slice: x: 4 (x_hi: 2, x_lo: 2; x = x_hi * 2 + x_lo), y: 4, z: 4, core: 2. Of those that a mesh axis runs over, the one named last changes fastest.
Arguments:
- tokens: bfloat16 [8, 4096, 1024], P('dp', 'fsdp'), may hold values from -6 to 6
- cotangent: bfloat16 [8, 4096, 1024], P('dp', 'fsdp'), may hold values from -6 to 6
- qkv_weight: float32 [1024, 3072], P('fsdp'), may hold values from -0.1875 to 0.1875
- dense_weight: float32 [1024, 1024], P('fsdp'), may hold values from -0.75 to 0.75
- fc1_weight: float32 [1024, 4096], P('fsdp'), may hold values from -0.1875 to 0.1875
- fc2_weight: float32 [4096, 1024], P('fsdp'), may hold values from -0.09375 to 0.09375
- vectors: float32 [11, 1024], P(None, 'fsdp'), may hold values from -1.2 to 1.5, as said below
- qkv_first: float32 [1024, 3072], P('fsdp'), may hold values from -256 to 256
- dense_first: float32 [1024, 1024], P('fsdp'), may hold values from -32 to 32
- fc1_first: float32 [1024, 4096], P('fsdp'), may hold values from -32 to 32
- fc2_first: float32 [4096, 1024], P('fsdp'), may hold values from -64 to 64
- vectors_first: float32 [11, 1024], P(None, 'fsdp'), may hold values from -128 to 128
- qkv_second: float32 [1024, 3072], P('fsdp'), may hold values from 6553.6 to 26214.4
- dense_second: float32 [1024, 1024], P('fsdp'), may hold values from 147.456 to 589.824
- fc1_second: float32 [1024, 4096], P('fsdp'), may hold values from 147.456 to 589.824
- fc2_second: float32 [4096, 1024], P('fsdp'), may hold values from 589.824 to 2359.296
- vectors_second: float32 [11, 1024], P(None, 'fsdp'), may hold values from 1638.4 to 6553.6
Outputs:
- output: bfloat16 [8, 4096, 1024], P('dp', 'fsdp')
- input_grad: bfloat16 [8, 4096, 1024], P('dp', 'fsdp')
- qkv_new: float32 [1024, 3072], P('fsdp')
- dense_new: float32 [1024, 1024], P('fsdp')
- fc1_new: float32 [1024, 4096], P('fsdp')
- fc2_new: float32 [4096, 1024], P('fsdp')
- vectors_new: float32 [11, 1024], P(None, 'fsdp')
- qkv_first_new: float32 [1024, 3072], P('fsdp')
- dense_first_new: float32 [1024, 1024], P('fsdp')
- fc1_first_new: float32 [1024, 4096], P('fsdp')
- fc2_first_new: float32 [4096, 1024], P('fsdp')
- vectors_first_new: float32 [11, 1024], P(None, 'fsdp')
- qkv_second_new: float32 [1024, 3072], P('fsdp')
- dense_second_new: float32 [1024, 1024], P('fsdp')
- fc1_second_new: float32 [1024, 4096], P('fsdp')
- fc2_second_new: float32 [4096, 1024], P('fsdp')
- vectors_second_new: float32 [11, 1024], P(None, 'fsdp')
The draws below stay inside these ranges and needn't reach their ends.
Inputs may be any that keep to these rules, and one draw needn't show every extreme that they name: `vectors`: rows 0 to 8 and 10 are biases, row 9 is the norm's gain between 0.5 and 1.5.
All inputs are finite; a program needn't handle non-finite values.
Results may differ from the reference program's by a relative error of at most 0.024.
Values may be sent and summed in bfloat16 or wider, within the bound.
No kernel may reach another device: no remote copies, remote signals or barrier semaphores. Data moves between devices by JAX's collectives and lax.ppermute only.
A program may use at most 192 MiB of HBM per device.

```python
import math
import jax
import jax.numpy as jnp
from jax import lax

D = 1024
HEAD = 64
ROT = 32
FF = 4096
VEC = 11
STEP = 10
SEQS = 8
LENGTH = 4096
TOKEN_COUNT = 32768


def draw_vectors(key, part):
    key = jax.random.fold_in(key, 5)
    key_bias, key_gain = jax.random.split(key)
    biases = jnp.clip(jax.random.normal(key_bias, (VEC, D), jnp.float32) * 0.3, -1.2, 1.2)
    gains = jax.random.uniform(key_gain, (VEC, D), jnp.float32, 0.5, 1.5)
    row_index = jnp.arange(VEC, dtype=jnp.int32)[:, None]
    return jnp.where(row_index == 9, gains, biases)


def level_of(stream_key, shape, cuts, smallest, top_value):
    def one(dim, parts):
        steps = jax.random.uniform(jax.random.fold_in(jax.random.fold_in(stream_key, 6), dim), (parts,), jnp.float32, smallest / len(cuts), top_value / len(cuts))
        return jnp.repeat(jnp.exp(steps), shape[dim] // parts).reshape((-1,) + (1,) * (len(shape) - dim - 1))

    level = one(*cuts[0])
    for cut in cuts[1:]:
        level = level * one(*cut)
    return level


def scatter_about(key, shape, deviation, most, shards=(), kind=jnp.bfloat16):
    loudness = level_of(key, shape, shards, -0.22, 0.18) if shards else 1.0
    drawn = jax.random.normal(key, shape, jnp.float32) * deviation * loudness
    return jnp.minimum(jnp.maximum(drawn, -most), most).astype(kind)


def setup_inputs(seed: int = 0) -> dict:
    key_of = jax.random.split(jax.random.key(seed), 18)
    return {
        "tokens": scatter_about(key_of[0], (SEQS, LENGTH, D), 1.0, 6.0, ((0, 8), (1, 16))),
        "cotangent": scatter_about(key_of[1], (SEQS, LENGTH, D), 1.0, 6.0, ((0, 8), (1, 16))),
        "qkv_weight": scatter_about(key_of[2], (D, 3 * D), D ** -0.5, 0.1875, ((0, 16),), jnp.float32),
        "dense_weight": scatter_about(key_of[3], (D, D), (D // 16) ** -0.5, 0.75, ((0, 16),), jnp.float32),
        "fc1_weight": scatter_about(key_of[4], (D, FF), D ** -0.5, 0.1875, ((0, 16),), jnp.float32),
        "fc2_weight": scatter_about(key_of[5], (FF, D), FF ** -0.5, 0.09375, ((0, 16),), jnp.float32),
        "vectors": draw_vectors(jax.random.fold_in(key_of[17], 71), 0),
        "qkv_first": scatter_about(key_of[7], (D, 3 * D), (0.22 * TOKEN_COUNT ** 0.5), 256.0, ((0, 16),), jnp.float32),
        "dense_first": scatter_about(key_of[8], (D, D), (0.033 * TOKEN_COUNT ** 0.5), 32.0, ((0, 16),), jnp.float32),
        "fc1_first": scatter_about(key_of[9], (D, FF), (0.033 * TOKEN_COUNT ** 0.5), 32.0, ((0, 16),), jnp.float32),
        "fc2_first": scatter_about(key_of[10], (FF, D), (0.066 * TOKEN_COUNT ** 0.5), 64.0, ((0, 16),), jnp.float32),
        "vectors_first": scatter_about(key_of[11], (VEC, D), (0.11 * TOKEN_COUNT ** 0.5), 128.0, ((1, 16),), jnp.float32),
        "qkv_second": jnp.clip(jnp.exp(math.log(26214.4) - 1.3862944 * jax.random.uniform(key_of[12], (D, 3 * D), jnp.float32) ** level_of(key_of[12], (D, 3 * D), ((0, 16),), -0.2, 0.2)), 6553.6, 26214.4),
        "dense_second": jnp.clip(jnp.exp(math.log(589.824) - 1.3862944 * jax.random.uniform(key_of[13], (D, D), jnp.float32) ** level_of(key_of[13], (D, D), ((0, 16),), -0.2, 0.2)), 147.456, 589.824),
        "fc1_second": jnp.clip(jnp.exp(math.log(589.824) - 1.3862944 * jax.random.uniform(key_of[14], (D, FF), jnp.float32) ** level_of(key_of[14], (D, FF), ((0, 16),), -0.2, 0.2)), 147.456, 589.824),
        "fc2_second": jnp.clip(jnp.exp(math.log(2359.296) - 1.3862944 * jax.random.uniform(key_of[15], (FF, D), jnp.float32) ** level_of(key_of[15], (FF, D), ((0, 16),), -0.2, 0.2)), 589.824, 2359.296),
        "vectors_second": jnp.clip(jnp.exp(math.log(6553.6) - 1.3862944 * jax.random.uniform(key_of[16], (VEC, D), jnp.float32) ** level_of(key_of[16], (VEC, D), ((1, 16),), -0.2, 0.2)), 1638.4, 6553.6),
    }


@jax.custom_vjp
def low(v):
    return lax.optimization_barrier(v.astype(jnp.bfloat16)).astype(jnp.float32)

@jax.custom_vjp
def low_back(v):
    return v

def low_keep(v):
    return (low(v), None)

def low_pass(kept, grad):
    return (grad,)

def back_keep(v):
    return (v, None)

def back_low(kept, grad):
    return (low(grad),)
low.defvjp(low_keep, low_pass)
low_back.defvjp(back_keep, back_low)
SCORE_SCALE = 0.125
HIGH = lax.Precision.HIGHEST

def tables(positions):
    freqs = 10000.0 ** (-(jnp.arange(ROT // 2, dtype=jnp.float32) * 2.0) / ROT)
    angles = positions.astype(jnp.float32)[:, None] * freqs[None, :]
    return (jnp.cos(angles), jnp.sin(angles))

def rotate(cosine, sine, values):
    half_rot = ROT // 2
    first = values[..., :half_rot]
    second = values[..., half_rot:ROT]
    others = values[..., ROT:]
    cos_b = cosine[:, None, :]
    sin_b = sine[:, None, :]
    return jnp.concatenate([first * cos_b - second * sin_b, second * cos_b + first * sin_b, others], -1)

def normalize(values):
    middle = lax.optimization_barrier(jnp.mean(values, -1, keepdims=True))
    centered = values - middle
    spread = lax.optimization_barrier(jnp.mean(centered * centered, -1, keepdims=True))
    inverse = lax.rsqrt(spread + 1e-05)
    return (centered * inverse, inverse)

def unpack(packed):
    return (packed[0:3].reshape(-1), packed[3], packed[4:8].reshape(-1), packed[8], packed[9], packed[10])

def gelu_new(values):
    return jax.nn.gelu(values, approximate=True)

def attend_block(query_block, start, keys, values):
    query_count = query_block.shape[0]
    key_count = keys.shape[0]
    raw = low_back(jnp.einsum('qhd,khd->hqk', query_block, keys, precision=HIGH))
    scores = raw * SCORE_SCALE
    query_pos = start + jnp.arange(query_count, dtype=jnp.int32)
    key_pos = jnp.arange(key_count, dtype=jnp.int32)
    mask = (query_pos[:, None] >= key_pos[None, :])[None]
    scores = jnp.where(mask, scores, -1e+30)
    highest = lax.optimization_barrier(jnp.max(scores, -1, keepdims=True))
    expo = jnp.where(mask, jnp.exp(scores - highest), 0.0)
    probs = low(expo / lax.optimization_barrier(jnp.sum(expo, -1, keepdims=True)))
    return jnp.einsum('hqk,khd->qhd', probs, values, precision=HIGH)

def layer(inputs, qkv_weight, dense_weight, fc1_weight, fc2_weight, vectors, cosine, sine):
    length_all = inputs.shape[0]
    width_all = inputs.shape[1]
    head_count = width_all // HEAD
    bias_qkv, bias_dense, bias_up, bias_down, gain, shift = unpack(low(vectors))
    normed, inverse = normalize(inputs)
    hidden = low(normed * gain + shift)
    mixed = low_back(jnp.dot(hidden, low(qkv_weight), precision=HIGH) + bias_qkv)
    queries = low(rotate(cosine, sine, mixed[:, :width_all].reshape(length_all, head_count, HEAD)))
    keys = low(rotate(cosine, sine, mixed[:, width_all:2 * width_all].reshape(length_all, head_count, HEAD)))
    values = low(mixed[:, 2 * width_all:].reshape(length_all, head_count, HEAD))
    block_size = min(512, length_all)
    block_count = length_all // block_size
    query_blocks = queries.reshape(block_count, block_size, head_count, HEAD)
    starts = jnp.arange(block_count, dtype=jnp.int32) * block_size
    checked = jax.checkpoint(attend_block)
    attended = lax.map(lambda pair: checked(pair[0], pair[1], keys, values), (query_blocks, starts))
    attended = low(low_back(attended.reshape(length_all, width_all)))
    attn_out = jnp.dot(attended, low(dense_weight), precision=HIGH) + bias_dense
    upper = low_back(jnp.dot(hidden, low(fc1_weight), precision=HIGH) + bias_up)
    active = low(gelu_new(upper))
    mlp_out = jnp.dot(active, low(fc2_weight), precision=HIGH) + bias_down
    return inputs + attn_out + mlp_out

def adamw(master, grad, first, second, rate):
    first_new = 0.9 * first + 0.1 * grad
    second_new = 0.95 * second + 0.05 * grad * grad
    first_hat = first_new / (1.0 - 0.9 ** STEP)
    second_hat = second_new / (1.0 - 0.95 ** STEP)
    fresh = master - rate * (first_hat / (jnp.sqrt(second_hat) + 1e-08) + 0.1 * master)
    return (fresh, first_new, second_new)

def reference(tokens, cotangent, qkv_weight, dense_weight, fc1_weight, fc2_weight, vectors, qkv_first, dense_first, fc1_first, fc2_first, vectors_first, qkv_second, dense_second, fc1_second, fc2_second, vectors_second):
    masters = (qkv_weight, dense_weight, fc1_weight, fc2_weight, vectors)
    positions = jnp.arange(LENGTH, dtype=jnp.int32)
    cosine, sine = tables(positions)

    def forward(inputs, wqkv, wdense, wup, wdown, packed):
        return layer(inputs, wqkv, wdense, wup, wdown, packed, cosine, sine)

    def one_sequence(carry, pair):
        seq_in, seq_cot = pair
        result, pull = jax.vjp(forward, seq_in.astype(jnp.float32), *masters)
        grads = pull(seq_cot.astype(jnp.float32))
        carry = tuple((total + piece for total, piece in zip(carry, grads[1:])))
        return (carry, (result.astype(jnp.bfloat16), grads[0].astype(jnp.bfloat16)))
    start_sums = tuple((jnp.zeros_like(item) for item in masters))
    totals, (outputs, input_grads) = lax.scan(one_sequence, start_sums, (tokens, cotangent))
    firsts = (qkv_first, dense_first, fc1_first, fc2_first, vectors_first)
    seconds = (qkv_second, dense_second, fc1_second, fc2_second, vectors_second)
    rates = (2.0 * D ** (-0.5), 2.0 * D ** (-0.5), 2.0 * D ** (-0.5), 2.0 * FF ** (-0.5), 0.3)
    updated = [adamw(masters[index], totals[index], firsts[index], seconds[index], rates[index]) for index in range(5)]
    return (outputs, input_grads, updated[0][0], updated[1][0], updated[2][0], updated[3][0], updated[4][0], updated[0][1], updated[1][1], updated[2][1], updated[3][1], updated[4][1], updated[0][2], updated[1][2], updated[2][2], updated[3][2], updated[4][2])
```

```python
import functools

import jax
import jax.numpy as jnp
from jax import lax
from jax.experimental import pallas as pl
from jax.experimental.pallas import tpu as pltpu
from jax.sharding import Mesh
from jax.sharding import PartitionSpec as P

D = 1024
HEAD = 64
ROT = 32
FF = 4096
STEP = 10
S = 4096
NEG = -1e30
F32 = jnp.float32
BF = jnp.bfloat16


def dot(a, b, dims=((1,), (0,))):
    return lax.dot_general(a, b, (dims, ((), ())), preferred_element_type=F32)


def place(piece, z, c):
    inner = piece % 8
    k = lax.rem(inner // 2 - z + 4, 4)
    s = lax.rem(inner % 2 + c, 2)
    return pl.multiple_of((s * 4 + k) * 256, 256)


def load_pieces(ids, own, oth, dst):
    h, z, c = ids[0], ids[1], ids[2]
    for piece in range(16):
        off = place(piece, z, c)
        mine = (piece // 8) == h

        @pl.when(mine)
        def _():
            dst[:, piece * 256 : (piece + 1) * 256] = own[:, pl.ds(off, 256)]

        @pl.when(jnp.logical_not(mine))
        def _():
            dst[:, piece * 256 : (piece + 1) * 256] = oth[:, pl.ds(off, 256)]


def store_pieces(ids, src, own, away):
    h, z, c = ids[0], ids[1], ids[2]
    for piece in range(16):
        off = place(piece, z, c)
        mine = (piece // 8) == h

        @pl.when(mine)
        def _():
            own[:, pl.ds(off, 256)] = src[:, piece * 256 : (piece + 1) * 256].astype(own.dtype)

        @pl.when(jnp.logical_not(mine))
        def _():
            away[:, pl.ds(off, 256)] = src[:, piece * 256 : (piece + 1) * 256].astype(own.dtype)


def causal(koff, qoff, shape):
    kp = koff + lax.broadcasted_iota(jnp.int32, shape, 0)
    qp = qoff + lax.broadcasted_iota(jnp.int32, shape, 1)
    return kp <= qp


def attend_kernel(BQ, BK, ids, own, oth, o_full, lse, o_own, o_away, qkv, kk):
    load_pieces(ids, own, oth, qkv)
    for j in range(8):
        sl = slice(j * 512, (j + 1) * 512)
        kk[sl, :] = qkv[64:128, sl].T

    def q_block(qi, unused):
        qoff = pl.multiple_of(qi * BQ, BQ)
        qT = qkv[0:64, pl.ds(qoff, BQ)] * jnp.asarray(0.125, BF)

        def step(kj, carry, masked):
            m, l, acc = carry
            koff = pl.multiple_of(kj * BK, BK)
            s = dot(kk[pl.ds(koff, BK), :], qT)
            if masked:
                s = jnp.where(causal(koff, qoff, (BK, BQ)), s, NEG)
            m2 = jnp.maximum(m, jnp.max(s, 0, keepdims=True))
            p = jnp.exp(s - m2)
            a = jnp.exp(m - m2)
            l = l * a + jnp.sum(p, 0, keepdims=True)
            acc = acc * a + dot(qkv[128:192, pl.ds(koff, BK)], p.astype(BF))
            return m2, l, acc

        n = qoff // BK
        carry = (jnp.full((1, BQ), NEG, F32), jnp.zeros((1, BQ), F32), jnp.zeros((64, BQ), F32))
        carry = lax.fori_loop(0, n, lambda j, cc: step(j, cc, False), carry)
        m, l, acc = step(n, carry, True)
        o_full[:, pl.ds(qoff, BQ)] = acc / l
        lse[:, pl.ds(qoff, BQ)] = m + jnp.log(l)
        return unused

    lax.fori_loop(0, S // BQ, q_block, 0)
    store_pieces(ids, o_full, o_own, o_away)


VM = pl.BlockSpec(memory_space=pltpu.VMEM)
SM = pl.BlockSpec(memory_space=pltpu.SMEM)


def attend(ids, own, oth, BQ=1024, BK=1024):
    return pl.pallas_call(
        functools.partial(attend_kernel, BQ, BK),
        out_shape=(
            jax.ShapeDtypeStruct((64, S), F32),
            jax.ShapeDtypeStruct((1, S), F32),
            jax.ShapeDtypeStruct((64, S // 2), BF),
            jax.ShapeDtypeStruct((64, S // 2), BF),
        ),
        in_specs=[SM, VM, VM],
        out_specs=(VM,) * 4,
        scratch_shapes=[pltpu.VMEM((192, S), BF), pltpu.VMEM((S, 64), BF)],
        compiler_params=pltpu.CompilerParams(vmem_limit_bytes=56 << 20),
        cost_estimate=pl.CostEstimate(
            flops=8 * S * S * 64, bytes_accessed=4 << 20, transcendentals=S * S // 2
        ),
        name="attend",
    )(ids, own, oth)


def unrotate(d, cos, sin):
    a, b = d[0:16], d[16:32]
    return jnp.concatenate([a * cos + b * sin, b * cos - a * sin, d[32:64]], 0)


def attend_back_kernel(
    BQ, BK, ids, own, oth, do_own, do_oth, o_full, lse, cos, sin, d_own, d_away,
    qkv, kk, vv, qq, doT, dd, dq, dk, dv,
):
    load_pieces(ids, own, oth, qkv)
    load_pieces(ids, do_own, do_oth, doT)
    for j in range(8):
        sl = slice(j * 512, (j + 1) * 512)
        qkv[0:64, sl] = qkv[0:64, sl] * jnp.asarray(0.125, BF)
        qq[sl, :] = qkv[0:64, sl].T
        kk[sl, :] = qkv[64:128, sl].T
        vv[sl, :] = qkv[128:192, sl].T
        dd[sl, :] = doT[:, sl].T
    dk[...] = jnp.zeros_like(dk)
    dv[...] = jnp.zeros_like(dv)

    def q_block(qi, unused):
        qoff = pl.multiple_of(qi * BQ, BQ)
        qs = pl.ds(qoff, BQ)
        qT = qkv[0:64, qs]
        gT = doT[:, qs]
        delta = jnp.sum(gT.astype(F32) * o_full[:, qs], 0, keepdims=True)
        ls = lse[:, qs]

        def step(kj, acc, masked):
            koff = pl.multiple_of(kj * BK, BK)
            ks = pl.ds(koff, BK)
            s = dot(kk[ks, :], qT)
            if masked:
                s = jnp.where(causal(koff, qoff, (BK, BQ)), s, NEG)
            p = jnp.exp(s - ls)
            ds = (p * (dot(vv[ks, :], gT) - delta)).astype(BF)
            dv[ks, :] += dot(p.astype(BF), dd[qs, :])
            dk[ks, :] += dot(ds, qq[qs, :])
            return acc + dot(qkv[64:128, ks], ds)

        n = qoff // BK
        acc = lax.fori_loop(0, n, lambda j, a: step(j, a, False), jnp.zeros((64, BQ), F32))
        acc = step(n, acc, True) * 0.125
        dq[0:64, qs] = unrotate(acc, cos[:, qs], sin[:, qs]).astype(BF)
        return unused

    lax.fori_loop(0, S // BQ, q_block, 0)
    for j in range(8):
        sl = slice(j * 512, (j + 1) * 512)
        dq[64:128, sl] = unrotate(dk[sl, :].T, cos[:, sl], sin[:, sl]).astype(BF)
        dq[128:192, sl] = dv[sl, :].T.astype(BF)
    store_pieces(ids, dq, d_own, d_away)


def attend_back(ids, own, oth, do_own, do_oth, o_full, lse, cos, sin, BQ=1024, BK=1024):
    return pl.pallas_call(
        functools.partial(attend_back_kernel, BQ, BK),
        out_shape=(jax.ShapeDtypeStruct((192, S // 2), BF),) * 2,
        in_specs=[SM] + [VM] * 8,
        out_specs=(VM,) * 2,
        scratch_shapes=[
            pltpu.VMEM((192, S), BF),
            pltpu.VMEM((S, 64), BF),
            pltpu.VMEM((S, 64), BF),
            pltpu.VMEM((S, 64), BF),
            pltpu.VMEM((64, S), BF),
            pltpu.VMEM((S, 64), BF),
            pltpu.VMEM((192, S), BF),
            pltpu.VMEM((S, 64), F32),
            pltpu.VMEM((S, 64), F32),
        ],
        compiler_params=pltpu.CompilerParams(vmem_limit_bytes=56 << 20),
        cost_estimate=pl.CostEstimate(
            flops=20 * S * S * 64, bytes_accessed=6 << 20, transcendentals=S * S // 2
        ),
        name="attend_back",
    )(ids, own, oth, do_own, do_oth, o_full, lse, cos, sin)


SWAP = [(0, 1), (1, 0)]
GROUP = ("z", "core")
BATCH = ("xlo", "y")


def swap_core(v):
    return lax.ppermute(v, "core", SWAP)


def swap_x(v):
    return lax.ppermute(v, "xhi", SWAP)


def from_z(v, k):
    return lax.ppermute(v, "z", [(i, (i - k) % 4) for i in range(4)])


def gather_tokens(v):
    mine = [v] + [from_z(v, k) for k in (1, 3, 2)]
    mine = [mine[0], mine[1], mine[3], mine[2]]
    return jnp.concatenate(mine + [swap_core(b) for b in mine], 0)


def scatter_sum(v):
    half = v.shape[0] // 2
    theirs = swap_core(v[half:])
    mine = (v[:half].astype(F32) + theirs.astype(F32)).astype(BF)
    blocks = mine.reshape(4, half // 4, v.shape[1])
    total = blocks[0].astype(F32)
    for k in (2, 1, 3):
        total = total + from_z(blocks[k], -k).astype(F32)
    return total


def halves_swapped(v, axis):
    n = v.shape[axis] // 2
    lo = lax.slice_in_dim(v, 0, n, axis=axis)
    hi = lax.slice_in_dim(v, n, 2 * n, axis=axis)
    return jnp.concatenate([hi, lo], axis)


def sum_batch(v):
    rows, columns = v.shape
    parts = lax.all_to_all(v.astype(BF).reshape(8, rows // 8, columns), BATCH, 0, 0, tiled=True)
    piece = jnp.sum(parts.astype(F32), 0).astype(BF)
    spread = jnp.broadcast_to(piece[None], (8,) + piece.shape)
    return lax.all_to_all(spread, BATCH, 0, 0, tiled=True).reshape(rows, columns)


def normalize(values):
    middle = jnp.mean(values, -1, keepdims=True)
    centered = values - middle
    spread = jnp.mean(centered * centered, -1, keepdims=True)
    inverse = lax.rsqrt(spread + 1e-05)
    return (centered * inverse, inverse)


def gelu_new(values):
    return jax.nn.gelu(values, approximate=True)


def tables(positions):
    freqs = 10000.0 ** (-(jnp.arange(ROT // 2, dtype=F32) * 2.0) / ROT)
    angles = positions.astype(F32)[None, :] * freqs[:, None]
    return (jnp.cos(angles), jnp.sin(angles))


def rotate(cos, sin, mixed):
    out = []
    for n in (0, 64):
        a, b = mixed[n : n + 16], mixed[n + 16 : n + 32]
        out += [a * cos - b * sin, b * cos + a * sin, mixed[n + 32 : n + 64]]
    return jnp.concatenate(out + [mixed[128:]], 0).astype(BF)


def adamw(master, grad, first, second, rate):
    first_new = 0.9 * first + 0.1 * grad
    second_new = 0.95 * second + 0.05 * grad * grad
    first_hat = first_new / (1.0 - 0.9**STEP)
    second_hat = second_new / (1.0 - 0.95**STEP)
    fresh = master - rate * (first_hat / (jnp.sqrt(second_hat) + 1e-08) + 0.1 * master)
    return (fresh, first_new, second_new)


def local(
    tokens,
    cotangent,
    qkv_weight,
    dense_weight,
    fc1_weight,
    fc2_weight,
    vectors,
    qkv_first,
    dense_first,
    fc1_first,
    fc2_first,
    vectors_first,
    qkv_second,
    dense_second,
    fc1_second,
    fc2_second,
    vectors_second,
):
    h, z, c = lax.axis_index("xhi"), lax.axis_index("z"), lax.axis_index("core")
    zc = 2 * z + c
    low = h == 0
    ids = jnp.stack([h, z, c]).astype(jnp.int32)

    def own_first(v, axis):
        return jnp.where(low, v, halves_swapped(v, axis))

    x_own = tokens[0]
    g_own = cotangent[0]

    x_all = gather_tokens(own_first(x_own, 1))

    vec_b = vectors.astype(BF)
    head_cols = own_first(qkv_weight.astype(BF).reshape(64, 3, 2, 8, 64), 2)
    head_cols = head_cols.transpose(3, 0, 2, 1, 4).reshape(8, 64, 384)
    vec_rows = jnp.pad(vec_b.reshape(704), (0, 16 * 384 - 704)).reshape(1, 16, 384)
    message = jnp.concatenate([head_cols, jnp.broadcast_to(vec_rows, (8, 16, 384))], 1)
    got = lax.all_to_all(message, GROUP, 0, 0, tiled=True)
    got_x = swap_x(got)
    w_qkv = jnp.concatenate(
        [got[:, :64].reshape(512, 384), halves_swapped(got_x[:, :64].reshape(512, 384), 1)], 0
    )
    w_own, w_oth = w_qkv[:, :192], w_qkv[:, 192:]
    vec16 = jnp.stack([got[:, 64:], got_x[:, 64:]]).reshape(2, 8, 16 * 384)[:, :, :704]
    vec16 = vec16.reshape(2, 8, 11, 64).astype(F32)
    vec = vec16.transpose(2, 0, 1, 3).reshape(11, 1024)
    vec_g = own_first(vec, 1)
    gain, shift = vec[9], vec[10]
    at_zc = lax.dynamic_index_in_dim(vec16, zc, 1, keepdims=False)
    bias_own = at_zc[0, 0:3].reshape(192, 1)
    bias_oth = at_zc[1, 0:3].reshape(192, 1)
    b1_flat = vec_g[4:8].reshape(4096)
    mine_at, their_at = (h * 8 + zc) * 256, ((1 - h) * 8 + zc) * 256
    b1 = jnp.concatenate(
        [
            lax.dynamic_slice_in_dim(b1_flat, mine_at, 256),
            lax.dynamic_slice_in_dim(b1_flat, their_at, 256),
        ]
    )

    rows_b = jnp.concatenate([fc2_weight.astype(BF), dense_weight.astype(BF)], 0)
    rows_x = swap_x(rows_b)
    w2 = jnp.concatenate([rows_b[:256], rows_x[:256]], 0)
    wd_own, wd_oth = rows_b[256:], rows_x[256:]

    up_cols = own_first(fc1_weight.astype(BF).reshape(64, 2, 8, 256), 1)
    up_cols = up_cols.transpose(2, 0, 1, 3).reshape(8, 64, 512)
    got1 = lax.all_to_all(up_cols, GROUP, 0, 0, tiled=True).reshape(512, 512)
    got1_x = swap_x(got1)
    w1 = jnp.concatenate([got1, halves_swapped(got1_x, 1)], 0)

    index = jnp.arange(2048, dtype=jnp.int32)
    block = index // 256
    zz, cc = (block % 4 + z) % 4, (block // 4 + c) % 2
    positions = h * 2048 + (2 * zz + cc) * 256 + index % 256
    cos_here, sin_here = tables(positions)
    cos_all, sin_all = tables(jnp.arange(S, dtype=jnp.int32))

    normed, unused = normalize(x_all.astype(F32))
    hidden = (normed * gain + shift).astype(BF)
    mixed_oth = dot(w_oth, hidden, ((0,), (1,))) + bias_oth
    away = rotate(cos_here, sin_here, mixed_oth)
    came = swap_x(away)
    mixed_own = dot(w_own, hidden, ((0,), (1,))) + bias_own
    here = rotate(cos_here, sin_here, mixed_own)

    g_all = gather_tokens(g_own)

    upper = dot(hidden, w1) + b1
    active = gelu_new(upper).astype(BF)

    do_away = dot(wd_oth, g_all, ((1,), (1,))).astype(BF)
    do_came = swap_x(do_away)
    do_here = dot(wd_own, g_all, ((1,), (1,))).astype(BF)

    o_full, lse, o_here, o_away = attend(ids, here, came)
    o_came = swap_x(o_away)

    grad_active = dot(g_all, w2, ((1,), (1,)))
    unused_value, gelu_pull = jax.vjp(gelu_new, upper)
    grad_upper = gelu_pull(grad_active)[0].astype(BF)
    grad_w2 = dot(active, g_all, ((0,), (0,))).astype(BF)
    grad_w1 = dot(hidden, grad_upper, ((0,), (0,))).astype(BF)
    grad_b1 = jnp.sum(grad_upper.astype(F32), 0)

    g2 = (grad_w2[:256].astype(F32) + swap_x(grad_w2[256:]).astype(F32)).astype(BF)
    g1x = halves_swapped(swap_x(grad_w1[512:]), 1)
    g1 = (grad_w1[:512].astype(F32) + g1x.astype(F32)).astype(BF).reshape(8, 64, 512)
    g1 = lax.all_to_all(g1, GROUP, 0, 0, tiled=True)
    g1 = own_first(g1.reshape(8, 64, 2, 256).transpose(1, 2, 0, 3), 1).reshape(64, 4096)
    g1, g2 = lax.psum((g1, g2), BATCH)

    d_here, d_away = attend_back(
        ids, here, came, do_here, do_came, o_full, lse, cos_all, sin_all
    )
    d_came = swap_x(d_away)

    attended = jnp.concatenate([o_here, o_came], 0)
    wd = jnp.concatenate([wd_own, wd_oth], 0)
    out_part = dot(active, w2) + dot(attended, wd, ((0,), (0,)))
    out_sum = scatter_sum(out_part.astype(BF))
    output = (x_own.astype(F32) + out_sum + vec_g[3] + vec_g[8]).astype(BF)[None]

    grad_wd = dot(attended, g_all).astype(BF)
    gd = (grad_wd[:64].astype(F32) + swap_x(grad_wd[64:]).astype(F32)).astype(BF)

    d_both = jnp.concatenate([d_here, d_came], 0)
    grad_hidden = dot(d_both, w_qkv, ((0,), (1,))) + dot(grad_upper, w1, ((1,), (1,)))
    hidden_sum = scatter_sum(grad_hidden.astype(BF))
    grad_qkv = dot(hidden, d_both, ((0,), (1,))).astype(BF)

    grad_gain = jnp.sum(grad_hidden * normed, 0)
    grad_shift = jnp.sum(grad_hidden, 0)
    grad_bout = own_first(jnp.sum(g_own.astype(F32), 0), 0)
    hot = (jnp.arange(8) == zc).astype(F32)[None, :, None, None]
    gb = jnp.sum(d_both.astype(F32), 1).reshape(2, 1, 3, 64) * hot
    zeros = jnp.zeros((4096,), F32)
    gb1 = lax.dynamic_update_slice_in_dim(zeros, grad_b1[:256], mine_at, 0)
    gb1 = lax.dynamic_update_slice_in_dim(gb1, grad_b1[256:], their_at, 0)
    gb1 = own_first(gb1.reshape(4, 1024), 1).reshape(4, 2, 8, 64).transpose(1, 2, 0, 3)

    def by_device(row):
        return row.reshape(2, 8, 1, 64)

    grad_vec = jnp.concatenate(
        [gb, by_device(grad_bout), gb1, by_device(grad_bout), by_device(grad_gain), by_device(grad_shift)],
        2,
    )
    grad_vec = jnp.pad(grad_vec.astype(BF).reshape(2, 8, 704), ((0, 0), (0, 0), (0, 16 * 384 - 704)))
    grad_vec = grad_vec.reshape(2, 8, 16, 384)

    back_x = swap_x(
        jnp.concatenate(
            [halves_swapped(grad_qkv[512:], 1).reshape(8, 64, 384), grad_vec[1]], 1
        )
    )
    back = jnp.concatenate([grad_qkv[:512].reshape(8, 64, 384), grad_vec[0]], 1)
    back = (back.astype(F32) + back_x.astype(F32)).astype(BF)
    back = lax.all_to_all(back, GROUP, 0, 0, tiled=True)
    vec_sum = jnp.sum(back[:, 64:].astype(F32), 0).astype(BF)
    late = jnp.concatenate([back[:, :64].reshape(512, 384), vec_sum, gd_rows(gd)], 0)
    late = sum_batch(late)
    gq = late[:512].reshape(8, 64, 2, 3, 64).transpose(1, 3, 2, 0, 4)
    gq = own_first(gq, 2).reshape(64, 3072)
    gv = late[512:528].reshape(-1)[:704].reshape(11, 64)
    gd = late[528:].reshape(-1)[: 64 * 1024].reshape(64, 1024)

    x_f = x_own.astype(F32)
    normed_own, inverse_own = normalize(x_f)
    grad_normed = own_first(hidden_sum, 1) * vec_g[9]
    grad_inputs = g_own.astype(F32) + inverse_own * (
        grad_normed
        - jnp.mean(grad_normed, -1, keepdims=True)
        - normed_own * jnp.mean(grad_normed * normed_own, -1, keepdims=True)
    )
    input_grad = grad_inputs.astype(BF)[None]

    masters = (qkv_weight, dense_weight, fc1_weight, fc2_weight, vectors)
    firsts = (qkv_first, dense_first, fc1_first, fc2_first, vectors_first)
    seconds = (qkv_second, dense_second, fc1_second, fc2_second, vectors_second)
    total_grads = [t.astype(F32) for t in (gq, gd, g1, g2, gv)]
    rates = (2.0 * D ** (-0.5), 2.0 * D ** (-0.5), 2.0 * D ** (-0.5), 2.0 * FF ** (-0.5), 0.3)
    updated = [
        adamw(masters[index], total_grads[index], firsts[index], seconds[index], rates[index])
        for index in range(5)
    ]
    return (output, input_grad) + tuple(updated[i][j] for j in range(3) for i in range(5))


def gd_rows(gd):
    flat = jnp.pad(gd.reshape(-1), (0, 176 * 384 - gd.size))
    return flat.reshape(176, 384)


def solution(mesh):
    fine = Mesh(mesh.devices.reshape(2, 4, 2, 4, 2), ("xlo", "y", "xhi", "z", "core"))
    dp, fsdp = ("xlo", "y"), ("xhi", "z", "core")
    token = P(dp, fsdp, None)
    row = P(fsdp, None)
    column = P(None, fsdp)
    params = (row, row, row, row, column)
    return jax.shard_map(
        local,
        mesh=fine,
        in_specs=(token, token) + params * 3,
        out_specs=(token, token) + params * 3,
        check_vma=False,
    )
```

```python
import functools

import jax
import jax.numpy as jnp
from jax import lax
from jax.experimental import pallas as pl
from jax.experimental.pallas import tpu as pltpu
from jax.sharding import Mesh
from jax.sharding import PartitionSpec as P

D = 1024
HEAD = 64
ROT = 32
FF = 4096
STEP = 10
S = 4096
NEG = -1e30
F32 = jnp.float32
BF = jnp.bfloat16


def dot(a, b, dims=((1,), (0,))):
    return lax.dot_general(a, b, (dims, ((), ())), preferred_element_type=F32)


def load_halves(ids, own, oth, dst):
    @pl.when(ids[0] == 0)
    def _():
        dst[:, 0 : S // 2] = own[...]
        dst[:, S // 2 : S] = oth[...]

    @pl.when(ids[0] == 1)
    def _():
        dst[:, 0 : S // 2] = oth[...]
        dst[:, S // 2 : S] = own[...]


def store_halves(ids, src, own, away):
    @pl.when(ids[0] == 0)
    def _():
        own[...] = src[:, 0 : S // 2].astype(own.dtype)
        away[...] = src[:, S // 2 : S].astype(own.dtype)

    @pl.when(ids[0] == 1)
    def _():
        away[...] = src[:, 0 : S // 2].astype(own.dtype)
        own[...] = src[:, S // 2 : S].astype(own.dtype)


def causal(koff, qoff, shape):
    kp = koff + lax.broadcasted_iota(jnp.int32, shape, 0)
    qp = qoff + lax.broadcasted_iota(jnp.int32, shape, 1)
    return kp <= qp


def attend_kernel(BQ, BK, ids, own, oth, o_full, lse, o_own, o_away, qkv, kk):
    load_halves(ids, own, oth, qkv)
    for j in range(8):
        sl = slice(j * 512, (j + 1) * 512)
        kk[sl, :] = qkv[64:128, sl].T

    def q_block(qi, unused):
        qoff = pl.multiple_of(qi * BQ, BQ)
        qT = qkv[0:64, pl.ds(qoff, BQ)] * jnp.asarray(0.125, BF)

        def step(kj, carry, masked):
            m, l, acc = carry
            koff = pl.multiple_of(kj * BK, BK)
            s = dot(kk[pl.ds(koff, BK), :], qT)
            if masked:
                s = jnp.where(causal(koff, qoff, (BK, BQ)), s, NEG)
            m2 = jnp.maximum(m, jnp.max(s, 0, keepdims=True))
            p = jnp.exp(s - m2)
            a = jnp.exp(m - m2)
            l = l * a + jnp.sum(p, 0, keepdims=True)
            acc = acc * a + dot(qkv[128:192, pl.ds(koff, BK)], p.astype(BF))
            return m2, l, acc

        n = qoff // BK
        carry = (jnp.full((1, BQ), NEG, F32), jnp.zeros((1, BQ), F32), jnp.zeros((64, BQ), F32))
        carry = lax.fori_loop(0, n, lambda j, cc: step(j, cc, False), carry)
        m, l, acc = step(n, carry, True)
        o_full[:, pl.ds(qoff, BQ)] = acc / l
        lse[:, pl.ds(qoff, BQ)] = m + jnp.log(l)
        return unused

    lax.fori_loop(0, S // BQ, q_block, 0)
    store_halves(ids, o_full, o_own, o_away)


VMEM = 60 << 20
VM = pl.BlockSpec(memory_space=pltpu.VMEM)
SM = pl.BlockSpec(memory_space=pltpu.SMEM)


def attend(ids, own, oth, tie, BQ=1024, BK=1024):
    kernel = functools.partial(attend_kernel, BQ, BK)
    return pl.pallas_call(
        lambda *refs: kernel(*refs[:3], *refs[4:]),
        out_shape=(
            jax.ShapeDtypeStruct((64, S), F32),
            jax.ShapeDtypeStruct((1, S), F32),
            jax.ShapeDtypeStruct((64, S // 2), BF),
            jax.ShapeDtypeStruct((64, S // 2), BF),
        ),
        in_specs=[SM, VM, VM, pl.BlockSpec(memory_space=pl.ANY)],
        out_specs=(VM,) * 4,
        scratch_shapes=[pltpu.VMEM((192, S), BF), pltpu.VMEM((S, 64), BF)],
        compiler_params=pltpu.CompilerParams(vmem_limit_bytes=60 << 20),
        cost_estimate=pl.CostEstimate(
            flops=8 * S * S * 64, bytes_accessed=4 << 20, transcendentals=S * S // 2
        ),
        name="attend",
    )(ids, own, oth, tie)


def unrotate(d, cos, sin):
    a, b = d[0:16], d[16:32]
    return jnp.concatenate([a * cos + b * sin, b * cos - a * sin, d[32:64]], 0)


def attend_back_kernel(
    BQ, BK, ids, own, oth, do_own, do_oth, o_full, lse, cos, sin, d_own, d_away,
    qkv, kk, vv, qq, doT, dd, dq, dk, dv,
):
    load_halves(ids, own, oth, qkv)
    load_halves(ids, do_own, do_oth, doT)
    for j in range(8):
        sl = slice(j * 512, (j + 1) * 512)
        qkv[0:64, sl] = qkv[0:64, sl] * jnp.asarray(0.125, BF)
        qq[sl, :] = qkv[0:64, sl].T
        kk[sl, :] = qkv[64:128, sl].T
        vv[sl, :] = qkv[128:192, sl].T
        dd[sl, :] = doT[:, sl].T
    dk[...] = jnp.zeros_like(dk)
    dv[...] = jnp.zeros_like(dv)

    def q_block(qi, unused):
        qoff = pl.multiple_of(qi * BQ, BQ)
        qs = pl.ds(qoff, BQ)
        qT = qkv[0:64, qs]
        gT = doT[:, qs]
        delta = jnp.sum(gT.astype(F32) * o_full[:, qs], 0, keepdims=True)
        ls = lse[:, qs]

        def step(kj, acc, masked):
            koff = pl.multiple_of(kj * BK, BK)
            ks = pl.ds(koff, BK)
            s = dot(kk[ks, :], qT)
            if masked:
                s = jnp.where(causal(koff, qoff, (BK, BQ)), s, NEG)
            p = jnp.exp(s - ls)
            ds = (p * (dot(vv[ks, :], gT) - delta)).astype(BF)
            dv[ks, :] += dot(p.astype(BF), dd[qs, :])
            dk[ks, :] += dot(ds, qq[qs, :])
            return acc + dot(qkv[64:128, ks], ds)

        n = qoff // BK
        acc = lax.fori_loop(0, n, lambda j, a: step(j, a, False), jnp.zeros((64, BQ), F32))
        acc = step(n, acc, True) * 0.125
        dq[0:64, qs] = unrotate(acc, cos[:, qs], sin[:, qs]).astype(BF)
        return unused

    lax.fori_loop(0, S // BQ, q_block, 0)
    for j in range(8):
        sl = slice(j * 512, (j + 1) * 512)
        dq[64:128, sl] = unrotate(dk[sl, :].T, cos[:, sl], sin[:, sl]).astype(BF)
        dq[128:192, sl] = dv[sl, :].T.astype(BF)
    store_halves(ids, dq, d_own, d_away)


def attend_back(ids, own, oth, do_own, do_oth, o_full, lse, cos, sin, tie, BQ=1024, BK=1024):
    kernel = functools.partial(attend_back_kernel, BQ, BK)
    return pl.pallas_call(
        lambda *refs: kernel(*refs[:9], *refs[10:]),
        out_shape=(jax.ShapeDtypeStruct((192, S // 2), BF),) * 2,
        in_specs=[SM] + [VM] * 8 + [pl.BlockSpec(memory_space=pl.ANY)],
        out_specs=(VM,) * 2,
        scratch_shapes=[
            pltpu.VMEM((192, S), BF),
            pltpu.VMEM((S, 64), BF),
            pltpu.VMEM((S, 64), BF),
            pltpu.VMEM((S, 64), BF),
            pltpu.VMEM((64, S), BF),
            pltpu.VMEM((S, 64), BF),
            pltpu.VMEM((192, S), BF),
            pltpu.VMEM((S, 64), F32),
            pltpu.VMEM((S, 64), F32),
        ],
        compiler_params=pltpu.CompilerParams(vmem_limit_bytes=60 << 20),
        cost_estimate=pl.CostEstimate(
            flops=20 * S * S * 64, bytes_accessed=6 << 20, transcendentals=S * S // 2
        ),
        name="attend_back",
    )(ids, own, oth, do_own, do_oth, o_full, lse, cos, sin, tie)


ANY = pl.BlockSpec(memory_space=pl.ANY)
DMA = pltpu.SemaphoreType.DMA
NT = ((1,), (1,))
TN = ((0,), (0,))


def call(kernel, name, inputs, specs, outs, scratch, flops=0, moved=0, ties=(), out_specs=None):
    shapes = tuple(jax.ShapeDtypeStruct(shape, kind) for shape, kind in outs)
    n, k = len(inputs), len(ties)

    def body(*refs):
        kernel(*refs[:n], *refs[n + k :])

    return pl.pallas_call(
        body,
        out_shape=shapes,
        in_specs=list(specs) + [ANY] * k,
        out_specs=out_specs or (VM,) * len(outs),
        scratch_shapes=scratch,
        compiler_params=pltpu.CompilerParams(vmem_limit_bytes=VMEM),
        cost_estimate=pl.CostEstimate(flops=flops, bytes_accessed=moved, transcendentals=0),
        name=name,
    )(*inputs, *ties)


def hold(v, *ties):
    return pl.pallas_call(
        lambda *refs: None,
        out_shape=jax.ShapeDtypeStruct(v.shape, v.dtype),
        in_specs=[ANY] * (1 + len(ties)),
        out_specs=ANY,
        input_output_aliases={0: 0},
        name="hold",
    )(v, *ties)


def start_rows_in(src, dst, sems):
    for i in range(8):
        at = pl.ds(i * 256, 256)
        pltpu.make_async_copy(src.at[at], dst.at[at], sems.at[i]).start()


def start_pieces(ids, pieces, dst, sems):
    z, c = ids[1], ids[2]
    for n, piece in enumerate(pieces):
        there = 2 * lax.rem(z + n % 4, 4) + (c if n < 4 else 1 - c)
        to = dst.at[pl.ds(pl.multiple_of(there * 256, 256), 256)]
        pltpu.make_async_copy(piece, to, sems.at[n]).start()


def wait_pair(ids, dst, sems, k):
    for n in (k, 4 + k):
        rows = dst.at[pl.ds(0, 256)]
        pltpu.make_async_copy(rows, rows, sems.at[n]).wait()
    return pl.ds(pl.multiple_of(lax.rem(ids[1] + k, 4) * 512, 512), 512)


def wait_piece(dst, sems, i):
    rows = dst.at[pl.ds(pl.multiple_of(i * 256, 256), 256)]
    pltpu.make_async_copy(rows, rows, sems.at[i]).wait()


def pack_kernel(w, vec, msg):
    v = jnp.concatenate([vec[...], jnp.zeros((5, 64), F32)], 0).astype(BF)
    for d in range(16):
        hd, zcd = d // 8, d % 8
        for part in range(2):
            block = (hd if part == 0 else 1 - hd) * 8 + zcd
            for t in range(3):
                col = t * 1024 + block * 64
                at = part * 192 + t * 64
                msg[d, 0:64, at : at + 64] = w[:, col : col + 64].astype(BF)
        msg[d, 64:80, :] = jnp.zeros((16, 384), BF)
        msg[d, 64:80, 0:64] = v


def pack(w, vec):
    return call(pack_kernel, "pack", (w, vec), [VM] * 2, [((16, 80, 384), BF)], [], 0, 2 << 20)[0]


def pack_up_kernel(w1, msg):
    for d in range(16):
        hd, zcd = d // 8, d % 8
        for part in range(2):
            block = (hd if part == 0 else 1 - hd) * 8 + zcd
            msg[d, :, part * 256 : part * 256 + 256] = w1[:, block * 256 : block * 256 + 256].astype(BF)


def pack_up(w1, *ties):
    return call(pack_up_kernel, "pack_up", (w1,), [VM], [((16, 64, 512), BF)], [], 0, 4 << 20, ties)[0]


def copy_kernel(src, dst):
    dst[...] = src[...]


def after(v, *ties):
    return call(copy_kernel, "after", (v,), [VM], [(v.shape, v.dtype)], [], 0, 1 << 20, ties)[0]


def pack_rows_kernel(w2, wd, rows):
    rows[0:256, :] = w2[...].astype(BF)
    rows[256:320, :] = wd[...].astype(BF)


def pack_rows(w2, wd):
    return call(pack_rows_kernel, "pack_rows", (w2, wd), [VM] * 2, [((320, 1024), BF)], [], 0, 2 << 20)[0]


def normalize(values):
    middle = jnp.mean(values, -1, keepdims=True)
    centered = values - middle
    spread = jnp.mean(centered * centered, -1, keepdims=True)
    inverse = lax.rsqrt(spread + 1e-05)
    return (centered * inverse, inverse)


def rotate(cos, sin, mixed):
    out = []
    for n in (0, 64):
        a, b = mixed[n : n + 16], mixed[n + 16 : n + 32]
        out += [a * cos - b * sin, b * cos + a * sin, mixed[n + 32 : n + 64]]
    return jnp.concatenate(out + [mixed[128:]], 0).astype(BF)


def project_kernel(ids, msg, cos, sin, *refs):
    pieces = refs[:8]
    hidden, here, away, vec, b1, w_qkv, xs = refs[8:15]
    raw, sems = refs[15:]
    h, z, c = ids[0], ids[1], ids[2]
    zc = 2 * z + c
    start_pieces(ids, pieces, xs, sems)
    for s in range(16):
        w_qkv[s * 64 : (s + 1) * 64, :] = msg[s, 0:64, 0:384]
        v = msg[s, 64:80, 0:64].astype(F32)
        raw[s] = v
        vec[:, s * 64 : (s + 1) * 64] = v
    own, oth = h * 8 + zc, (1 - h) * 8 + zc
    v_own, v_oth = raw[own], raw[oth]
    bias = jnp.concatenate(
        [v_own[t : t + 1, :] for t in range(3)] + [v_oth[t : t + 1, :] for t in range(3)], 1
    )
    for n, i in enumerate((own, oth)):
        for j in range(4):
            at = n * 256 + j * 64
            b1[:, at : at + 64] = raw[4 * lax.rem(i, 4) + j, pl.ds(4 + i // 4, 1), :]
    gain, shift = vec[9:10, :], vec[10:11, :]

    def pair(k, unused):
        at = wait_pair(ids, xs, sems, k)
        normed, unused_inverse = normalize(xs[at, :].astype(F32))
        hid = (normed * gain + shift).astype(BF)
        hidden[at, :] = hid
        mixed = (dot(hid, w_qkv[...]) + bias).T
        here[:, at] = rotate(cos[:, at], sin[:, at], mixed[:192])
        away[:, at] = rotate(cos[:, at], sin[:, at], mixed[192:])
        return unused

    lax.fori_loop(0, 4, pair, 0)


def project(ids, msg, cos, sin, pieces, *ties):
    outs = [
        ((2048, 1024), BF),
        ((192, 2048), BF),
        ((192, 2048), BF),
        ((16, 1024), F32),
        ((1, 512), F32),
        ((1024, 384), BF),
        ((2048, 1024), BF),
    ]
    scratch = [pltpu.VMEM((16, 16, 64), F32), DMA((8,))]
    inputs = (ids, msg, cos, sin) + tuple(pieces)
    return call(
        project_kernel, "project", inputs, [SM, VM, VM, VM] + [ANY] * 8, outs, scratch,
        4 * 2048 * 1024 * 384, 12 << 20, ties,
    )


def rows_kernel(ids, rows, g_ref, do_here, do_away, gs, wd, sems):
    h = ids[0]
    start_rows_in(g_ref, gs, sems)
    wd[0:64, :] = rows[h, 256:320, :]
    wd[64:128, :] = rows[1 - h, 256:320, :]

    def pair(n, unused):
        for i in range(2):
            wait_piece(gs, sems, 2 * n + i)
        at = pl.ds(pl.multiple_of(n * 512, 512), 512)
        both = dot(gs[at, :], wd[...], NT).T.astype(BF)
        do_here[:, at] = both[:64]
        do_away[:, at] = both[64:]
        return unused

    lax.fori_loop(0, 4, pair, 0)


def attended_back(ids, rows, g_all, *ties):
    outs = [((64, 2048), BF)] * 2
    scratch = [pltpu.VMEM((2048, 1024), BF), pltpu.VMEM((128, 1024), BF), DMA((8,))]
    return call(
        rows_kernel, "attended_back", (ids, rows, g_all), [SM, VM, ANY], outs, scratch,
        4 * 2048 * 1024 * 128, 6 << 20, ties,
    )


ROOT = 0.7978845608028654


def units_kernel(hid_ref, w1, b1, act, slope, hs, sems):
    start_rows_in(hid_ref, hs, sems)

    def block(n, unused):
        for i in range(2):
            wait_piece(hs, sems, 2 * n + i)
        at = pl.ds(pl.multiple_of(n * 512, 512), 512)
        u = dot(hs[at, :], w1[...]) + b1[...]
        square = u * u
        th = jnp.tanh(ROOT * u * (1.0 + 0.044715 * square))
        half = 0.5 * (1.0 + th)
        act[at, :] = (u * half).astype(BF)
        slope[at, :] = half + 0.5 * u * (1.0 - th * th) * (ROOT * (1.0 + 3.0 * 0.044715 * square))
        return unused

    lax.fori_loop(0, 4, block, 0)


def units(hidden, w1, b1, *ties):
    outs = [((2048, 512), BF), ((2048, 512), F32)]
    scratch = [pltpu.VMEM((2048, 1024), BF), DMA((8,))]
    return call(
        units_kernel, "units", (hidden, w1, b1), [ANY, VM, VM], outs, scratch,
        2 * 2048 * 1024 * 512, 11 << 20, ties,
    )


def units_back_kernel(ids, hid_ref, act, slope_ref, rows, g_ref, *refs):
    dup, msg, gb1 = refs[:3]
    hs, gs, ss, w2, acc1, acc2, sems, hsems, ssems = refs[3:]
    h = ids[0]
    start_rows_in(g_ref, gs, sems)
    start_rows_in(slope_ref, ss, ssems)
    start_rows_in(hid_ref, hs, hsems)
    w2[0:256, :] = rows[h, 0:256, :]
    w2[256:512, :] = rows[1 - h, 0:256, :]
    acc1[...] = jnp.zeros_like(acc1)
    acc2[...] = jnp.zeros_like(acc2)
    gb1[...] = jnp.zeros_like(gb1)


    def block(n, unused):
        for i in range(2):
            wait_piece(gs, sems, 2 * n + i)
            wait_piece(ss, ssems, 2 * n + i)
            wait_piece(hs, hsems, 2 * n + i)
        at = pl.ds(pl.multiple_of(n * 512, 512), 512)
        hid, g = hs[at, :], gs[at, :]
        back_b = (dot(g, w2[...], NT) * ss[at, :]).astype(BF)
        dup[at, :] = back_b
        gb1[...] += jnp.sum(back_b.astype(F32), 0, keepdims=True)
        acc2[...] += dot(act[at, :], g, TN)
        acc1[...] += dot(hid, back_b, TN)
        return unused

    lax.fori_loop(0, 4, block, 0)
    for p in range(8):
        for hd in range(2):
            rows_at = slice(hd * 512 + p * 64, hd * 512 + p * 64 + 64)
            for part in range(2):
                hh = h if part == 0 else 1 - h
                msg[2 * p + hd, pl.ds(pl.multiple_of(hh * 64, 64), 64), :] = acc1[
                    rows_at, part * 256 : part * 256 + 256
                ].astype(BF)
        for part in range(2):
            hh = h if part == 0 else 1 - h
            for q in range(4):
                msg[2 * p + hh, 128 + q * 32 : 160 + q * 32, :] = acc2[
                    part * 256 + p * 32 : part * 256 + p * 32 + 32, q * 256 : q * 256 + 256
                ].astype(BF)


def units_back(ids, hidden, act, slope, rows, g_all, *ties):
    outs = [((2048, 512), BF), ((16, 256, 256), BF), ((1, 512), F32)]
    scratch = [
        pltpu.VMEM((2048, 1024), BF),
        pltpu.VMEM((2048, 1024), BF),
        pltpu.VMEM((2048, 512), F32),
        pltpu.VMEM((512, 1024), BF),
        pltpu.VMEM((1024, 512), F32),
        pltpu.VMEM((512, 1024), F32),
        DMA((8,)),
        DMA((8,)),
        DMA((8,)),
    ]
    return call(
        units_back_kernel, "units_back", (ids, hidden, act, slope, rows, g_all),
        [SM, ANY, VM, ANY, VM, ANY], outs, scratch, 6 * 2048 * 1024 * 512, 18 << 20, ties,
    )


def start_rows_out(src, n, to, sems):
    at = pl.ds(n * 512, 512)
    copy = pltpu.make_async_copy(src.at[at], to.at[at], sems.at[n])
    copy.start()
    return copy


def out_kernel(ids, act, rows, o_here, o_came, g_ref, total, gd, gs, both, out, sems, osems):
    h = ids[0]
    start_rows_in(g_ref, gs, sems)
    both[0:64, :] = o_here[...]
    both[64:128, :] = o_came[...]
    wd = jnp.concatenate([rows[h, 256:320, :], rows[1 - h, 256:320, :]], 0)
    w2, w2_x = rows.at[h], rows.at[1 - h]
    copies = []
    for n in range(4):
        at = slice(n * 512, n * 512 + 512)
        part = dot(act[at, 0:256], w2[0:256, :]) + dot(act[at, 256:512], w2_x[0:256, :])
        part += dot(both[:, at], wd, TN)
        out[at, :] = part.astype(BF)
        copies.append(start_rows_out(out, n, total, osems))
    for i in range(8):
        wait_piece(gs, sems, i)
    grad = dot(both[...], gs[...]).astype(BF)
    gd[h] = grad[:64]
    gd[1 - h] = grad[64:]
    for copy in copies:
        copy.wait()


def out_part(ids, act, rows, o_here, o_came, g_all, *ties):
    outs = [((2048, 1024), BF), ((2, 64, 1024), BF)]
    scratch = [
        pltpu.VMEM((2048, 1024), BF),
        pltpu.VMEM((128, 2048), BF),
        pltpu.VMEM((2048, 1024), BF),
        DMA((8,)),
        DMA((4,)),
    ]
    return call(
        out_kernel, "out_part", (ids, act, rows, o_here, o_came, g_all),
        [SM] + [VM] * 4 + [ANY], outs, scratch, 4 * 2048 * 1024 * 640, 12 << 20, ties,
        (ANY, VM),
    )


def hidden_kernel(ids, d_here, d_came, w_qkv, dup, w1, hid_ref, g_own, gb1, gd, x_ref, *refs):
    total, msg = refs[:2]
    hs, xs, both, out, gq, vec, sums, sems, hsem, osems = refs[2:]
    h, zc = ids[0], 2 * ids[1] + ids[2]
    whole = pltpu.make_async_copy(hid_ref, hs, hsem)
    start_rows_in(x_ref, xs, sems)
    whole.start()
    both[0:192, :] = d_here[...]
    both[192:384, :] = d_came[...]
    sums[...] = jnp.zeros_like(sums)
    copies = []
    for n in range(4):
        at = slice(n * 512, n * 512 + 512)
        part = dot(dup[at, :], w1[...], NT) + dot(both[:, at].T, w_qkv[...], NT)
        out[at, :] = part.astype(BF)
        copies.append(start_rows_out(out, n, total, osems))
        wait_piece(xs, sems, 2 * n)
        wait_piece(xs, sems, 2 * n + 1)
        normed, unused_inverse = normalize(xs[at, :].astype(F32))
        sums[0:1, :] += jnp.sum(part * normed, 0, keepdims=True)
        sums[1:2, :] += jnp.sum(part, 0, keepdims=True)
    whole.wait()
    grad = dot(both[...], hs[...])
    gq[pl.ds(pl.multiple_of(h * 192, 64), 192), :] = grad[:192]
    gq[pl.ds(pl.multiple_of((1 - h) * 192, 64), 192), :] = grad[192:]
    ones = jnp.ones((8, 2048), BF)
    bias_own = dot(ones, d_here[...], NT)[0:1]
    bias_oth = dot(ones, d_came[...], NT)[0:1]
    own, oth = h * 8 + zc, (1 - h) * 8 + zc
    lane = lax.broadcasted_iota(jnp.int32, (1, 1024), 1)
    out_sum = jnp.sum(g_own[...].astype(F32), 0, keepdims=True)
    rows = []
    for t in range(3):
        a = jnp.concatenate([bias_own[:, t * 64 : t * 64 + 64]] * 16, 1)
        b = jnp.concatenate([bias_oth[:, t * 64 : t * 64 + 64]] * 16, 1)
        rows.append(jnp.where(lane // 64 == own, a, 0.0) + jnp.where(lane // 64 == oth, b, 0.0))
    rows.append(out_sum)
    a = jnp.concatenate([gb1[:, 0:256]] * 4, 1)
    b = jnp.concatenate([gb1[:, 256:512]] * 4, 1)
    for r in range(4):
        block = lane // 256 + 4 * r
        rows.append(jnp.where(block == own, a, 0.0) + jnp.where(block == oth, b, 0.0))
    rows += [out_sum, sums[0:1, :], sums[1:2, :]]
    for r, row in enumerate(rows):
        vec[r : r + 1, :] = row
    flat = gq[...].T
    zeros = jnp.zeros((8, 64), F32)
    for p in range(8):
        for hd in range(2):
            at = hd * 512 + p * 64
            msg[2 * p + hd, 0:64, :] = flat[at : at + 64, :].astype(BF)
            cols = slice((hd * 8 + p) * 64, (hd * 8 + p) * 64 + 64)
            v0 = vec[0:8, cols]
            v1 = vec[8:16, cols]
            vrows = jnp.concatenate([v0, zeros, v1, zeros, zeros, zeros], 1)
            d = gd[hd, p * 8 : p * 8 + 8, :].astype(F32)
            d2 = jnp.concatenate([d[:, 768:1024], jnp.zeros((8, 128), F32)], 1)
            tail = jnp.concatenate([vrows, d[:, 0:384], d[:, 384:768], d2], 0)
            msg[2 * p + hd, 64:96, :] = tail.astype(BF)
    for copy in copies:
        copy.wait()


def hidden_part(ids, d_here, d_came, w_qkv, dup, w1, hidden, g_own, gb1, gd, x_all, *ties):
    outs = [((2048, 1024), BF), ((16, 96, 384), BF)]
    scratch = [
        pltpu.VMEM((2048, 1024), BF),
        pltpu.VMEM((2048, 1024), BF),
        pltpu.VMEM((384, 2048), BF),
        pltpu.VMEM((2048, 1024), BF),
        pltpu.VMEM((384, 1024), F32),
        pltpu.VMEM((16, 1024), F32),
        pltpu.VMEM((8, 1024), F32),
        DMA((8,)),
        DMA(()),
        DMA((4,)),
    ]
    return call(
        hidden_kernel, "hidden_part",
        (ids, d_here, d_came, w_qkv, dup, w1, hidden, g_own, gb1, gd, x_all),
        [SM] + [VM] * 5 + [ANY] + [VM] * 3 + [ANY], outs, scratch, 4 * 2048 * 1024 * 1280, 16 << 20, ties,
        (ANY, VM),
    )


SWAP = [(0, 1), (1, 0)]
GROUP = ("z", "core")
MODEL = ("xhi", "z", "core")
BATCH = ("xlo", "y")
SUM = ("xlo", "y", "xhi")


def swap_core(v):
    return lax.ppermute(v, "core", SWAP)


def swap_x(v):
    return lax.ppermute(v, "xhi", SWAP)


def from_z(v, k):
    return lax.ppermute(v, "z", [(i, (i - k) % 4) for i in range(4)])


def along_z(v):
    mine = {0: v}
    for k in (2, 1, 3):
        mine[k] = from_z(v, k)
    return [mine[k] for k in range(4)]


def gather_tokens(v):
    mine = along_z(v)
    return mine + [swap_core(b) for b in mine]


def group_sum(v):
    return lax.psum_scatter(v, GROUP, scatter_dimension=0, tiled=True)


def sum_kernel(n, parts, lo, hi):
    total = parts[0].astype(F32)
    for i in range(1, 16):
        total = total + parts[i].astype(F32)
    lo[...] = total[:n].astype(BF)
    hi[...] = total[n:].astype(BF)


def sum_parts(parts, n, *ties):
    rows, columns = parts.shape[1:]
    outs = [((n, columns), BF), ((rows - n, columns), BF)]
    return call(functools.partial(sum_kernel, n), "sum_parts", (parts,), [VM], outs, [], 0, 2 << 20, ties)


def fan_kernel(lo, hi, out):
    n = lo.shape[0]
    for p in range(8):
        out[p, 0:n, :] = lo[...]
        out[p, n:, :] = hi[...]


def join_kernel(lo, hi, out):
    n = lo.shape[0]
    out[0:n, :] = lo[...]
    out[n:, :] = hi[...]


def join(lo, hi, *ties):
    shape = (lo.shape[0] + hi.shape[0], lo.shape[1])
    return call(join_kernel, "join", (lo, hi), [VM] * 2, [(shape, BF)], [], 0, 1 << 18, ties)[0]


def from_batch(v, j):
    return lax.ppermute(v, BATCH, [(i, i ^ j) for i in range(8)])


def fan(lo, hi, *ties):
    shape = (8, lo.shape[0] + hi.shape[0], lo.shape[1])
    return call(fan_kernel, "fan", (lo, hi), [VM] * 2, [(shape, BF)], [], 0, 2 << 20, ties)[0]


def turn(v):
    return lax.ppermute(v, ("xlo", "y", "z", "core"), [(p * 8 + m, m * 8 + p) for p in range(8) for m in range(8)])


def tables(positions):
    freqs = 10000.0 ** (-(jnp.arange(ROT // 2, dtype=F32) * 2.0) / ROT)
    angles = positions.astype(F32)[None, :] * freqs[:, None]
    return (jnp.cos(angles), jnp.sin(angles))


def adamw(master, grad, first, second, rate):
    first_new = 0.9 * first + 0.1 * grad
    second_new = 0.95 * second + 0.05 * grad * grad
    first_hat = first_new / (1.0 - 0.9**STEP)
    second_hat = second_new / (1.0 - 0.95**STEP)
    fresh = master - rate * (first_hat / (jnp.sqrt(second_hat) + 1e-08) + 0.1 * master)
    return (fresh, first_new, second_new)


RATE = 2.0 * D ** (-0.5)
RATE_DOWN = 2.0 * FF ** (-0.5)


def update_units_kernel(early, w1, m1, v1, w2, m2, v2, w1n, m1n, v1n, w2n, m2n, v2n):
    for p in range(8):
        for hh in range(2):
            at = slice((hh * 8 + p) * 256, (hh * 8 + p) * 256 + 256)
            grad = early[p, hh * 64 : hh * 64 + 64, :].astype(F32)
            w1n[:, at], m1n[:, at], v1n[:, at] = adamw(w1[:, at], grad, m1[:, at], v1[:, at], RATE)
        for q in range(4):
            at = (slice(p * 32, p * 32 + 32), slice(q * 256, q * 256 + 256))
            grad = early[p, 128 + q * 32 : 160 + q * 32, :].astype(F32)
            w2n[at], m2n[at], v2n[at] = adamw(w2[at], grad, m2[at], v2[at], RATE_DOWN)


def update_units(early, *state):
    outs = [((64, 4096), F32)] * 3 + [((256, 1024), F32)] * 3
    return call(update_units_kernel, "update_units", (early,) + state, [VM] * 7, outs, [], 0, 13 << 20)


def update_heads_kernel(late, w, m, v, wd, md, vd, vec, mv, vv, wn, mn, vn, wdn, mdn, vdn, vecn, mvn, vvn, gq, gd):
    for zc in range(8):
        for hh in range(2):
            for t in range(3):
                col = t * 1024 + (hh * 8 + zc) * 64
                at = hh * 192 + t * 64
                gq[:, col : col + 64] = late[zc, 0:64, at : at + 64].astype(F32)
        rows = late[zc, 64:96, :].astype(F32)
        gd[zc * 8 : zc * 8 + 8, 0:384] = rows[8:16]
        gd[zc * 8 : zc * 8 + 8, 384:768] = rows[16:24]
        gd[zc * 8 : zc * 8 + 8, 768:1024] = rows[24:32, 0:256]
        total = rows[0:8] if zc == 0 else total + rows[0:8]
    grad = jnp.concatenate([total[:, 0:64], total[0:3, 128:192]], 0)
    wn[...], mn[...], vn[...] = adamw(w[...], gq[...], m[...], v[...], RATE)
    wdn[...], mdn[...], vdn[...] = adamw(wd[...], gd[...], md[...], vd[...], RATE)
    vecn[...], mvn[...], vvn[...] = adamw(vec[...], grad, mv[...], vv[...], 0.3)


def update_heads(late, *state):
    outs = [((64, 3072), F32)] * 3 + [((64, 1024), F32)] * 3 + [((11, 64), F32)] * 3
    scratch = [pltpu.VMEM((64, 3072), F32), pltpu.VMEM((64, 1024), F32)]
    return call(update_heads_kernel, "update_heads", (late,) + state, [VM] * 10, outs, scratch, 0, 7 << 20)


def input_kernel(came, x, g, vec, out):
    total = came[...].astype(F32)
    normed, inverse = normalize(x[...].astype(F32))
    back = total * vec[9:10, :]
    mean = jnp.mean(back, -1, keepdims=True)
    along = jnp.mean(back * normed, -1, keepdims=True)
    out[...] = (g[...].astype(F32) + inverse * (back - mean - normed * along)).astype(BF)


def input_part(blocks, x, g, vec, *ties):
    inputs = (blocks, x, g, vec)
    return call(input_kernel, "input_part", inputs, [VM] * 4, [((256, 1024), BF)], [], 0, 4 << 20, ties)[0]


def output_kernel(came, x, vec, out):
    total = came[...].astype(F32)
    out[...] = (x[...].astype(F32) + total + (vec[3:4, :] + vec[8:9, :])).astype(BF)


def output_part(blocks, x, vec, *ties):
    inputs = (blocks, x, vec)
    return call(output_kernel, "output_part", inputs, [VM] * 3, [((256, 1024), BF)], [], 0, 4 << 20, ties)[0]


def local(
    tokens,
    cotangent,
    qkv_weight,
    dense_weight,
    fc1_weight,
    fc2_weight,
    vectors,
    qkv_first,
    dense_first,
    fc1_first,
    fc2_first,
    vectors_first,
    qkv_second,
    dense_second,
    fc1_second,
    fc2_second,
    vectors_second,
):
    h, z, c = lax.axis_index("xhi"), lax.axis_index("z"), lax.axis_index("core")
    ids = jnp.stack([h, z, c, lax.axis_index(BATCH)]).astype(jnp.int32)
    x_own = tokens[0]
    g_own = cotangent[0]

    xs = gather_tokens(x_own)
    msg = lax.all_to_all(pack(qkv_weight, vectors), MODEL, 0, 0, tiled=True)
    rows = lax.all_gather(pack_rows(fc2_weight, dense_weight), "xhi", axis=0, tiled=False)
    up_msg = pack_up(fc1_weight, msg)
    w1 = lax.all_to_all(up_msg, MODEL, 0, 0, tiled=True).reshape(1024, 512)
    g_tied = hold(g_own, msg, xs[1], xs[2], xs[3])
    g_all = lax.all_gather(g_tied, GROUP, axis=0, tiled=True)
    cos_all, sin_all = tables(jnp.arange(S, dtype=jnp.int32))
    cos_here = lax.dynamic_slice_in_dim(cos_all, h * (S // 2), S // 2, 1)
    sin_here = lax.dynamic_slice_in_dim(sin_all, h * (S // 2), S // 2, 1)

    hidden, here, away, vec, b1, w_qkv, x_all = project(ids, msg, cos_here, sin_here, xs, up_msg)
    came = swap_x(away)
    act, slope = units(hidden, w1, b1, away)
    dup, early, gb1 = units_back(ids, hidden, act, slope, rows, g_all, came)
    early = lax.all_to_all(early, SUM, 0, 0, tiled=True)

    o_full, lse, o_here, o_away = attend(ids, here, came, dup)
    o_came = swap_x(o_away)
    do_here, do_away = attended_back(ids, rows, g_all, o_away)
    do_came = swap_x(do_away)
    early_turn, early_stay = sum_parts(early, 128, do_away)
    early_turn = turn(early_turn)
    total, gd = out_part(ids, act, rows, o_here, o_came, g_all, early_turn, do_came)
    out_sum = group_sum(total)
    d_here, d_away = attend_back(
        ids, here, came, do_here, do_came, o_full, lse, cos_all, sin_all, total
    )
    d_came = swap_x(d_away)
    early = fan(early_turn, early_stay, d_here)
    total, late = hidden_part(
        ids, d_here, d_came, w_qkv, dup, w1, hidden, g_own, gb1, gd, x_all, early
    )
    early = lax.all_to_all(early, BATCH, 0, 0, tiled=True)
    total = hold(total, early)
    hidden_sum = group_sum(total)
    late = lax.all_to_all(hold(late, early), SUM, 0, 0, tiled=True)
    new1 = update_units(
        hold(early, total), fc1_weight, fc1_first, fc1_second, fc2_weight, fc2_first, fc2_second
    )
    output = output_part(out_sum, x_own, vec, new1[0])
    late_turn, late_stay = sum_parts(late, 72, output)
    late = fan(turn(late_turn), late_stay)
    input_grad = input_part(hidden_sum, x_own, g_own, vec, late)
    late = lax.all_to_all(late, BATCH, 0, 0, tiled=True)
    new2 = update_heads(
        hold(late, input_grad),
        *(qkv_weight, qkv_first, qkv_second),
        *(dense_weight, dense_first, dense_second),
        *(vectors, vectors_first, vectors_second),
    )
    news = [(new2[j], new2[3 + j], new1[j], new1[3 + j], new2[6 + j]) for j in range(3)]
    return (output[None], input_grad[None]) + news[0] + news[1] + news[2]


def solution(mesh):
    fine = Mesh(mesh.devices.reshape(2, 4, 2, 4, 2), ("xlo", "y", "xhi", "z", "core"))
    dp, fsdp = ("xlo", "y"), ("xhi", "z", "core")
    token = P(dp, fsdp, None)
    row = P(fsdp, None)
    column = P(None, fsdp)
    params = (row, row, row, row, column)
    return jax.shard_map(
        local,
        mesh=fine,
        in_specs=(token, token) + params * 3,
        out_specs=(token, token) + params * 3,
        check_vma=False,
    )
```

```python
import functools

import jax
import jax.numpy as jnp
from jax import lax
from jax.experimental import pallas as pl
from jax.experimental.pallas import tpu as pltpu
from jax.sharding import Mesh
from jax.sharding import PartitionSpec as P

D = 1024
HEAD = 64
ROT = 32
FF = 4096
STEP = 10
S = 4096
NEG = -1e30
F32 = jnp.float32
BF = jnp.bfloat16


def dot(a, b, dims=((1,), (0,))):
    return lax.dot_general(a, b, (dims, ((), ())), preferred_element_type=F32)


def load_halves(ids, own, oth, dst):
    @pl.when(ids[0] == 0)
    def _():
        dst[:, 0 : S // 2] = own[...]
        dst[:, S // 2 : S] = oth[...]

    @pl.when(ids[0] == 1)
    def _():
        dst[:, 0 : S // 2] = oth[...]
        dst[:, S // 2 : S] = own[...]


def store_halves(ids, src, own, away):
    @pl.when(ids[0] == 0)
    def _():
        own[...] = src[:, 0 : S // 2].astype(own.dtype)
        away[...] = src[:, S // 2 : S].astype(own.dtype)

    @pl.when(ids[0] == 1)
    def _():
        away[...] = src[:, 0 : S // 2].astype(own.dtype)
        own[...] = src[:, S // 2 : S].astype(own.dtype)


VMEM = 60 << 20
VM = pl.BlockSpec(memory_space=pltpu.VMEM)
SM = pl.BlockSpec(memory_space=pltpu.SMEM)
BQ = 1024
BK = 512


def causal(s, shift):
    kp = shift + lax.broadcasted_iota(jnp.int32, s.shape, 0)
    qp = lax.broadcasted_iota(jnp.int32, s.shape, 1)
    return jnp.where(kp <= qp, s, NEG)


def attend_kernel(ids, own, oth, o_full, lse, o_own, o_away, qkv, kk, qs, s0, s1, acc, top, total):
    load_halves(ids, own, oth, qkv)
    for j in range(8):
        sl = slice(j * 512, (j + 1) * 512)
        kk[sl, :] = qkv[64:128, sl].T

    def q_block(qi, unused):
        at = pl.ds(pl.multiple_of(qi * BQ, BQ), BQ)
        qs[...] = qkv[0:64, at] * jnp.asarray(0.125, BF)
        top[...] = jnp.full_like(top, NEG)
        total[...] = jnp.zeros_like(total)
        acc[...] = jnp.zeros_like(acc)

        def scores(j, cols):
            return dot(kk[pl.ds(pl.multiple_of(j * BK, BK), BK), :], qs[:, cols])

        def fold(s, j, cols):
            m = top[:, cols]
            m2 = jnp.maximum(m, jnp.max(s, 0, keepdims=True))
            p = jnp.exp(s - m2)
            a = jnp.exp(m - m2)
            top[:, cols] = m2
            total[:, cols] = total[:, cols] * a + jnp.sum(p, 0, keepdims=True)
            v = qkv[128:192, pl.ds(pl.multiple_of(j * BK, BK), BK)]
            acc[:, cols] = acc[:, cols] * a + dot(v, p.astype(BF))

        every, later = slice(0, BQ), slice(BK, BQ)
        s0[...] = scores(0, every)

        def pair(jj, unused):
            s1[...] = scores(2 * jj + 1, every)
            fold(s0[...], 2 * jj, every)
            s0[...] = scores(2 * jj + 2, every)
            fold(s1[...], 2 * jj + 1, every)
            return unused

        lax.fori_loop(0, qi, pair, 0)
        last = scores(2 * qi + 1, later)
        fold(causal(s0[...], 0), 2 * qi, every)
        fold(causal(last, 0), 2 * qi + 1, later)
        o_full[:, at] = acc[...] / total[...]
        lse[:, at] = top[...] + jnp.log(total[...])
        return unused

    lax.fori_loop(0, S // BQ, q_block, 0)
    store_halves(ids, o_full, o_own, o_away)


def attend(ids, own, oth, tie):
    return pl.pallas_call(
        lambda *refs: attend_kernel(*refs[:3], *refs[4:]),
        out_shape=(
            jax.ShapeDtypeStruct((64, S), F32),
            jax.ShapeDtypeStruct((1, S), F32),
            jax.ShapeDtypeStruct((64, S // 2), BF),
            jax.ShapeDtypeStruct((64, S // 2), BF),
        ),
        in_specs=[SM, VM, VM, pl.BlockSpec(memory_space=pl.ANY)],
        out_specs=(VM,) * 4,
        scratch_shapes=[
            pltpu.VMEM((192, S), BF),
            pltpu.VMEM((S, 64), BF),
            pltpu.VMEM((64, BQ), BF),
            pltpu.VMEM((BK, BQ), F32),
            pltpu.VMEM((BK, BQ), F32),
            pltpu.VMEM((64, BQ), F32),
            pltpu.VMEM((1, BQ), F32),
            pltpu.VMEM((1, BQ), F32),
        ],
        compiler_params=pltpu.CompilerParams(vmem_limit_bytes=VMEM),
        cost_estimate=pl.CostEstimate(
            flops=8 * S * S * 64, bytes_accessed=4 << 20, transcendentals=S * S // 2
        ),
        name="attend",
    )(ids, own, oth, tie)


def unrotate(d, cos, sin):
    a, b = d[0:16], d[16:32]
    return jnp.concatenate([a * cos + b * sin, b * cos - a * sin, d[32:64]], 0)


class Back:
    def __init__(self, q, doT, kk, vv, kT, qq, dd, lse, o, dk, dv, work):
        self.q, self.doT, self.kk, self.vv, self.kT, self.qq, self.dd = q, doT, kk, vv, kT, qq, dd
        self.lse, self.o, self.dk, self.dv = lse, o, dk, dv
        self.s0, self.s1, self.t0, self.t1, self.acc, self.delta = work

    def products(self, qoff, j, half):
        ks = pl.ds(pl.multiple_of(j * BK, BK), BK)
        cols = pl.ds(pl.multiple_of(qoff + half, BK), BQ - half)
        return dot(self.kk[ks, :], self.q[:, cols]), dot(self.vv[ks, :], self.doT[:, cols])

    def fold(self, qoff, s, t, j, half):
        ks = pl.ds(pl.multiple_of(j * BK, BK), BK)
        cols = pl.ds(pl.multiple_of(qoff + half, BK), BQ - half)
        p = jnp.exp(s - self.lse[:, cols])
        ds = (p * (t - self.delta[:, half:])).astype(BF)
        self.dv[ks, :] += dot(p.astype(BF), self.dd[cols, :])
        self.dk[ks, :] += dot(ds, self.qq[cols, :])
        self.acc[:, half:] += dot(self.kT[:, ks], ds)

    def block(self, qi, pairs, diagonal, dq):
        qoff = pl.multiple_of(qi * BQ, BQ)
        at = pl.ds(qoff, BQ)
        self.delta[...] = jnp.sum(self.doT[:, at].astype(F32) * self.o[:, at], 0, keepdims=True)
        self.acc[...] = dq[:, at]
        self.s0[...], self.t0[...] = self.products(qoff, 0, 0)

        def pair(jj, unused):
            self.s1[...], self.t1[...] = self.products(qoff, 2 * jj + 1, 0)
            self.fold(qoff, self.s0[...], self.t0[...], 2 * jj, 0)
            self.s0[...], self.t0[...] = self.products(qoff, 2 * jj + 2, 0)
            self.fold(qoff, self.s1[...], self.t1[...], 2 * jj + 1, 0)
            return unused

        lax.fori_loop(0, pairs, pair, 0)

        @pl.when(diagonal)
        def _():
            s, t = self.products(qoff, 2 * qi + 1, BK)
            self.fold(qoff, causal(self.s0[...], 0), self.t0[...], 2 * qi, 0)
            self.fold(qoff, causal(s, 0), t, 2 * qi + 1, BK)

        dq[:, at] = self.acc[...]


def work_shapes():
    return [pltpu.VMEM((BK, BQ), F32)] * 4 + [pltpu.VMEM((64, BQ), F32), pltpu.VMEM((1, BQ), F32)]


def turned(qkv, doT, qq, kk, vv, dd, n):
    for j in range(n // 512):
        sl = slice(j * 512, (j + 1) * 512)
        qkv[0:64, sl] = qkv[0:64, sl] * jnp.asarray(0.125, BF)
        qq[sl, :] = qkv[0:64, sl].T
        kk[sl, :] = qkv[64:128, sl].T
        vv[sl, :] = qkv[128:192, sl].T
        dd[sl, :] = doT[:, sl].T


def finish(dq, dk, dv, cos, sin, out):
    for j in range(S // 1024):
        sl = slice(j * 512, (j + 1) * 512)
        out[0:64, sl] = unrotate(dq[:, sl] * 0.125, cos[:, sl], sin[:, sl]).astype(BF)
        out[64:128, sl] = unrotate(dk[sl, :].T, cos[:, sl], sin[:, sl]).astype(BF)
        out[128:192, sl] = dv[sl, :].T.astype(BF)


def far_kernel(
    ids, own, oth, do_own, do_oth, o_full, lse, cos, sin, d_away, pq, pk, pv,
    qkv, kk, vv, qq, doT, dd, dq, dk, dv, *work,
):
    h = ids[0]
    load_halves(ids, own, oth, qkv)
    load_halves(ids, do_own, do_oth, doT)
    turned(qkv, doT, qq, kk, vv, dd, S)
    dq[...] = jnp.zeros_like(dq)
    dk[...] = jnp.zeros_like(dk)
    dv[...] = jnp.zeros_like(dv)
    back = Back(
        qkv.at[0:64], doT, kk, vv, qkv.at[64:128], qq, dd, lse, o_full, dk, dv, work
    )

    def q_block(qi, unused):
        @pl.when(jnp.logical_or(h == 1, qi >= 2))
        def _():
            pairs = jnp.where(h == 0, qi, jnp.minimum(qi, 2))
            back.block(qi, pairs, jnp.logical_or(h == 0, qi < 2), dq)

        return unused

    lax.fori_loop(0, S // BQ, q_block, 0)
    half = S // 2
    there = pl.ds(pl.multiple_of((1 - h) * half, half), half)
    here = pl.ds(pl.multiple_of(h * half, half), half)
    finish(dq.at[:, there], dk.at[there], dv.at[there], cos, sin, d_away)
    pq[...] = dq[:, here]
    pk[...] = dk[here, :]
    pv[...] = dv[here, :]


def attend_back_far(ids, own, oth, do_own, do_oth, o_full, lse, cos, sin, tie):
    half = S // 2
    return pl.pallas_call(
        lambda *refs: far_kernel(*refs[:9], *refs[10:]),
        out_shape=(
            jax.ShapeDtypeStruct((192, half), BF),
            jax.ShapeDtypeStruct((64, half), F32),
            jax.ShapeDtypeStruct((half, 64), F32),
            jax.ShapeDtypeStruct((half, 64), F32),
        ),
        in_specs=[SM] + [VM] * 8 + [pl.BlockSpec(memory_space=pl.ANY)],
        out_specs=(VM,) * 4,
        scratch_shapes=[
            pltpu.VMEM((192, S), BF),
            pltpu.VMEM((S, 64), BF),
            pltpu.VMEM((S, 64), BF),
            pltpu.VMEM((S, 64), BF),
            pltpu.VMEM((64, S), BF),
            pltpu.VMEM((S, 64), BF),
            pltpu.VMEM((64, S), F32),
            pltpu.VMEM((S, 64), F32),
            pltpu.VMEM((S, 64), F32),
        ]
        + work_shapes(),
        compiler_params=pltpu.CompilerParams(vmem_limit_bytes=VMEM),
        cost_estimate=pl.CostEstimate(
            flops=14 * S * S * 64, bytes_accessed=6 << 20, transcendentals=S * S // 2
        ),
        name="attend_back_far",
    )(ids, own, oth, do_own, do_oth, o_full, lse, cos, sin, tie)


def near_kernel(
    ids, own, do_own, o_full, lse, cos, sin, pq, pk, pv, d_own,
    qkv, kk, vv, qq, dd, dq, dk, dv, *work,
):
    half = S // 2
    here = pl.ds(pl.multiple_of(ids[0] * half, half), half)
    qkv[...] = own[...]
    turned(qkv, do_own, qq, kk, vv, dd, half)
    dq[...] = pq[...]
    dk[...] = pk[...]
    dv[...] = pv[...]
    back = Back(
        qkv.at[0:64], do_own, kk, vv, qkv.at[64:128], qq, dd,
        lse.at[:, here], o_full.at[:, here], dk, dv, work,
    )

    def q_block(qi, unused):
        back.block(qi, qi, qi >= 0, dq)
        return unused

    lax.fori_loop(0, half // BQ, q_block, 0)
    finish(dq, dk, dv, cos, sin, d_own)


def attend_back_near(ids, own, do_own, o_full, lse, cos, sin, partial, *ties):
    half = S // 2
    n = len(ties)
    return pl.pallas_call(
        lambda *refs: near_kernel(*refs[:10], *refs[10 + n :]),
        out_shape=jax.ShapeDtypeStruct((192, half), BF),
        in_specs=[SM] + [VM] * 9 + [pl.BlockSpec(memory_space=pl.ANY)] * n,
        out_specs=VM,
        scratch_shapes=[
            pltpu.VMEM((192, half), BF),
            pltpu.VMEM((half, 64), BF),
            pltpu.VMEM((half, 64), BF),
            pltpu.VMEM((half, 64), BF),
            pltpu.VMEM((half, 64), BF),
            pltpu.VMEM((64, half), F32),
            pltpu.VMEM((half, 64), F32),
            pltpu.VMEM((half, 64), F32),
        ]
        + work_shapes(),
        compiler_params=pltpu.CompilerParams(vmem_limit_bytes=VMEM),
        cost_estimate=pl.CostEstimate(
            flops=6 * S * S * 64, bytes_accessed=6 << 20, transcendentals=S * S // 2
        ),
        name="attend_back_near",
    )(ids, own, do_own, o_full, lse, cos, sin, *partial, *ties)


ANY = pl.BlockSpec(memory_space=pl.ANY)
DMA = pltpu.SemaphoreType.DMA
NT = ((1,), (1,))
TN = ((0,), (0,))


def call(kernel, name, inputs, specs, outs, scratch, flops=0, moved=0, ties=(), out_specs=None):
    shapes = tuple(jax.ShapeDtypeStruct(shape, kind) for shape, kind in outs)
    n, k = len(inputs), len(ties)

    def body(*refs):
        kernel(*refs[:n], *refs[n + k :])

    return pl.pallas_call(
        body,
        out_shape=shapes,
        in_specs=list(specs) + [ANY] * k,
        out_specs=out_specs or (VM,) * len(outs),
        scratch_shapes=scratch,
        compiler_params=pltpu.CompilerParams(vmem_limit_bytes=VMEM),
        cost_estimate=pl.CostEstimate(flops=flops, bytes_accessed=moved, transcendentals=0),
        name=name,
    )(*inputs, *ties)


def hold(v, *ties):
    return pl.pallas_call(
        lambda *refs: None,
        out_shape=jax.ShapeDtypeStruct(v.shape, v.dtype),
        in_specs=[ANY] * (1 + len(ties)),
        out_specs=ANY,
        input_output_aliases={0: 0},
        name="hold",
    )(v, *ties)


def start_rows_in(src, dst, sems):
    for i in range(8):
        at = pl.ds(i * 256, 256)
        pltpu.make_async_copy(src.at[at], dst.at[at], sems.at[i]).start()


def wait_piece(dst, sems, i):
    rows = dst.at[pl.ds(pl.multiple_of(i * 256, 256), 256)]
    pltpu.make_async_copy(rows, rows, sems.at[i]).wait()


def pack_kernel(w, vec, w2, wd, msg, rows):
    v = jnp.concatenate([vec[...], jnp.zeros((5, 64), F32)], 0).astype(BF)
    for d in range(16):
        hd, zcd = d // 8, d % 8
        for part in range(2):
            block = (hd if part == 0 else 1 - hd) * 8 + zcd
            for t in range(3):
                col = t * 1024 + block * 64
                at = part * 192 + t * 64
                msg[d, 0:64, at : at + 64] = w[:, col : col + 64].astype(BF)
        msg[d, 64:80, :] = jnp.zeros((16, 384), BF)
        msg[d, 64:80, 0:64] = v
    rows[0:256, :] = w2[...].astype(BF)
    rows[256:320, :] = wd[...].astype(BF)


def pack(w, vec, w2, wd):
    outs = [((16, 80, 384), BF), ((320, 1024), BF)]
    return call(pack_kernel, "pack", (w, vec, w2, wd), [VM] * 4, outs, [], 0, 4 << 20)


def pack_up_kernel(w1, msg):
    for d in range(16):
        hd, zcd = d // 8, d % 8
        for part in range(2):
            block = (hd if part == 0 else 1 - hd) * 8 + zcd
            msg[d, :, part * 256 : part * 256 + 256] = w1[:, block * 256 : block * 256 + 256].astype(BF)


def pack_up(w1, *ties):
    return call(pack_up_kernel, "pack_up", (w1,), [VM], [((16, 64, 512), BF)], [], 0, 4 << 20, ties)[0]


def copy_kernel(src, dst):
    dst[...] = src[...]


def after(v, *ties):
    return call(copy_kernel, "after", (v,), [VM], [(v.shape, v.dtype)], [], 0, 1 << 20, ties)[0]


def normalize(values):
    middle = jnp.mean(values, -1, keepdims=True)
    centered = values - middle
    spread = jnp.mean(centered * centered, -1, keepdims=True)
    inverse = lax.rsqrt(spread + 1e-05)
    return (centered * inverse, inverse)


def rotate(cos, sin, mixed):
    out = []
    for n in (0, 64):
        a, b = mixed[n : n + 16], mixed[n + 16 : n + 32]
        out += [a * cos - b * sin, b * cos + a * sin, mixed[n + 32 : n + 64]]
    return jnp.concatenate(out + [mixed[128:]], 0).astype(BF)


def project_kernel(ids, msg, cos, sin, x_ref, hidden, here, away, vec, b1, w_qkv, raw, xs, sems):
    h, zc = ids[0], 2 * ids[1] + ids[2]
    start_rows_in(x_ref, xs, sems)
    for s in range(16):
        w_qkv[s * 64 : (s + 1) * 64, :] = msg[s, 0:64, 0:384]
        v = msg[s, 64:80, 0:64].astype(F32)
        raw[s] = v
        vec[:, s * 64 : (s + 1) * 64] = v
    own, oth = h * 8 + zc, (1 - h) * 8 + zc
    v_own, v_oth = raw[own], raw[oth]
    bias = jnp.concatenate(
        [v_own[t : t + 1, :] for t in range(3)] + [v_oth[t : t + 1, :] for t in range(3)], 1
    )
    for n, i in enumerate((own, oth)):
        for j in range(4):
            at = n * 256 + j * 64
            b1[:, at : at + 64] = raw[4 * lax.rem(i, 4) + j, pl.ds(4 + i // 4, 1), :]
    gain, shift = vec[9:10, :], vec[10:11, :]

    def pair(n, unused):
        for i in range(2):
            wait_piece(xs, sems, 2 * n + i)
        at = pl.ds(pl.multiple_of(n * 512, 512), 512)
        normed, unused_inverse = normalize(xs[at, :].astype(F32))
        hid = (normed * gain + shift).astype(BF)
        hidden[at, :] = hid
        mixed = (dot(hid, w_qkv[...]) + bias).T
        here[:, at] = rotate(cos[:, at], sin[:, at], mixed[:192])
        away[:, at] = rotate(cos[:, at], sin[:, at], mixed[192:])
        return unused

    lax.fori_loop(0, 4, pair, 0)


def project(ids, msg, cos, sin, x_all, *ties):
    outs = [
        ((2048, 1024), BF),
        ((192, 2048), BF),
        ((192, 2048), BF),
        ((16, 1024), F32),
        ((1, 512), F32),
        ((1024, 384), BF),
    ]
    scratch = [pltpu.VMEM((16, 16, 64), F32), pltpu.VMEM((2048, 1024), BF), DMA((8,))]
    inputs = (ids, msg, cos, sin, x_all)
    return call(
        project_kernel, "project", inputs, [SM, VM, VM, VM, ANY], outs, scratch,
        4 * 2048 * 1024 * 384, 12 << 20, ties,
    )


def rows_kernel(rows, rows_x, g_ref, do_here, do_away, gs, wd, sems):
    start_rows_in(g_ref, gs, sems)
    wd[0:64, :] = rows[256:320, :]
    wd[64:128, :] = rows_x[256:320, :]

    def pair(n, unused):
        for i in range(2):
            wait_piece(gs, sems, 2 * n + i)
        at = pl.ds(pl.multiple_of(n * 512, 512), 512)
        both = dot(gs[at, :], wd[...], NT).T.astype(BF)
        do_here[:, at] = both[:64]
        do_away[:, at] = both[64:]
        return unused

    lax.fori_loop(0, 4, pair, 0)


def attended_back(rows, rows_x, g_all, *ties):
    outs = [((64, 2048), BF)] * 2
    scratch = [pltpu.VMEM((2048, 1024), BF), pltpu.VMEM((128, 1024), BF), DMA((8,))]
    return call(
        rows_kernel, "attended_back", (rows, rows_x, g_all), [VM, VM, ANY], outs, scratch,
        4 * 2048 * 1024 * 128, 6 << 20, ties,
    )


ROOT = 0.7978845608028654


def units_kernel(hid_ref, w1, b1, act, slope, hs, sems):
    start_rows_in(hid_ref, hs, sems)

    def block(n, unused):
        for i in range(2):
            wait_piece(hs, sems, 2 * n + i)
        at = pl.ds(pl.multiple_of(n * 512, 512), 512)
        u = dot(hs[at, :], w1[...]) + b1[...]
        square = u * u
        th = jnp.tanh(ROOT * u * (1.0 + 0.044715 * square))
        half = 0.5 * (1.0 + th)
        act[at, :] = (u * half).astype(BF)
        back = half + 0.5 * u * (1.0 - th * th) * (ROOT * (1.0 + 3.0 * 0.044715 * square))
        slope[at, :] = back.astype(BF)
        return unused

    lax.fori_loop(0, 4, block, 0)


def units(hidden, w1, b1, *ties):
    outs = [((2048, 512), BF), ((2048, 512), BF)]
    scratch = [pltpu.VMEM((2048, 1024), BF), DMA((8,))]
    return call(
        units_kernel, "units", (hidden, w1, b1), [ANY, VM, VM], outs, scratch,
        2 * 2048 * 1024 * 512, 11 << 20, ties,
    )


def along_rows(w, grad, bias):
    first = jnp.sum(w * grad, 1, keepdims=True)
    second = jnp.sum(w * bias, 1, keepdims=True)
    lane = lax.broadcasted_iota(jnp.int32, (1024, 128), 1)
    return jnp.where(lane == 0, first, second).T[0:2, :]


def units_back_kernel(ids, hid_ref, act, slope_ref, rows, rows_x, w1, g_ref, *refs):
    dup, msg, gb1, along = refs[:4]
    hs, gs, ss, w2, acc1, acc2, sems, hsems, ssems = refs[4:]
    h = ids[0]
    start_rows_in(g_ref, gs, sems)
    start_rows_in(slope_ref, ss, ssems)
    start_rows_in(hid_ref, hs, hsems)
    w2[0:256, :] = rows[0:256, :]
    w2[256:512, :] = rows_x[0:256, :]
    acc1[...] = jnp.zeros_like(acc1)
    acc2[...] = jnp.zeros_like(acc2)
    gb1[...] = jnp.zeros_like(gb1)


    def block(n, unused):
        for i in range(2):
            wait_piece(gs, sems, 2 * n + i)
            wait_piece(ss, ssems, 2 * n + i)
            wait_piece(hs, hsems, 2 * n + i)
        at = pl.ds(pl.multiple_of(n * 512, 512), 512)
        hid, g = hs[at, :], gs[at, :]
        back_b = (dot(g, w2[...], NT) * ss[at, :].astype(F32)).astype(BF)
        dup[at, :] = back_b
        gb1[...] += jnp.sum(back_b.astype(F32), 0, keepdims=True)
        acc2[...] += dot(act[at, :], g, TN)
        acc1[...] += dot(hid, back_b, TN)
        return unused

    lax.fori_loop(0, 4, block, 0)
    along[...] = along_rows(w1[...].astype(F32), acc1[...], gb1[...])
    for p in range(8):
        for hd in range(2):
            rows_at = slice(hd * 512 + p * 64, hd * 512 + p * 64 + 64)
            for part in range(2):
                hh = h if part == 0 else 1 - h
                msg[2 * p + hd, pl.ds(pl.multiple_of(hh * 64, 64), 64), :] = acc1[
                    rows_at, part * 256 : part * 256 + 256
                ].astype(BF)
        for part in range(2):
            hh = h if part == 0 else 1 - h
            for q in range(4):
                msg[2 * p + hh, 128 + q * 32 : 160 + q * 32, :] = acc2[
                    part * 256 + p * 32 : part * 256 + p * 32 + 32, q * 256 : q * 256 + 256
                ].astype(BF)


def units_back(ids, hidden, act, slope, rows, rows_x, w1, g_all, *ties):
    outs = [((2048, 512), BF), ((16, 256, 256), BF), ((1, 512), F32), ((2, 1024), F32)]
    scratch = [
        pltpu.VMEM((2048, 1024), BF),
        pltpu.VMEM((2048, 1024), BF),
        pltpu.VMEM((2048, 512), BF),
        pltpu.VMEM((512, 1024), BF),
        pltpu.VMEM((1024, 512), F32),
        pltpu.VMEM((512, 1024), F32),
        DMA((8,)),
        DMA((8,)),
        DMA((8,)),
    ]
    return call(
        units_back_kernel, "units_back", (ids, hidden, act, slope, rows, rows_x, w1, g_all),
        [SM, ANY, VM, ANY, VM, VM, VM, ANY], outs, scratch, 6 * 2048 * 1024 * 512, 18 << 20, ties,
    )


def start_rows_out(src, n, to, sems):
    at = pl.ds(n * 512, 512)
    copy = pltpu.make_async_copy(src.at[at], to.at[at], sems.at[n])
    copy.start()
    return copy


def unit_parts_kernel(act, rows, rows_x, dup, w1, part_out, part_in, out, back, sems, bsems):
    copies = []
    for n in range(4):
        at = slice(n * 512, n * 512 + 512)
        part = dot(act[at, 0:256], rows[0:256, :]) + dot(act[at, 256:512], rows_x[0:256, :])
        out[at, :] = part.astype(BF)
        copies.append(start_rows_out(out, n, part_out, sems))
        back[at, :] = dot(dup[at, :], w1[...], NT).astype(BF)
        copies.append(start_rows_out(back, n, part_in, bsems))
    for copy in copies:
        copy.wait()


def unit_parts(act, rows, rows_x, dup, w1, *ties):
    outs = [((2048, 1024), BF)] * 2
    scratch = [pltpu.VMEM((2048, 1024), BF)] * 2 + [DMA((4,))] * 2
    return call(
        unit_parts_kernel, "unit_parts", (act, rows, rows_x, dup, w1), [VM] * 5, outs, scratch,
        4 * 2048 * 1024 * 512, 14 << 20, ties, (ANY, ANY),
    )


def out_kernel(ids, part_ref, rows, rows_x, o_here, o_came, g_ref, total, gd, gs, both, part, out, sems, psems, osems):
    h = ids[0]
    start_rows_in(part_ref, part, psems)
    start_rows_in(g_ref, gs, sems)
    both[0:64, :] = o_here[...]
    both[64:128, :] = o_came[...]
    wd = jnp.concatenate([rows[256:320, :], rows_x[256:320, :]], 0)
    copies = []
    for n in range(4):
        at = slice(n * 512, n * 512 + 512)
        more = dot(both[:, at], wd, TN)
        wait_piece(part, psems, 2 * n)
        wait_piece(part, psems, 2 * n + 1)
        out[at, :] = (part[at, :].astype(F32) + more).astype(BF)
        copies.append(start_rows_out(out, n, total, osems))
    for i in range(8):
        wait_piece(gs, sems, i)
    grad = dot(both[...], gs[...]).astype(BF)
    gd[h] = grad[:64]
    gd[1 - h] = grad[64:]
    for copy in copies:
        copy.wait()


def out_part(ids, part, rows, rows_x, o_here, o_came, g_all, *ties):
    outs = [((2048, 1024), BF), ((2, 64, 1024), BF)]
    scratch = [
        pltpu.VMEM((2048, 1024), BF),
        pltpu.VMEM((128, 2048), BF),
        pltpu.VMEM((2048, 1024), BF),
        pltpu.VMEM((2048, 1024), BF),
        DMA((8,)),
        DMA((8,)),
        DMA((4,)),
    ]
    return call(
        out_kernel, "out_part", (ids, part, rows, rows_x, o_here, o_came, g_all),
        [SM, ANY] + [VM] * 4 + [ANY], outs, scratch, 4 * 2048 * 1024 * 128, 12 << 20, ties,
        (ANY, VM),
    )


def late_kernel(ids, d_here, d_came, w_qkv, hid_ref, g_own, gb1, gd, along, vin, msg, hs, both, gq, vec, sems):
    h, zc = ids[0], 2 * ids[1] + ids[2]
    start_rows_in(hid_ref, hs, sems)
    both[0:192, :] = d_here[...]
    both[192:384, :] = d_came[...]
    ones = jnp.ones((8, 2048), BF)
    bias = dot(ones, both[...], NT)[0:1]
    for i in range(8):
        wait_piece(hs, sems, i)
    grad = dot(both[...], hs[...])
    turned = grad.T
    sums = along[...] + along_rows(w_qkv[...].astype(F32), turned, bias)
    gq[pl.ds(pl.multiple_of(h * 192, 64), 192), :] = grad[:192]
    gq[pl.ds(pl.multiple_of((1 - h) * 192, 64), 192), :] = grad[192:]
    own, oth = h * 8 + zc, (1 - h) * 8 + zc
    lane = lax.broadcasted_iota(jnp.int32, (1, 1024), 1)
    out_sum = jnp.sum(g_own[...].astype(F32), 0, keepdims=True)
    rows = []
    for t in range(3):
        a = jnp.concatenate([bias[:, t * 64 : t * 64 + 64]] * 16, 1)
        b = jnp.concatenate([bias[:, 192 + t * 64 : 256 + t * 64]] * 16, 1)
        rows.append(jnp.where(lane // 64 == own, a, 0.0) + jnp.where(lane // 64 == oth, b, 0.0))
    rows.append(out_sum)
    a = jnp.concatenate([gb1[:, 0:256]] * 4, 1)
    b = jnp.concatenate([gb1[:, 256:512]] * 4, 1)
    for r in range(4):
        block = lane // 256 + 4 * r
        rows.append(jnp.where(block == own, a, 0.0) + jnp.where(block == oth, b, 0.0))
    shift_sum = sums[1:2, :]
    gain_sum = (sums[0:1, :] - vin[10:11, :] * shift_sum) / vin[9:10, :]
    rows += [out_sum, gain_sum, shift_sum]
    for r, row in enumerate(rows):
        vec[r : r + 1, :] = row
    flat = gq[...].T
    zeros = jnp.zeros((8, 64), F32)
    for p in range(8):
        for hd in range(2):
            at = hd * 512 + p * 64
            msg[2 * p + hd, 0:64, :] = flat[at : at + 64, :].astype(BF)
            cols = slice((hd * 8 + p) * 64, (hd * 8 + p) * 64 + 64)
            v0 = vec[0:8, cols]
            v1 = vec[8:16, cols]
            vrows = jnp.concatenate([v0, zeros, v1, zeros, zeros, zeros], 1)
            d = gd[hd, p * 8 : p * 8 + 8, :].astype(F32)
            d2 = jnp.concatenate([d[:, 768:1024], jnp.zeros((8, 128), F32)], 1)
            tail = jnp.concatenate([vrows, d[:, 0:384], d[:, 384:768], d2], 0)
            msg[2 * p + hd, 64:96, :] = tail.astype(BF)


def late_part(ids, d_here, d_came, w_qkv, hidden, g_own, gb1, gd, along, vec, *ties):
    scratch = [
        pltpu.VMEM((2048, 1024), BF),
        pltpu.VMEM((384, 2048), BF),
        pltpu.VMEM((384, 1024), F32),
        pltpu.VMEM((16, 1024), F32),
        DMA((8,)),
    ]
    return call(
        late_kernel, "late_part", (ids, d_here, d_came, w_qkv, hidden, g_own, gb1, gd, along, vec),
        [SM] + [VM] * 3 + [ANY] + [VM] * 5, [((16, 96, 384), BF)], scratch,
        2 * 2048 * 1024 * 384, 8 << 20, ties,
    )[0]


def hidden_kernel(d_here, d_came, w_qkv, part_ref, total, both, part, out, sems, osems):
    start_rows_in(part_ref, part, sems)
    both[0:192, :] = d_here[...]
    both[192:384, :] = d_came[...]
    copies = []
    for n in range(4):
        at = slice(n * 512, n * 512 + 512)
        more = dot(both[:, at].T, w_qkv[...], NT)
        wait_piece(part, sems, 2 * n)
        wait_piece(part, sems, 2 * n + 1)
        out[at, :] = (part[at, :].astype(F32) + more).astype(BF)
        copies.append(start_rows_out(out, n, total, osems))
    for copy in copies:
        copy.wait()


def hidden_part(d_here, d_came, w_qkv, part, *ties):
    scratch = [
        pltpu.VMEM((384, 2048), BF),
        pltpu.VMEM((2048, 1024), BF),
        pltpu.VMEM((2048, 1024), BF),
        DMA((8,)),
        DMA((4,)),
    ]
    return call(
        hidden_kernel, "hidden_part", (d_here, d_came, w_qkv, part), [VM] * 3 + [ANY], [((2048, 1024), BF)], scratch,
        2 * 2048 * 1024 * 384, 10 << 20, ties, (ANY,),
    )[0]


SWAP = [(0, 1), (1, 0)]
GROUP = ("z", "core")
MODEL = ("xhi", "z", "core")
BATCH = ("xlo", "y")
SUM = ("xlo", "y", "xhi")


def swap_core(v):
    return lax.ppermute(v, "core", SWAP)


def swap_x(v):
    return lax.ppermute(v, "xhi", SWAP)


def group_sum(v):
    return lax.psum_scatter(v, GROUP, scatter_dimension=0, tiled=True)


def sum_kernel(n, parts, lo, hi, ps, sems):
    for i in range(8):
        at = pl.ds(2 * i, 2)
        pltpu.make_async_copy(parts.at[at], ps.at[at], sems.at[i]).start()
    total = None
    for i in range(8):
        at = pl.ds(2 * i, 2)
        pltpu.make_async_copy(ps.at[at], ps.at[at], sems.at[i]).wait()
        pair = ps[2 * i].astype(F32) + ps[2 * i + 1].astype(F32)
        total = pair if total is None else total + pair
    lo[...] = total[:n].astype(BF)
    hi[...] = total[n:].astype(BF)


def sum_parts(parts, n, *ties):
    rows, columns = parts.shape[1:]
    outs = [((n, columns), BF), ((rows - n, columns), BF)]
    scratch = [pltpu.VMEM(parts.shape, BF), DMA((8,))]
    return call(functools.partial(sum_kernel, n), "sum_parts", (parts,), [ANY], outs, scratch, 0, 2 << 20, ties)


def fan_kernel(lo, hi, out):
    n = lo.shape[0]
    for p in range(8):
        out[p, 0:n, :] = lo[...]
        out[p, n:, :] = hi[...]


def fan(lo, hi, *ties):
    shape = (8, lo.shape[0] + hi.shape[0], lo.shape[1])
    return call(fan_kernel, "fan", (lo, hi), [VM] * 2, [(shape, BF)], [], 0, 2 << 20, ties)[0]


def turn(v):
    return lax.ppermute(v, ("xlo", "y", "z", "core"), [(p * 8 + m, m * 8 + p) for p in range(8) for m in range(8)])


def tables(positions):
    freqs = 10000.0 ** (-(jnp.arange(ROT // 2, dtype=F32) * 2.0) / ROT)
    angles = positions.astype(F32)[None, :] * freqs[:, None]
    return (jnp.cos(angles), jnp.sin(angles))


def adamw(master, grad, first, second, rate):
    first_new = 0.9 * first + 0.1 * grad
    second_new = 0.95 * second + 0.05 * grad * grad
    first_hat = first_new / (1.0 - 0.9**STEP)
    second_hat = second_new / (1.0 - 0.95**STEP)
    fresh = master - rate * (first_hat / (jnp.sqrt(second_hat) + 1e-08) + 0.1 * master)
    return (fresh, first_new, second_new)


RATE = 2.0 * D ** (-0.5)
RATE_DOWN = 2.0 * FF ** (-0.5)


def update_units_kernel(early, w1, m1, v1, w2, m2, v2, w1n, m1n, v1n, w2n, m2n, v2n):
    for p in range(8):
        for hh in range(2):
            at = slice((hh * 8 + p) * 256, (hh * 8 + p) * 256 + 256)
            grad = early[p, hh * 64 : hh * 64 + 64, :].astype(F32)
            w1n[:, at], m1n[:, at], v1n[:, at] = adamw(w1[:, at], grad, m1[:, at], v1[:, at], RATE)
        for q in range(4):
            at = (slice(p * 32, p * 32 + 32), slice(q * 256, q * 256 + 256))
            grad = early[p, 128 + q * 32 : 160 + q * 32, :].astype(F32)
            w2n[at], m2n[at], v2n[at] = adamw(w2[at], grad, m2[at], v2[at], RATE_DOWN)


def update_units(early, *state, ties=()):
    outs = [((64, 4096), F32)] * 3 + [((256, 1024), F32)] * 3
    return call(update_units_kernel, "update_units", (early,) + state, [VM] * 7, outs, [], 0, 13 << 20, ties)


def update_heads_kernel(late, w, m, v, wd, md, vd, vec, mv, vv, wn, mn, vn, wdn, mdn, vdn, vecn, mvn, vvn, gq, gd):
    for zc in range(8):
        for hh in range(2):
            for t in range(3):
                col = t * 1024 + (hh * 8 + zc) * 64
                at = hh * 192 + t * 64
                gq[:, col : col + 64] = late[zc, 0:64, at : at + 64].astype(F32)
        rows = late[zc, 64:96, :].astype(F32)
        gd[zc * 8 : zc * 8 + 8, 0:384] = rows[8:16]
        gd[zc * 8 : zc * 8 + 8, 384:768] = rows[16:24]
        gd[zc * 8 : zc * 8 + 8, 768:1024] = rows[24:32, 0:256]
        total = rows[0:8] if zc == 0 else total + rows[0:8]
    grad = jnp.concatenate([total[:, 0:64], total[0:3, 128:192]], 0)
    wn[...], mn[...], vn[...] = adamw(w[...], gq[...], m[...], v[...], RATE)
    wdn[...], mdn[...], vdn[...] = adamw(wd[...], gd[...], md[...], vd[...], RATE)
    vecn[...], mvn[...], vvn[...] = adamw(vec[...], grad, mv[...], vv[...], 0.3)


def update_heads(late, *state):
    outs = [((64, 3072), F32)] * 3 + [((64, 1024), F32)] * 3 + [((11, 64), F32)] * 3
    scratch = [pltpu.VMEM((64, 3072), F32), pltpu.VMEM((64, 1024), F32)]
    return call(update_heads_kernel, "update_heads", (late,) + state, [VM] * 10, outs, scratch, 0, 7 << 20)


def input_kernel(came, x, g, vec, out):
    total = came[...].astype(F32)
    normed, inverse = normalize(x[...].astype(F32))
    back = total * vec[9:10, :]
    mean = jnp.mean(back, -1, keepdims=True)
    along = jnp.mean(back * normed, -1, keepdims=True)
    out[...] = (g[...].astype(F32) + inverse * (back - mean - normed * along)).astype(BF)


def input_part(blocks, x, g, vec, *ties):
    inputs = (blocks, x, g, vec)
    return call(input_kernel, "input_part", inputs, [VM] * 4, [((256, 1024), BF)], [], 0, 4 << 20, ties)[0]


def output_kernel(came, x, vec, out):
    total = came[...].astype(F32)
    out[...] = (x[...].astype(F32) + total + (vec[3:4, :] + vec[8:9, :])).astype(BF)


def output_part(blocks, x, vec, *ties):
    inputs = (blocks, x, vec)
    return call(output_kernel, "output_part", inputs, [VM] * 3, [((256, 1024), BF)], [], 0, 4 << 20, ties)[0]


def local(
    tokens,
    cotangent,
    qkv_weight,
    dense_weight,
    fc1_weight,
    fc2_weight,
    vectors,
    qkv_first,
    dense_first,
    fc1_first,
    fc2_first,
    vectors_first,
    qkv_second,
    dense_second,
    fc1_second,
    fc2_second,
    vectors_second,
):
    h, z, c = lax.axis_index("xhi"), lax.axis_index("z"), lax.axis_index("core")
    ids = jnp.stack([h, z, c, lax.axis_index(BATCH)]).astype(jnp.int32)
    x_own = tokens[0]
    g_own = cotangent[0]

    cos_all, sin_all = tables(jnp.arange(S, dtype=jnp.int32))
    cos_here = lax.dynamic_slice_in_dim(cos_all, h * (S // 2), S // 2, 1)
    sin_here = lax.dynamic_slice_in_dim(sin_all, h * (S // 2), S // 2, 1)
    cos_away = lax.dynamic_slice_in_dim(cos_all, (1 - h) * (S // 2), S // 2, 1)
    sin_away = lax.dynamic_slice_in_dim(sin_all, (1 - h) * (S // 2), S // 2, 1)

    x_all = lax.all_gather(x_own, GROUP, axis=0, tiled=True)
    msg, rows = pack(qkv_weight, vectors, fc2_weight, dense_weight)
    msg = lax.all_to_all(msg, MODEL, 0, 0, tiled=True)
    rows_x = swap_x(rows)
    up_msg = pack_up(fc1_weight, cos_here, sin_here, cos_away, sin_away, ids)
    w1 = lax.all_to_all(hold(up_msg, x_all), MODEL, 0, 0, tiled=True).reshape(1024, 512)
    g_all = lax.all_gather(hold(g_own, x_all, msg, rows_x, up_msg), GROUP, axis=0, tiled=True)
    hidden, here, away, vec, b1, w_qkv = project(
        ids, msg, cos_here, sin_here, x_all
    )
    came = swap_x(away)
    act, slope = units(hidden, w1, b1, away)
    do_here, do_away = attended_back(rows, rows_x, g_all, act)
    do_came = swap_x(do_away)
    dup, early, gb1, along = units_back(
        ids, hidden, act, slope, rows, rows_x, w1, g_all, came, do_away
    )
    early = lax.all_to_all(hold(early, do_came), SUM, 0, 0, tiled=True)

    o_full, lse, o_here, o_away = attend(ids, here, came, dup)
    o_came = swap_x(o_away)
    part_out, part_in = unit_parts(act, rows, rows_x, dup, w1, o_away)
    total, gd = out_part(
        ids, part_out, rows, rows_x, o_here, o_came, g_all
    )
    early_turn, early_stay = sum_parts(early, 128, gd)
    out_sum = group_sum(hold(total, early_stay))
    early_turn = turn(early_turn)
    d_away, *partial = attend_back_far(
        ids, here, came, do_here, do_came, o_full, lse, cos_away, sin_away, early_stay
    )
    d_came = swap_x(d_away)
    early = fan(early_turn, early_stay, d_away)
    d_here = attend_back_near(ids, here, do_here, o_full, lse, cos_here, sin_here, partial, early)
    late = late_part(ids, d_here, d_came, w_qkv, hidden, g_own, gb1, gd, along, vec, early)
    early = lax.all_to_all(early, BATCH, 0, 0, tiled=True)
    late = hold(late, early)
    total = hidden_part(d_here, d_came, w_qkv, part_in, late)
    hidden_sum = group_sum(total)
    late = lax.all_to_all(late, SUM, 0, 0, tiled=True)
    new1 = update_units(
        early,
        *(fc1_weight, fc1_first, fc1_second, fc2_weight, fc2_first, fc2_second),
        ties=(total,),
    )
    output = output_part(out_sum, x_own, vec, new1[0])
    late_turn, late_stay = sum_parts(late, 72, output)
    late = fan(turn(late_turn), late_stay)
    input_grad = input_part(hidden_sum, x_own, g_own, vec, late)
    late = lax.all_to_all(late, BATCH, 0, 0, tiled=True)
    new2 = update_heads(
        hold(late, input_grad),
        *(qkv_weight, qkv_first, qkv_second),
        *(dense_weight, dense_first, dense_second),
        *(vectors, vectors_first, vectors_second),
    )
    news = [(new2[j], new2[3 + j], new1[j], new1[3 + j], new2[6 + j]) for j in range(3)]
    return (output[None], input_grad[None]) + news[0] + news[1] + news[2]


def solution(mesh):
    fine = Mesh(mesh.devices.reshape(2, 4, 2, 4, 2), ("xlo", "y", "xhi", "z", "core"))
    dp, fsdp = ("xlo", "y"), ("xhi", "z", "core")
    token = P(dp, fsdp, None)
    row = P(fsdp, None)
    column = P(None, fsdp)
    params = (row, row, row, row, column)
    return jax.shard_map(
        local,
        mesh=fine,
        in_specs=(token, token) + params * 3,
        out_specs=(token, token) + params * 3,
        check_vma=False,
    )
```

```python
import functools

import jax
import jax.numpy as jnp
from jax import lax
from jax.experimental import pallas as pl
from jax.experimental.pallas import tpu as pltpu
from jax.sharding import Mesh
from jax.sharding import PartitionSpec as P

D = 1024
HEAD = 64
ROT = 32
FF = 4096
STEP = 10
S = 4096
NEG = -1e30
F32 = jnp.float32
BF = jnp.bfloat16


def dot(a, b, dims=((1,), (0,))):
    return lax.dot_general(a, b, (dims, ((), ())), preferred_element_type=F32)


def load_halves(ids, own, oth, dst):
    @pl.when(ids[0] == 0)
    def _():
        dst[:, 0 : S // 2] = own[...]
        dst[:, S // 2 : S] = oth[...]

    @pl.when(ids[0] == 1)
    def _():
        dst[:, 0 : S // 2] = oth[...]
        dst[:, S // 2 : S] = own[...]


def store_halves(ids, src, own, away):
    @pl.when(ids[0] == 0)
    def _():
        own[...] = src[:, 0 : S // 2].astype(own.dtype)
        away[...] = src[:, S // 2 : S].astype(own.dtype)

    @pl.when(ids[0] == 1)
    def _():
        away[...] = src[:, 0 : S // 2].astype(own.dtype)
        own[...] = src[:, S // 2 : S].astype(own.dtype)


VMEM = 60 << 20
VM = pl.BlockSpec(memory_space=pltpu.VMEM)
SM = pl.BlockSpec(memory_space=pltpu.SMEM)
BQ = 1024
BK = 512


def causal(s, shift):
    kp = shift + lax.broadcasted_iota(jnp.int32, s.shape, 0)
    qp = lax.broadcasted_iota(jnp.int32, s.shape, 1)
    return jnp.where(kp <= qp, s, NEG)


def attend_kernel(ids, own, oth, o_full, lse, o_own, o_away, qkv, kk, qs, s0, s1, acc, top, total):
    load_halves(ids, own, oth, qkv)
    for j in range(8):
        sl = slice(j * 512, (j + 1) * 512)
        kk[sl, :] = qkv[64:128, sl].T

    def q_block(qi, unused):
        at = pl.ds(pl.multiple_of(qi * BQ, BQ), BQ)
        qs[...] = qkv[0:64, at] * jnp.asarray(0.125, BF)
        top[...] = jnp.full_like(top, NEG)
        total[...] = jnp.zeros_like(total)
        acc[...] = jnp.zeros_like(acc)

        def scores(j, cols):
            return dot(kk[pl.ds(pl.multiple_of(j * BK, BK), BK), :], qs[:, cols])

        def fold(s, j, cols):
            m = top[:, cols]
            m2 = jnp.maximum(m, jnp.max(s, 0, keepdims=True))
            p = jnp.exp(s - m2)
            a = jnp.exp(m - m2)
            top[:, cols] = m2
            total[:, cols] = total[:, cols] * a + jnp.sum(p, 0, keepdims=True)
            v = qkv[128:192, pl.ds(pl.multiple_of(j * BK, BK), BK)]
            acc[:, cols] = acc[:, cols] * a + dot(v, p.astype(BF))

        every, later = slice(0, BQ), slice(BK, BQ)
        s0[...] = scores(0, every)

        def pair(jj, unused):
            s1[...] = scores(2 * jj + 1, every)
            fold(s0[...], 2 * jj, every)
            s0[...] = scores(2 * jj + 2, every)
            fold(s1[...], 2 * jj + 1, every)
            return unused

        lax.fori_loop(0, qi, pair, 0)
        last = scores(2 * qi + 1, later)
        fold(causal(s0[...], 0), 2 * qi, every)
        fold(causal(last, 0), 2 * qi + 1, later)
        o_full[:, at] = acc[...] / total[...]
        lse[:, at] = top[...] + jnp.log(total[...])
        return unused

    lax.fori_loop(0, S // BQ, q_block, 0)
    store_halves(ids, o_full, o_own, o_away)


def attend(ids, own, oth, tie):
    return pl.pallas_call(
        lambda *refs: attend_kernel(*refs[:3], *refs[4:]),
        out_shape=(
            jax.ShapeDtypeStruct((64, S), F32),
            jax.ShapeDtypeStruct((1, S), F32),
            jax.ShapeDtypeStruct((64, S // 2), BF),
            jax.ShapeDtypeStruct((64, S // 2), BF),
        ),
        in_specs=[SM, VM, VM, pl.BlockSpec(memory_space=pl.ANY)],
        out_specs=(VM,) * 4,
        scratch_shapes=[
            pltpu.VMEM((192, S), BF),
            pltpu.VMEM((S, 64), BF),
            pltpu.VMEM((64, BQ), BF),
            pltpu.VMEM((BK, BQ), F32),
            pltpu.VMEM((BK, BQ), F32),
            pltpu.VMEM((64, BQ), F32),
            pltpu.VMEM((1, BQ), F32),
            pltpu.VMEM((1, BQ), F32),
        ],
        compiler_params=pltpu.CompilerParams(vmem_limit_bytes=VMEM),
        cost_estimate=pl.CostEstimate(
            flops=8 * S * S * 64, bytes_accessed=4 << 20, transcendentals=S * S // 2
        ),
        name="attend",
    )(ids, own, oth, tie)


def unrotate(d, cos, sin):
    a, b = d[0:16], d[16:32]
    return jnp.concatenate([a * cos + b * sin, b * cos - a * sin, d[32:64]], 0)


class Back:
    def __init__(self, q, doT, kk, vv, kT, qq, dd, lse, o, dk, dv, work):
        self.q, self.doT, self.kk, self.vv, self.kT, self.qq, self.dd = q, doT, kk, vv, kT, qq, dd
        self.lse, self.o, self.dk, self.dv = lse, o, dk, dv
        self.s0, self.s1, self.t0, self.t1, self.acc, self.delta = work

    def products(self, qoff, j, half):
        ks = pl.ds(pl.multiple_of(j * BK, BK), BK)
        cols = pl.ds(pl.multiple_of(qoff + half, BK), BQ - half)
        return dot(self.kk[ks, :], self.q[:, cols]), dot(self.vv[ks, :], self.doT[:, cols])

    def fold(self, qoff, s, t, j, half):
        ks = pl.ds(pl.multiple_of(j * BK, BK), BK)
        cols = pl.ds(pl.multiple_of(qoff + half, BK), BQ - half)
        p = jnp.exp(s - self.lse[:, cols])
        ds = (p * (t - self.delta[:, half:])).astype(BF)
        self.dv[ks, :] += dot(p.astype(BF), self.dd[cols, :])
        self.dk[ks, :] += dot(ds, self.qq[cols, :])
        self.acc[:, half:] += dot(self.kT[:, ks], ds)

    def block(self, qi, pairs, diagonal, dq):
        qoff = pl.multiple_of(qi * BQ, BQ)
        at = pl.ds(qoff, BQ)
        self.delta[...] = jnp.sum(self.doT[:, at].astype(F32) * self.o[:, at], 0, keepdims=True)
        self.acc[...] = dq[:, at]
        self.s0[...], self.t0[...] = self.products(qoff, 0, 0)

        def pair(jj, unused):
            self.s1[...], self.t1[...] = self.products(qoff, 2 * jj + 1, 0)
            self.fold(qoff, self.s0[...], self.t0[...], 2 * jj, 0)
            self.s0[...], self.t0[...] = self.products(qoff, 2 * jj + 2, 0)
            self.fold(qoff, self.s1[...], self.t1[...], 2 * jj + 1, 0)
            return unused

        lax.fori_loop(0, pairs, pair, 0)

        @pl.when(diagonal)
        def _():
            s, t = self.products(qoff, 2 * qi + 1, BK)
            self.fold(qoff, causal(self.s0[...], 0), self.t0[...], 2 * qi, 0)
            self.fold(qoff, causal(s, 0), t, 2 * qi + 1, BK)

        dq[:, at] = self.acc[...]


def work_shapes():
    return [pltpu.VMEM((BK, BQ), F32)] * 4 + [pltpu.VMEM((64, BQ), F32), pltpu.VMEM((1, BQ), F32)]


def turned(qkv, doT, qq, kk, vv, dd, n):
    for j in range(n // 512):
        sl = slice(j * 512, (j + 1) * 512)
        qkv[0:64, sl] = qkv[0:64, sl] * jnp.asarray(0.125, BF)
        qq[sl, :] = qkv[0:64, sl].T
        kk[sl, :] = qkv[64:128, sl].T
        vv[sl, :] = qkv[128:192, sl].T
        dd[sl, :] = doT[:, sl].T


def finish(dq, dk, dv, cos, sin, out):
    for j in range(S // 1024):
        sl = slice(j * 512, (j + 1) * 512)
        out[0:64, sl] = unrotate(dq[:, sl] * 0.125, cos[:, sl], sin[:, sl]).astype(BF)
        out[64:128, sl] = unrotate(dk[sl, :].T, cos[:, sl], sin[:, sl]).astype(BF)
        out[128:192, sl] = dv[sl, :].T.astype(BF)


def far_kernel(
    ids, own, oth, do_own, do_oth, o_full, lse, cos, sin, d_away, pq, pk, pv,
    qkv, kk, vv, qq, doT, dd, dq, dk, dv, *work,
):
    h = ids[0]
    load_halves(ids, own, oth, qkv)
    load_halves(ids, do_own, do_oth, doT)
    turned(qkv, doT, qq, kk, vv, dd, S)
    dq[...] = jnp.zeros_like(dq)
    dk[...] = jnp.zeros_like(dk)
    dv[...] = jnp.zeros_like(dv)
    back = Back(
        qkv.at[0:64], doT, kk, vv, qkv.at[64:128], qq, dd, lse, o_full, dk, dv, work
    )

    def q_block(qi, unused):
        @pl.when(jnp.logical_or(h == 1, qi >= 2))
        def _():
            pairs = jnp.where(h == 0, qi, jnp.minimum(qi, 2))
            back.block(qi, pairs, jnp.logical_or(h == 0, qi < 2), dq)

        return unused

    lax.fori_loop(0, S // BQ, q_block, 0)
    half = S // 2
    there = pl.ds(pl.multiple_of((1 - h) * half, half), half)
    here = pl.ds(pl.multiple_of(h * half, half), half)
    finish(dq.at[:, there], dk.at[there], dv.at[there], cos, sin, d_away)
    pq[...] = dq[:, here]
    pk[...] = dk[here, :]
    pv[...] = dv[here, :]


def attend_back_far(ids, own, oth, do_own, do_oth, o_full, lse, cos, sin, tie):
    half = S // 2
    return pl.pallas_call(
        lambda *refs: far_kernel(*refs[:9], *refs[10:]),
        out_shape=(
            jax.ShapeDtypeStruct((192, half), BF),
            jax.ShapeDtypeStruct((64, half), F32),
            jax.ShapeDtypeStruct((half, 64), F32),
            jax.ShapeDtypeStruct((half, 64), F32),
        ),
        in_specs=[SM] + [VM] * 8 + [pl.BlockSpec(memory_space=pl.ANY)],
        out_specs=(VM,) * 4,
        scratch_shapes=[
            pltpu.VMEM((192, S), BF),
            pltpu.VMEM((S, 64), BF),
            pltpu.VMEM((S, 64), BF),
            pltpu.VMEM((S, 64), BF),
            pltpu.VMEM((64, S), BF),
            pltpu.VMEM((S, 64), BF),
            pltpu.VMEM((64, S), F32),
            pltpu.VMEM((S, 64), F32),
            pltpu.VMEM((S, 64), F32),
        ]
        + work_shapes(),
        compiler_params=pltpu.CompilerParams(vmem_limit_bytes=VMEM),
        cost_estimate=pl.CostEstimate(
            flops=1 << 20, bytes_accessed=1 << 20, transcendentals=0
        ),
        name="attend_back_far",
    )(ids, own, oth, do_own, do_oth, o_full, lse, cos, sin, tie)


def near_kernel(
    ids, own, do_own, o_full, lse, cos, sin, pq, pk, pv, d_own,
    qkv, kk, vv, qq, dd, dq, dk, dv, *work,
):
    half = S // 2
    here = pl.ds(pl.multiple_of(ids[0] * half, half), half)
    qkv[...] = own[...]
    turned(qkv, do_own, qq, kk, vv, dd, half)
    dq[...] = pq[...]
    dk[...] = pk[...]
    dv[...] = pv[...]
    back = Back(
        qkv.at[0:64], do_own, kk, vv, qkv.at[64:128], qq, dd,
        lse.at[:, here], o_full.at[:, here], dk, dv, work,
    )

    def q_block(qi, unused):
        back.block(qi, qi, qi >= 0, dq)
        return unused

    lax.fori_loop(0, half // BQ, q_block, 0)
    finish(dq, dk, dv, cos, sin, d_own)


def attend_back_near(ids, own, do_own, o_full, lse, cos, sin, partial, *ties):
    half = S // 2
    n = len(ties)
    return pl.pallas_call(
        lambda *refs: near_kernel(*refs[:10], *refs[10 + n :]),
        out_shape=jax.ShapeDtypeStruct((192, half), BF),
        in_specs=[SM] + [VM] * 9 + [pl.BlockSpec(memory_space=pl.ANY)] * n,
        out_specs=VM,
        scratch_shapes=[
            pltpu.VMEM((192, half), BF),
            pltpu.VMEM((half, 64), BF),
            pltpu.VMEM((half, 64), BF),
            pltpu.VMEM((half, 64), BF),
            pltpu.VMEM((half, 64), BF),
            pltpu.VMEM((64, half), F32),
            pltpu.VMEM((half, 64), F32),
            pltpu.VMEM((half, 64), F32),
        ]
        + work_shapes(),
        compiler_params=pltpu.CompilerParams(vmem_limit_bytes=VMEM),
        cost_estimate=pl.CostEstimate(
            flops=1 << 20, bytes_accessed=1 << 20, transcendentals=0
        ),
        name="attend_back_near",
    )(ids, own, do_own, o_full, lse, cos, sin, *partial, *ties)


ANY = pl.BlockSpec(memory_space=pl.ANY)
DMA = pltpu.SemaphoreType.DMA
NT = ((1,), (1,))
TN = ((0,), (0,))


def call(kernel, name, inputs, specs, outs, scratch, flops=0, moved=0, ties=(), out_specs=None):
    shapes = tuple(jax.ShapeDtypeStruct(shape, kind) for shape, kind in outs)
    n, k = len(inputs), len(ties)

    def body(*refs):
        kernel(*refs[:n], *refs[n + k :])

    return pl.pallas_call(
        body,
        out_shape=shapes,
        in_specs=list(specs) + [ANY] * k,
        out_specs=out_specs or (VM,) * len(outs),
        scratch_shapes=scratch,
        compiler_params=pltpu.CompilerParams(vmem_limit_bytes=VMEM),
        cost_estimate=pl.CostEstimate(flops=flops, bytes_accessed=moved, transcendentals=0),
        name=name,
    )(*inputs, *ties)


def hold(v, *ties):
    return pl.pallas_call(
        lambda *refs: None,
        out_shape=jax.ShapeDtypeStruct(v.shape, v.dtype),
        in_specs=[ANY] * (1 + len(ties)),
        out_specs=ANY,
        input_output_aliases={0: 0},
        name="hold",
    )(v, *ties)


def start_rows_in(src, dst, sems):
    for i in range(8):
        at = pl.ds(i * 256, 256)
        pltpu.make_async_copy(src.at[at], dst.at[at], sems.at[i]).start()


def start_block(src, n, to, sems):
    at = pl.ds(pl.multiple_of(n * 512, 512), 512)
    pltpu.make_async_copy(src.at[at], to.at[at], sems.at[n]).start()


def wait_blocks(src, to, sems):
    for n in range(4):
        at = pl.ds(n * 512, 512)
        pltpu.make_async_copy(src.at[at], to.at[at], sems.at[n]).wait()


def wait_piece(dst, sems, i):
    rows = dst.at[pl.ds(pl.multiple_of(i * 256, 256), 256)]
    pltpu.make_async_copy(rows, rows, sems.at[i]).wait()


def pack_kernel(w, vec, w2, wd, msg, rows):
    v = jnp.concatenate([vec[...], jnp.zeros((5, 64), F32)], 0).astype(BF)
    for d in range(16):
        hd, zcd = d // 8, d % 8
        for part in range(2):
            block = (hd if part == 0 else 1 - hd) * 8 + zcd
            for t in range(3):
                col = t * 1024 + block * 64
                at = part * 192 + t * 64
                msg[d, 0:64, at : at + 64] = w[:, col : col + 64].astype(BF)
        msg[d, 64:80, :] = jnp.zeros((16, 384), BF)
        msg[d, 64:80, 0:64] = v
    rows[0:256, :] = w2[...].astype(BF)
    rows[256:320, :] = wd[...].astype(BF)


def pack(w, vec, w2, wd):
    outs = [((16, 80, 384), BF), ((320, 1024), BF)]
    return call(pack_kernel, "pack", (w, vec, w2, wd), [VM] * 4, outs, [], 0, 4 << 20)


def pack_up_kernel(w1, msg):
    for d in range(16):
        hd, zcd = d // 8, d % 8
        for part in range(2):
            block = (hd if part == 0 else 1 - hd) * 8 + zcd
            msg[d, :, part * 256 : part * 256 + 256] = w1[:, block * 256 : block * 256 + 256].astype(BF)


def pack_up(w1, *ties):
    return call(pack_up_kernel, "pack_up", (w1,), [VM], [((16, 64, 512), BF)], [], 0, 4 << 20, ties)[0]


def copy_kernel(src, dst):
    dst[...] = src[...]


def after(v, *ties):
    return call(copy_kernel, "after", (v,), [VM], [(v.shape, v.dtype)], [], 0, 1 << 20, ties)[0]


def normalize(values):
    middle = jnp.mean(values, -1, keepdims=True)
    centered = values - middle
    spread = jnp.mean(centered * centered, -1, keepdims=True)
    inverse = lax.rsqrt(spread + 1e-05)
    return (centered * inverse, inverse)


def rotate(cos, sin, mixed):
    out = []
    for n in (0, 64):
        a, b = mixed[n : n + 16], mixed[n + 16 : n + 32]
        out += [a * cos - b * sin, b * cos + a * sin, mixed[n + 32 : n + 64]]
    return jnp.concatenate(out + [mixed[128:]], 0).astype(BF)


def project_kernel(ids, msg, cos, sin, x_ref, hidden, here, away, vec, b1, w_qkv, raw, xs, sems):
    h, zc = ids[0], 2 * ids[1] + ids[2]
    start_rows_in(x_ref, xs, sems)
    for s in range(16):
        w_qkv[s * 64 : (s + 1) * 64, :] = msg[s, 0:64, 0:384]
        v = msg[s, 64:80, 0:64].astype(F32)
        raw[s] = v
        vec[:, s * 64 : (s + 1) * 64] = v
    own, oth = h * 8 + zc, (1 - h) * 8 + zc
    v_own, v_oth = raw[own], raw[oth]
    bias = jnp.concatenate(
        [v_own[t : t + 1, :] for t in range(3)] + [v_oth[t : t + 1, :] for t in range(3)], 1
    )
    for n, i in enumerate((own, oth)):
        for j in range(4):
            at = n * 256 + j * 64
            b1[:, at : at + 64] = raw[4 * lax.rem(i, 4) + j, pl.ds(4 + i // 4, 1), :]
    gain, shift = vec[9:10, :], vec[10:11, :]

    def pair(n, unused):
        for i in range(2):
            wait_piece(xs, sems, 2 * n + i)
        at = pl.ds(pl.multiple_of(n * 512, 512), 512)
        normed, unused_inverse = normalize(xs[at, :].astype(F32))
        hid = (normed * gain + shift).astype(BF)
        hidden[at, :] = hid
        mixed = (dot(hid, w_qkv[...]) + bias).T
        here[:, at] = rotate(cos[:, at], sin[:, at], mixed[:192])
        away[:, at] = rotate(cos[:, at], sin[:, at], mixed[192:])
        return unused

    lax.fori_loop(0, 4, pair, 0)


def project(ids, msg, cos, sin, x_all, *ties):
    outs = [
        ((2048, 1024), BF),
        ((192, 2048), BF),
        ((192, 2048), BF),
        ((16, 1024), F32),
        ((1, 512), F32),
        ((1024, 384), BF),
    ]
    scratch = [pltpu.VMEM((16, 16, 64), F32), pltpu.VMEM((2048, 1024), BF), DMA((8,))]
    inputs = (ids, msg, cos, sin, x_all)
    return call(
        project_kernel, "project", inputs, [SM, VM, VM, VM, ANY], outs, scratch,
        4 * 2048 * 1024 * 384, 12 << 20, ties,
    )


ROOT = 0.7978845608028654


def units_kernel(hid_ref, w1, b1, act_ref, slope_ref, hs, act, slope, sems, asems, ssems):
    start_rows_in(hid_ref, hs, sems)

    def block(n, unused):
        for i in range(2):
            wait_piece(hs, sems, 2 * n + i)
        at = pl.ds(pl.multiple_of(n * 512, 512), 512)
        u = dot(hs[at, :], w1[...]) + b1[...]
        square = u * u
        th = jnp.tanh(ROOT * u * (1.0 + 0.044715 * square))
        half = 0.5 * (1.0 + th)
        act[at, :] = (u * half).astype(BF)
        back = half + 0.5 * u * (1.0 - th * th) * (ROOT * (1.0 + 3.0 * 0.044715 * square))
        slope[at, :] = back.astype(BF)
        start_block(act, n, act_ref, asems)
        start_block(slope, n, slope_ref, ssems)
        return unused

    lax.fori_loop(0, 4, block, 0)
    wait_blocks(act, act_ref, asems)
    wait_blocks(slope, slope_ref, ssems)


def units(hidden, w1, b1, *ties):
    outs = [((2048, 512), BF), ((2048, 512), BF)]
    scratch = [pltpu.VMEM((2048, 1024), BF)] + [pltpu.VMEM((2048, 512), BF)] * 2
    scratch += [DMA((8,)), DMA((4,)), DMA((4,))]
    return call(
        units_kernel, "units", (hidden, w1, b1), [ANY, VM, VM], outs, scratch,
        2 * 2048 * 1024 * 512, 11 << 20, ties, (ANY, ANY),
    )


def along_rows(w, grad, bias):
    first = jnp.sum(w * grad, 1, keepdims=True)
    second = jnp.sum(w * bias, 1, keepdims=True)
    lane = lax.broadcasted_iota(jnp.int32, (1024, 128), 1)
    return jnp.where(lane == 0, first, second).T[0:2, :]


def units_back_kernel(ids, hid_ref, act_ref, slope_ref, rows, rows_x, w1, g_ref, *refs):
    part_out, part_in, msg, gb1, along, do_here, do_away = refs[:7]
    hs, gs, act, ss, out, back, w2, wd, acc1, acc2, sems, hsems, asems, ssems, osems, bsems = refs[7:]
    h = ids[0]
    start_rows_in(g_ref, gs, sems)
    start_rows_in(act_ref, act, asems)
    start_rows_in(slope_ref, ss, ssems)
    start_rows_in(hid_ref, hs, hsems)
    w2[0:256, :] = rows[0:256, :]
    w2[256:512, :] = rows_x[0:256, :]
    wd[0:64, :] = rows[256:320, :]
    wd[64:128, :] = rows_x[256:320, :]
    acc1[...] = jnp.zeros_like(acc1)
    acc2[...] = jnp.zeros_like(acc2)
    gb1[...] = jnp.zeros_like(gb1)

    def block(n, unused):
        for i in range(2):
            wait_piece(gs, sems, 2 * n + i)
            wait_piece(act, asems, 2 * n + i)
            wait_piece(ss, ssems, 2 * n + i)
            wait_piece(hs, hsems, 2 * n + i)
        at = pl.ds(pl.multiple_of(n * 512, 512), 512)
        hid, g = hs[at, :], gs[at, :]
        back_b = (dot(g, w2[...], NT) * ss[at, :].astype(F32)).astype(BF)
        back[at, :] = dot(back_b, w1[...], NT).astype(BF)
        start_block(back, n, part_in, bsems)
        out[at, :] = dot(act[at, :], w2[...]).astype(BF)
        start_block(out, n, part_out, osems)
        gb1[...] += jnp.sum(back_b.astype(F32), 0, keepdims=True)
        both = dot(g, wd[...], NT).T.astype(BF)
        do_here[:, at] = both[:64]
        do_away[:, at] = both[64:]
        acc2[...] += dot(act[at, :], g, TN)
        acc1[...] += dot(hid, back_b, TN)
        return unused

    lax.fori_loop(0, 4, block, 0)
    along[...] = along_rows(w1[...].astype(F32), acc1[...], gb1[...])
    for p in range(8):
        for hd in range(2):
            rows_at = slice(hd * 512 + p * 64, hd * 512 + p * 64 + 64)
            for part in range(2):
                hh = h if part == 0 else 1 - h
                msg[2 * p + hd, pl.ds(pl.multiple_of(hh * 64, 64), 64), :] = acc1[
                    rows_at, part * 256 : part * 256 + 256
                ].astype(BF)
        for part in range(2):
            hh = h if part == 0 else 1 - h
            for q in range(4):
                msg[2 * p + hh, 128 + q * 32 : 160 + q * 32, :] = acc2[
                    part * 256 + p * 32 : part * 256 + p * 32 + 32, q * 256 : q * 256 + 256
                ].astype(BF)
    wait_blocks(back, part_in, bsems)
    wait_blocks(out, part_out, osems)


def units_back(ids, hidden, act, slope, rows, rows_x, w1, g_all, *ties):
    outs = [((2048, 1024), BF)] * 2 + [((16, 256, 256), BF), ((1, 512), F32), ((2, 1024), F32)]
    outs += [((64, 2048), BF)] * 2
    scratch = [
        pltpu.VMEM((2048, 1024), BF),
        pltpu.VMEM((2048, 1024), BF),
        pltpu.VMEM((2048, 512), BF),
        pltpu.VMEM((2048, 512), BF),
        pltpu.VMEM((2048, 1024), BF),
        pltpu.VMEM((2048, 1024), BF),
        pltpu.VMEM((512, 1024), BF),
        pltpu.VMEM((128, 1024), BF),
        pltpu.VMEM((1024, 512), F32),
        pltpu.VMEM((512, 1024), F32),
        DMA((8,)),
        DMA((8,)),
        DMA((8,)),
        DMA((8,)),
        DMA((4,)),
        DMA((4,)),
    ]
    return call(
        units_back_kernel, "units_back", (ids, hidden, act, slope, rows, rows_x, w1, g_all),
        [SM, ANY, ANY, ANY, VM, VM, VM, ANY], outs, scratch, 10 * 2048 * 1024 * 512, 18 << 20, ties,
        (ANY, ANY) + (VM,) * 5,
    )


def start_rows_out(src, n, to, sems):
    at = pl.ds(n * 512, 512)
    copy = pltpu.make_async_copy(src.at[at], to.at[at], sems.at[n])
    copy.start()
    return copy


def out_kernel(ids, part_ref, rows, rows_x, o_here, o_came, g_ref, total, gd, gs, both, part, out, sems, psems, osems):
    h = ids[0]
    start_rows_in(part_ref, part, psems)
    start_rows_in(g_ref, gs, sems)
    both[0:64, :] = o_here[...]
    both[64:128, :] = o_came[...]
    wd = jnp.concatenate([rows[256:320, :], rows_x[256:320, :]], 0)
    copies = []
    for n in range(4):
        at = slice(n * 512, n * 512 + 512)
        more = dot(both[:, at], wd, TN)
        wait_piece(part, psems, 2 * n)
        wait_piece(part, psems, 2 * n + 1)
        out[at, :] = (part[at, :].astype(F32) + more).astype(BF)
        copies.append(start_rows_out(out, n, total, osems))
    for i in range(8):
        wait_piece(gs, sems, i)
    grad = dot(both[...], gs[...]).astype(BF)
    gd[h] = grad[:64]
    gd[1 - h] = grad[64:]
    for copy in copies:
        copy.wait()


def out_part(ids, part, rows, rows_x, o_here, o_came, g_all, *ties):
    outs = [((2048, 1024), BF), ((2, 64, 1024), BF)]
    scratch = [
        pltpu.VMEM((2048, 1024), BF),
        pltpu.VMEM((128, 2048), BF),
        pltpu.VMEM((2048, 1024), BF),
        pltpu.VMEM((2048, 1024), BF),
        DMA((8,)),
        DMA((8,)),
        DMA((4,)),
    ]
    return call(
        out_kernel, "out_part", (ids, part, rows, rows_x, o_here, o_came, g_all),
        [SM, ANY] + [VM] * 4 + [ANY], outs, scratch, 4 * 2048 * 1024 * 128, 12 << 20, ties,
        (ANY, VM),
    )


def last_kernel(
    ids, d_here, d_came, w_qkv, part_ref, hid_ref, g_own, gb1, gd, along, vin, total, msg,
    hs, part, out, both, gq, vec, sems, psems, osems,
):
    h, zc = ids[0], 2 * ids[1] + ids[2]
    start_rows_in(part_ref, part, psems)
    start_rows_in(hid_ref, hs, sems)
    both[0:192, :] = d_here[...]
    both[192:384, :] = d_came[...]
    copies = []
    for n in range(4):
        at = slice(n * 512, n * 512 + 512)
        more = dot(both[:, at].T, w_qkv[...], NT)
        wait_piece(part, psems, 2 * n)
        wait_piece(part, psems, 2 * n + 1)
        out[at, :] = (part[at, :].astype(F32) + more).astype(BF)
        copies.append(start_rows_out(out, n, total, osems))
    ones = jnp.ones((8, 2048), BF)
    bias = dot(ones, both[...], NT)[0:1]
    for i in range(8):
        wait_piece(hs, sems, i)
    grad = dot(both[...], hs[...])
    turned = grad.T
    sums = along[...] + along_rows(w_qkv[...].astype(F32), turned, bias)
    gq[pl.ds(pl.multiple_of(h * 192, 64), 192), :] = grad[:192]
    gq[pl.ds(pl.multiple_of((1 - h) * 192, 64), 192), :] = grad[192:]
    own, oth = h * 8 + zc, (1 - h) * 8 + zc
    lane = lax.broadcasted_iota(jnp.int32, (1, 1024), 1)
    out_sum = jnp.sum(g_own[...].astype(F32), 0, keepdims=True)
    rows = []
    for t in range(3):
        a = jnp.concatenate([bias[:, t * 64 : t * 64 + 64]] * 16, 1)
        b = jnp.concatenate([bias[:, 192 + t * 64 : 256 + t * 64]] * 16, 1)
        rows.append(jnp.where(lane // 64 == own, a, 0.0) + jnp.where(lane // 64 == oth, b, 0.0))
    rows.append(out_sum)
    a = jnp.concatenate([gb1[:, 0:256]] * 4, 1)
    b = jnp.concatenate([gb1[:, 256:512]] * 4, 1)
    for r in range(4):
        block = lane // 256 + 4 * r
        rows.append(jnp.where(block == own, a, 0.0) + jnp.where(block == oth, b, 0.0))
    shift_sum = sums[1:2, :]
    gain_sum = (sums[0:1, :] - vin[10:11, :] * shift_sum) / vin[9:10, :]
    rows += [out_sum, gain_sum, shift_sum]
    for r, row in enumerate(rows):
        vec[r : r + 1, :] = row
    flat = gq[...].T
    zeros = jnp.zeros((8, 64), F32)
    for p in range(8):
        for hd in range(2):
            at = hd * 512 + p * 64
            msg[2 * p + hd, 0:64, :] = flat[at : at + 64, :].astype(BF)
            cols = slice((hd * 8 + p) * 64, (hd * 8 + p) * 64 + 64)
            v0 = vec[0:8, cols]
            v1 = vec[8:16, cols]
            vrows = jnp.concatenate([v0, zeros, v1, zeros, zeros, zeros], 1)
            d = gd[hd, p * 8 : p * 8 + 8, :].astype(F32)
            d2 = jnp.concatenate([d[:, 768:1024], jnp.zeros((8, 128), F32)], 1)
            tail = jnp.concatenate([vrows, d[:, 0:384], d[:, 384:768], d2], 0)
            msg[2 * p + hd, 64:96, :] = tail.astype(BF)
    for copy in copies:
        copy.wait()


def last_part(ids, d_here, d_came, w_qkv, part, hidden, g_own, gb1, gd, along, vec, *ties):
    scratch = [
        pltpu.VMEM((2048, 1024), BF),
        pltpu.VMEM((2048, 1024), BF),
        pltpu.VMEM((2048, 1024), BF),
        pltpu.VMEM((384, 2048), BF),
        pltpu.VMEM((384, 1024), F32),
        pltpu.VMEM((16, 1024), F32),
        DMA((8,)),
        DMA((8,)),
        DMA((4,)),
    ]
    return call(
        last_kernel, "last_part",
        (ids, d_here, d_came, w_qkv, part, hidden, g_own, gb1, gd, along, vec),
        [SM] + [VM] * 3 + [ANY] * 2 + [VM] * 5, [((2048, 1024), BF), ((16, 96, 384), BF)], scratch,
        4 * 2048 * 1024 * 384, 16 << 20, ties, (ANY, VM),
    )


SWAP = [(0, 1), (1, 0)]
GROUP = ("z", "core")
MODEL = ("xhi", "z", "core")
BATCH = ("xlo", "y")
SUM = ("xlo", "y", "xhi")


def swap_core(v):
    return lax.ppermute(v, "core", SWAP)


def swap_x(v):
    return lax.ppermute(v, "xhi", SWAP)


def group_sum(v):
    return lax.psum_scatter(v, GROUP, scatter_dimension=0, tiled=True)


def sum_kernel(n, parts, lo, hi, ps, sems):
    for i in range(8):
        at = pl.ds(2 * i, 2)
        pltpu.make_async_copy(parts.at[at], ps.at[at], sems.at[i]).start()
    total = None
    for i in range(8):
        at = pl.ds(2 * i, 2)
        pltpu.make_async_copy(ps.at[at], ps.at[at], sems.at[i]).wait()
        pair = ps[2 * i].astype(F32) + ps[2 * i + 1].astype(F32)
        total = pair if total is None else total + pair
    lo[...] = total[:n].astype(BF)
    hi[...] = total[n:].astype(BF)


def sum_parts(parts, n, *ties):
    rows, columns = parts.shape[1:]
    outs = [((n, columns), BF), ((rows - n, columns), BF)]
    scratch = [pltpu.VMEM(parts.shape, BF), DMA((8,))]
    return call(functools.partial(sum_kernel, n), "sum_parts", (parts,), [ANY], outs, scratch, 0, 2 << 20, ties)


def fan_kernel(lo, hi, out):
    n = lo.shape[0]
    for p in range(8):
        out[p, 0:n, :] = lo[...]
        out[p, n:, :] = hi[...]


def fan(lo, hi, *ties):
    shape = (8, lo.shape[0] + hi.shape[0], lo.shape[1])
    return call(fan_kernel, "fan", (lo, hi), [VM] * 2, [(shape, BF)], [], 0, 2 << 20, ties)[0]


def turn(v):
    return lax.ppermute(v, ("xlo", "y", "z", "core"), [(p * 8 + m, m * 8 + p) for p in range(8) for m in range(8)])


def tables(positions):
    freqs = 10000.0 ** (-(jnp.arange(ROT // 2, dtype=F32) * 2.0) / ROT)
    angles = positions.astype(F32)[None, :] * freqs[:, None]
    return (jnp.cos(angles), jnp.sin(angles))


def adamw(master, grad, first, second, rate):
    first_new = 0.9 * first + 0.1 * grad
    second_new = 0.95 * second + 0.05 * grad * grad
    first_hat = first_new / (1.0 - 0.9**STEP)
    second_hat = second_new / (1.0 - 0.95**STEP)
    fresh = master - rate * (first_hat / (jnp.sqrt(second_hat) + 1e-08) + 0.1 * master)
    return (fresh, first_new, second_new)


RATE = 2.0 * D ** (-0.5)
RATE_DOWN = 2.0 * FF ** (-0.5)


def update_units_kernel(early, w1, m1, v1, w2, m2, v2, w1n, m1n, v1n, w2n, m2n, v2n):
    for p in range(8):
        for hh in range(2):
            at = slice((hh * 8 + p) * 256, (hh * 8 + p) * 256 + 256)
            grad = early[p, hh * 64 : hh * 64 + 64, :].astype(F32)
            w1n[:, at], m1n[:, at], v1n[:, at] = adamw(w1[:, at], grad, m1[:, at], v1[:, at], RATE)
        for q in range(4):
            at = (slice(p * 32, p * 32 + 32), slice(q * 256, q * 256 + 256))
            grad = early[p, 128 + q * 32 : 160 + q * 32, :].astype(F32)
            w2n[at], m2n[at], v2n[at] = adamw(w2[at], grad, m2[at], v2[at], RATE_DOWN)


def update_units(early, *state, ties=()):
    outs = [((64, 4096), F32)] * 3 + [((256, 1024), F32)] * 3
    return call(update_units_kernel, "update_units", (early,) + state, [VM] * 7, outs, [], 0, 13 << 20, ties)


def update_heads_kernel(late, w, m, v, wd, md, vd, vec, mv, vv, wn, mn, vn, wdn, mdn, vdn, vecn, mvn, vvn, gq, gd):
    for zc in range(8):
        for hh in range(2):
            for t in range(3):
                col = t * 1024 + (hh * 8 + zc) * 64
                at = hh * 192 + t * 64
                gq[:, col : col + 64] = late[zc, 0:64, at : at + 64].astype(F32)
        rows = late[zc, 64:96, :].astype(F32)
        gd[zc * 8 : zc * 8 + 8, 0:384] = rows[8:16]
        gd[zc * 8 : zc * 8 + 8, 384:768] = rows[16:24]
        gd[zc * 8 : zc * 8 + 8, 768:1024] = rows[24:32, 0:256]
        total = rows[0:8] if zc == 0 else total + rows[0:8]
    grad = jnp.concatenate([total[:, 0:64], total[0:3, 128:192]], 0)
    wn[...], mn[...], vn[...] = adamw(w[...], gq[...], m[...], v[...], RATE)
    wdn[...], mdn[...], vdn[...] = adamw(wd[...], gd[...], md[...], vd[...], RATE)
    vecn[...], mvn[...], vvn[...] = adamw(vec[...], grad, mv[...], vv[...], 0.3)


def update_heads(late, *state):
    outs = [((64, 3072), F32)] * 3 + [((64, 1024), F32)] * 3 + [((11, 64), F32)] * 3
    scratch = [pltpu.VMEM((64, 3072), F32), pltpu.VMEM((64, 1024), F32)]
    return call(update_heads_kernel, "update_heads", (late,) + state, [VM] * 10, outs, scratch, 0, 7 << 20)


def input_kernel(came, x, g, vec, out):
    total = came[...].astype(F32)
    normed, inverse = normalize(x[...].astype(F32))
    back = total * vec[9:10, :]
    mean = jnp.mean(back, -1, keepdims=True)
    along = jnp.mean(back * normed, -1, keepdims=True)
    out[...] = (g[...].astype(F32) + inverse * (back - mean - normed * along)).astype(BF)


def input_part(blocks, x, g, vec, *ties):
    inputs = (blocks, x, g, vec)
    return call(input_kernel, "input_part", inputs, [VM] * 4, [((256, 1024), BF)], [], 0, 4 << 20, ties)[0]


def output_kernel(came, x, vec, out):
    total = came[...].astype(F32)
    out[...] = (x[...].astype(F32) + total + (vec[3:4, :] + vec[8:9, :])).astype(BF)


def output_part(blocks, x, vec, *ties):
    inputs = (blocks, x, vec)
    return call(output_kernel, "output_part", inputs, [VM] * 3, [((256, 1024), BF)], [], 0, 4 << 20, ties)[0]


def local(
    tokens,
    cotangent,
    qkv_weight,
    dense_weight,
    fc1_weight,
    fc2_weight,
    vectors,
    qkv_first,
    dense_first,
    fc1_first,
    fc2_first,
    vectors_first,
    qkv_second,
    dense_second,
    fc1_second,
    fc2_second,
    vectors_second,
):
    h, z, c = lax.axis_index("xhi"), lax.axis_index("z"), lax.axis_index("core")
    ids = jnp.stack([h, z, c, lax.axis_index(BATCH)]).astype(jnp.int32)
    x_own = tokens[0]
    g_own = cotangent[0]

    cos_all, sin_all = tables(jnp.arange(S, dtype=jnp.int32))
    cos_here = lax.dynamic_slice_in_dim(cos_all, h * (S // 2), S // 2, 1)
    sin_here = lax.dynamic_slice_in_dim(sin_all, h * (S // 2), S // 2, 1)
    cos_away = lax.dynamic_slice_in_dim(cos_all, (1 - h) * (S // 2), S // 2, 1)
    sin_away = lax.dynamic_slice_in_dim(sin_all, (1 - h) * (S // 2), S // 2, 1)

    x_all = lax.all_gather(x_own, GROUP, axis=0, tiled=True)
    msg, rows = pack(qkv_weight, vectors, fc2_weight, dense_weight)
    msg = lax.all_to_all(msg, MODEL, 0, 0, tiled=True)
    rows_x = swap_x(rows)
    up_msg = pack_up(fc1_weight, cos_here, sin_here, cos_away, sin_away, ids)
    w1 = lax.all_to_all(hold(up_msg, x_all), MODEL, 0, 0, tiled=True).reshape(1024, 512)
    g_all = lax.all_gather(hold(g_own, x_all, msg, rows_x, up_msg), GROUP, axis=0, tiled=True)
    hidden, here, away, vec, b1, w_qkv = project(
        ids, msg, cos_here, sin_here, x_all
    )
    came = swap_x(away)
    act, slope = units(hidden, w1, b1, away)
    o_full, lse, o_here, o_away = attend(ids, here, came, act)
    o_came = swap_x(o_away)
    part_out, part_in, early, gb1, along, do_here, do_away = units_back(
        ids, hidden, act, slope, rows, rows_x, w1, g_all, o_away
    )
    do_came = swap_x(do_away)
    total, gd = out_part(
        ids, part_out, rows, rows_x, o_here, o_came, g_all
    )
    out_sum = group_sum(hold(total, do_came))
    early = lax.all_to_all(hold(early, do_came, gd), SUM, 0, 0, tiled=True)
    d_away, *partial = attend_back_far(
        ids, here, came, do_here, do_came, o_full, lse, cos_away, sin_away, gd
    )
    d_came = swap_x(d_away)
    d_here = attend_back_near(
        ids, here, do_here, o_full, lse, cos_here, sin_here, partial, d_away
    )
    total, late = last_part(
        ids, d_here, d_came, w_qkv, part_in, hidden, g_own, gb1, gd, along, vec, early
    )
    hidden_sum = group_sum(total)
    early_turn, early_stay = sum_parts(early, 128, late)
    early_turn = turn(early_turn)
    early = fan(early_turn, early_stay)
    late = lax.all_to_all(late, SUM, 0, 0, tiled=True)
    early = lax.all_to_all(hold(early, late), BATCH, 0, 0, tiled=True)
    late_turn, late_stay = sum_parts(late, 72, early_stay)
    late = fan(turn(late_turn), late_stay)
    late = lax.all_to_all(hold(late, early), BATCH, 0, 0, tiled=True)
    new1 = update_units(
        early,
        *(fc1_weight, fc1_first, fc1_second, fc2_weight, fc2_first, fc2_second),
    )
    output = output_part(out_sum, x_own, vec, new1[0])
    input_grad = input_part(hidden_sum, x_own, g_own, vec, output)
    new2 = update_heads(
        hold(late, input_grad),
        *(qkv_weight, qkv_first, qkv_second),
        *(dense_weight, dense_first, dense_second),
        *(vectors, vectors_first, vectors_second),
    )
    news = [(new2[j], new2[3 + j], new1[j], new1[3 + j], new2[6 + j]) for j in range(3)]
    return (output[None], input_grad[None]) + news[0] + news[1] + news[2]


def solution(mesh):
    fine = Mesh(mesh.devices.reshape(2, 4, 2, 4, 2), ("xlo", "y", "xhi", "z", "core"))
    dp, fsdp = ("xlo", "y"), ("xhi", "z", "core")
    token = P(dp, fsdp, None)
    row = P(fsdp, None)
    column = P(None, fsdp)
    params = (row, row, row, row, column)
    return jax.shard_map(
        local,
        mesh=fine,
        in_specs=(token, token) + params * 3,
        out_specs=(token, token) + params * 3,
        check_vma=False,
    )
```

```python
import functools

import jax
import jax.numpy as jnp
from jax import lax
from jax.experimental import pallas as pl
from jax.experimental.pallas import tpu as pltpu
from jax.sharding import Mesh
from jax.sharding import PartitionSpec as P

D = 1024
HEAD = 64
ROT = 32
FF = 4096
STEP = 10
S = 4096
NEG = -1e30
F32 = jnp.float32
BF = jnp.bfloat16


def dot(a, b, dims=((1,), (0,))):
    return lax.dot_general(a, b, (dims, ((), ())), preferred_element_type=F32)


def load_halves(ids, own, oth, dst):
    @pl.when(ids[0] == 0)
    def _():
        dst[:, 0 : S // 2] = own[...]
        dst[:, S // 2 : S] = oth[...]

    @pl.when(ids[0] == 1)
    def _():
        dst[:, 0 : S // 2] = oth[...]
        dst[:, S // 2 : S] = own[...]


def store_halves(ids, src, own, away):
    @pl.when(ids[0] == 0)
    def _():
        own[...] = src[:, 0 : S // 2].astype(own.dtype)
        away[...] = src[:, S // 2 : S].astype(own.dtype)

    @pl.when(ids[0] == 1)
    def _():
        away[...] = src[:, 0 : S // 2].astype(own.dtype)
        own[...] = src[:, S // 2 : S].astype(own.dtype)


VMEM = 60 << 20
VM = pl.BlockSpec(memory_space=pltpu.VMEM)
SM = pl.BlockSpec(memory_space=pltpu.SMEM)
BQ = 1024
BK = 512


def causal(s, shift):
    kp = shift + lax.broadcasted_iota(jnp.int32, s.shape, 0)
    qp = lax.broadcasted_iota(jnp.int32, s.shape, 1)
    return jnp.where(kp <= qp, s, NEG)


def attend_kernel(ids, own, oth, o_full, lse, o_own, o_away, qkv, kk, qs, s0, s1, acc, top, total):
    load_halves(ids, own, oth, qkv)
    for j in range(8):
        sl = slice(j * 512, (j + 1) * 512)
        kk[sl, :] = qkv[64:128, sl].T

    def q_block(qi, unused):
        at = pl.ds(pl.multiple_of(qi * BQ, BQ), BQ)
        qs[...] = qkv[0:64, at] * jnp.asarray(0.125, BF)
        top[...] = jnp.full_like(top, NEG)
        total[...] = jnp.zeros_like(total)
        acc[...] = jnp.zeros_like(acc)

        def scores(j, cols):
            return dot(kk[pl.ds(pl.multiple_of(j * BK, BK), BK), :], qs[:, cols])

        def fold(s, j, cols):
            m = top[:, cols]
            m2 = jnp.maximum(m, jnp.max(s, 0, keepdims=True))
            p = jnp.exp(s - m2)
            a = jnp.exp(m - m2)
            top[:, cols] = m2
            total[:, cols] = total[:, cols] * a + jnp.sum(p, 0, keepdims=True)
            v = qkv[128:192, pl.ds(pl.multiple_of(j * BK, BK), BK)]
            acc[:, cols] = acc[:, cols] * a + dot(v, p.astype(BF))

        every, later = slice(0, BQ), slice(BK, BQ)
        s0[...] = scores(0, every)

        def pair(jj, unused):
            s1[...] = scores(2 * jj + 1, every)
            fold(s0[...], 2 * jj, every)
            s0[...] = scores(2 * jj + 2, every)
            fold(s1[...], 2 * jj + 1, every)
            return unused

        lax.fori_loop(0, qi, pair, 0)
        last = scores(2 * qi + 1, later)
        fold(causal(s0[...], 0), 2 * qi, every)
        fold(causal(last, 0), 2 * qi + 1, later)
        o_full[:, at] = acc[...] / total[...]
        lse[:, at] = top[...] + jnp.log(total[...])
        return unused

    lax.fori_loop(0, S // BQ, q_block, 0)
    store_halves(ids, o_full, o_own, o_away)


def attend(ids, own, oth, tie):
    return pl.pallas_call(
        lambda *refs: attend_kernel(*refs[:3], *refs[4:]),
        out_shape=(
            jax.ShapeDtypeStruct((64, S), F32),
            jax.ShapeDtypeStruct((1, S), F32),
            jax.ShapeDtypeStruct((64, S // 2), BF),
            jax.ShapeDtypeStruct((64, S // 2), BF),
        ),
        in_specs=[SM, VM, VM, pl.BlockSpec(memory_space=pl.ANY)],
        out_specs=(VM,) * 4,
        scratch_shapes=[
            pltpu.VMEM((192, S), BF),
            pltpu.VMEM((S, 64), BF),
            pltpu.VMEM((64, BQ), BF),
            pltpu.VMEM((BK, BQ), F32),
            pltpu.VMEM((BK, BQ), F32),
            pltpu.VMEM((64, BQ), F32),
            pltpu.VMEM((1, BQ), F32),
            pltpu.VMEM((1, BQ), F32),
        ],
        compiler_params=pltpu.CompilerParams(vmem_limit_bytes=VMEM),
        cost_estimate=pl.CostEstimate(
            flops=8 * S * S * 64, bytes_accessed=4 << 20, transcendentals=S * S // 2
        ),
        name="attend",
    )(ids, own, oth, tie)


def unrotate(d, cos, sin):
    a, b = d[0:16], d[16:32]
    return jnp.concatenate([a * cos + b * sin, b * cos - a * sin, d[32:64]], 0)


class Back:
    def __init__(self, q, doT, kk, vv, kT, qq, dd, lse, o, dk, dv, work):
        self.q, self.doT, self.kk, self.vv, self.kT, self.qq, self.dd = q, doT, kk, vv, kT, qq, dd
        self.lse, self.o, self.dk, self.dv = lse, o, dk, dv
        self.s0, self.s1, self.t0, self.t1, self.acc, self.delta = work

    def products(self, qoff, j, half):
        ks = pl.ds(pl.multiple_of(j * BK, BK), BK)
        cols = pl.ds(pl.multiple_of(qoff + half, BK), BQ - half)
        return dot(self.kk[ks, :], self.q[:, cols]), dot(self.vv[ks, :], self.doT[:, cols])

    def fold(self, qoff, s, t, j, half):
        ks = pl.ds(pl.multiple_of(j * BK, BK), BK)
        cols = pl.ds(pl.multiple_of(qoff + half, BK), BQ - half)
        p = jnp.exp(s - self.lse[:, cols])
        ds = (p * (t - self.delta[:, half:])).astype(BF)
        self.dv[ks, :] += dot(p.astype(BF), self.dd[cols, :])
        self.dk[ks, :] += dot(ds, self.qq[cols, :])
        self.acc[:, half:] += dot(self.kT[:, ks], ds)

    def block(self, qi, pairs, diagonal, dq):
        qoff = pl.multiple_of(qi * BQ, BQ)
        at = pl.ds(qoff, BQ)
        self.delta[...] = jnp.sum(self.doT[:, at].astype(F32) * self.o[:, at], 0, keepdims=True)
        self.acc[...] = dq[:, at]
        self.s0[...], self.t0[...] = self.products(qoff, 0, 0)

        def pair(jj, unused):
            self.s1[...], self.t1[...] = self.products(qoff, 2 * jj + 1, 0)
            self.fold(qoff, self.s0[...], self.t0[...], 2 * jj, 0)
            self.s0[...], self.t0[...] = self.products(qoff, 2 * jj + 2, 0)
            self.fold(qoff, self.s1[...], self.t1[...], 2 * jj + 1, 0)
            return unused

        lax.fori_loop(0, pairs, pair, 0)

        @pl.when(diagonal)
        def _():
            s, t = self.products(qoff, 2 * qi + 1, BK)
            self.fold(qoff, causal(self.s0[...], 0), self.t0[...], 2 * qi, 0)
            self.fold(qoff, causal(s, 0), t, 2 * qi + 1, BK)

        dq[:, at] = self.acc[...]


def work_shapes():
    return [pltpu.VMEM((BK, BQ), F32)] * 4 + [pltpu.VMEM((64, BQ), F32), pltpu.VMEM((1, BQ), F32)]


def turned(qkv, doT, qq, kk, vv, dd, n):
    for j in range(n // 512):
        sl = slice(j * 512, (j + 1) * 512)
        qkv[0:64, sl] = qkv[0:64, sl] * jnp.asarray(0.125, BF)
        qq[sl, :] = qkv[0:64, sl].T
        kk[sl, :] = qkv[64:128, sl].T
        vv[sl, :] = qkv[128:192, sl].T
        dd[sl, :] = doT[:, sl].T


def finish(dq, dk, dv, cos, sin, out):
    for j in range(S // 1024):
        sl = slice(j * 512, (j + 1) * 512)
        out[0:64, sl] = unrotate(dq[:, sl] * 0.125, cos[:, sl], sin[:, sl]).astype(BF)
        out[64:128, sl] = unrotate(dk[sl, :].T, cos[:, sl], sin[:, sl]).astype(BF)
        out[128:192, sl] = dv[sl, :].T.astype(BF)


def far_kernel(
    ids, own, oth, do_own, do_oth, o_full, lse, cos, sin, d_away, pq, pk, pv,
    qkv, kk, vv, qq, doT, dd, dq, dk, dv, *work,
):
    h = ids[0]
    load_halves(ids, own, oth, qkv)
    load_halves(ids, do_own, do_oth, doT)
    turned(qkv, doT, qq, kk, vv, dd, S)
    dq[...] = jnp.zeros_like(dq)
    dk[...] = jnp.zeros_like(dk)
    dv[...] = jnp.zeros_like(dv)
    back = Back(
        qkv.at[0:64], doT, kk, vv, qkv.at[64:128], qq, dd, lse, o_full, dk, dv, work
    )

    def q_block(qi, unused):
        @pl.when(jnp.logical_or(h == 1, qi >= 2))
        def _():
            pairs = jnp.where(h == 0, qi, jnp.minimum(qi, 2))
            back.block(qi, pairs, jnp.logical_or(h == 0, qi < 2), dq)

        return unused

    lax.fori_loop(0, S // BQ, q_block, 0)
    half = S // 2
    there = pl.ds(pl.multiple_of((1 - h) * half, half), half)
    here = pl.ds(pl.multiple_of(h * half, half), half)
    finish(dq.at[:, there], dk.at[there], dv.at[there], cos, sin, d_away)
    pq[...] = dq[:, here]
    pk[...] = dk[here, :]
    pv[...] = dv[here, :]


def attend_back_far(ids, own, oth, do_own, do_oth, o_full, lse, cos, sin, tie):
    half = S // 2
    return pl.pallas_call(
        lambda *refs: far_kernel(*refs[:9], *refs[10:]),
        out_shape=(
            jax.ShapeDtypeStruct((192, half), BF),
            jax.ShapeDtypeStruct((64, half), F32),
            jax.ShapeDtypeStruct((half, 64), F32),
            jax.ShapeDtypeStruct((half, 64), F32),
        ),
        in_specs=[SM] + [VM] * 8 + [pl.BlockSpec(memory_space=pl.ANY)],
        out_specs=(VM,) * 4,
        scratch_shapes=[
            pltpu.VMEM((192, S), BF),
            pltpu.VMEM((S, 64), BF),
            pltpu.VMEM((S, 64), BF),
            pltpu.VMEM((S, 64), BF),
            pltpu.VMEM((64, S), BF),
            pltpu.VMEM((S, 64), BF),
            pltpu.VMEM((64, S), F32),
            pltpu.VMEM((S, 64), F32),
            pltpu.VMEM((S, 64), F32),
        ]
        + work_shapes(),
        compiler_params=pltpu.CompilerParams(vmem_limit_bytes=VMEM),
        cost_estimate=pl.CostEstimate(
            flops=1 << 20, bytes_accessed=1 << 20, transcendentals=0
        ),
        name="attend_back_far",
    )(ids, own, oth, do_own, do_oth, o_full, lse, cos, sin, tie)


def near_kernel(
    ids, own, do_own, o_full, lse, cos, sin, pq, pk, pv, d_own,
    qkv, kk, vv, qq, dd, dq, dk, dv, *work,
):
    half = S // 2
    here = pl.ds(pl.multiple_of(ids[0] * half, half), half)
    qkv[...] = own[...]
    turned(qkv, do_own, qq, kk, vv, dd, half)
    dq[...] = pq[...]
    dk[...] = pk[...]
    dv[...] = pv[...]
    back = Back(
        qkv.at[0:64], do_own, kk, vv, qkv.at[64:128], qq, dd,
        lse.at[:, here], o_full.at[:, here], dk, dv, work,
    )

    def q_block(qi, unused):
        back.block(qi, qi, qi >= 0, dq)
        return unused

    lax.fori_loop(0, half // BQ, q_block, 0)
    finish(dq, dk, dv, cos, sin, d_own)


def attend_back_near(ids, own, do_own, o_full, lse, cos, sin, partial, *ties):
    half = S // 2
    n = len(ties)
    return pl.pallas_call(
        lambda *refs: near_kernel(*refs[:10], *refs[10 + n :]),
        out_shape=jax.ShapeDtypeStruct((192, half), BF),
        in_specs=[SM] + [VM] * 9 + [pl.BlockSpec(memory_space=pl.ANY)] * n,
        out_specs=VM,
        scratch_shapes=[
            pltpu.VMEM((192, half), BF),
            pltpu.VMEM((half, 64), BF),
            pltpu.VMEM((half, 64), BF),
            pltpu.VMEM((half, 64), BF),
            pltpu.VMEM((half, 64), BF),
            pltpu.VMEM((64, half), F32),
            pltpu.VMEM((half, 64), F32),
            pltpu.VMEM((half, 64), F32),
        ]
        + work_shapes(),
        compiler_params=pltpu.CompilerParams(vmem_limit_bytes=VMEM),
        cost_estimate=pl.CostEstimate(
            flops=1 << 20, bytes_accessed=1 << 20, transcendentals=0
        ),
        name="attend_back_near",
    )(ids, own, do_own, o_full, lse, cos, sin, *partial, *ties)


ANY = pl.BlockSpec(memory_space=pl.ANY)
DMA = pltpu.SemaphoreType.DMA
NT = ((1,), (1,))
TN = ((0,), (0,))


def call(kernel, name, inputs, specs, outs, scratch, flops=0, moved=0, ties=(), out_specs=None):
    shapes = tuple(jax.ShapeDtypeStruct(shape, kind) for shape, kind in outs)
    n, k = len(inputs), len(ties)

    def body(*refs):
        kernel(*refs[:n], *refs[n + k :])

    return pl.pallas_call(
        body,
        out_shape=shapes,
        in_specs=list(specs) + [ANY] * k,
        out_specs=out_specs or (VM,) * len(outs),
        scratch_shapes=scratch,
        compiler_params=pltpu.CompilerParams(vmem_limit_bytes=VMEM),
        cost_estimate=pl.CostEstimate(flops=flops, bytes_accessed=moved, transcendentals=0),
        name=name,
    )(*inputs, *ties)


def hold(v, *ties):
    return pl.pallas_call(
        lambda *refs: None,
        out_shape=jax.ShapeDtypeStruct(v.shape, v.dtype),
        in_specs=[ANY] * (1 + len(ties)),
        out_specs=ANY,
        input_output_aliases={0: 0},
        name="hold",
    )(v, *ties)


def start_rows_in(src, dst, sems):
    for i in range(8):
        at = pl.ds(i * 256, 256)
        pltpu.make_async_copy(src.at[at], dst.at[at], sems.at[i]).start()


def start_block(src, n, to, sems):
    at = pl.ds(pl.multiple_of(n * 512, 512), 512)
    pltpu.make_async_copy(src.at[at], to.at[at], sems.at[n]).start()


def wait_blocks(src, to, sems):
    for n in range(4):
        at = pl.ds(n * 512, 512)
        pltpu.make_async_copy(src.at[at], to.at[at], sems.at[n]).wait()


def wait_piece(dst, sems, i):
    rows = dst.at[pl.ds(pl.multiple_of(i * 256, 256), 256)]
    pltpu.make_async_copy(rows, rows, sems.at[i]).wait()


def pack_kernel(w, vec, w2, wd, msg, rows):
    v = jnp.concatenate([vec[...], jnp.zeros((5, 64), F32)], 0).astype(BF)
    for d in range(16):
        hd, zcd = d // 8, d % 8
        for part in range(2):
            block = (hd if part == 0 else 1 - hd) * 8 + zcd
            for t in range(3):
                col = t * 1024 + block * 64
                at = part * 192 + t * 64
                msg[d, 0:64, at : at + 64] = w[:, col : col + 64].astype(BF)
        msg[d, 64:80, :] = jnp.zeros((16, 384), BF)
        msg[d, 64:80, 0:64] = v
    rows[0:256, :] = w2[...].astype(BF)
    rows[256:320, :] = wd[...].astype(BF)


def pack(w, vec, w2, wd):
    outs = [((16, 80, 384), BF), ((320, 1024), BF)]
    return call(pack_kernel, "pack", (w, vec, w2, wd), [VM] * 4, outs, [], 0, 4 << 20)


def pack_up_kernel(w1, msg):
    for d in range(16):
        hd, zcd = d // 8, d % 8
        for part in range(2):
            block = (hd if part == 0 else 1 - hd) * 8 + zcd
            msg[d, :, part * 256 : part * 256 + 256] = w1[:, block * 256 : block * 256 + 256].astype(BF)


def pack_up(w1, *ties):
    return call(pack_up_kernel, "pack_up", (w1,), [VM], [((16, 64, 512), BF)], [], 0, 4 << 20, ties)[0]


def copy_kernel(src, dst):
    dst[...] = src[...]


def after(v, *ties):
    return call(copy_kernel, "after", (v,), [VM], [(v.shape, v.dtype)], [], 0, 1 << 20, ties)[0]


def normalize(values):
    middle = jnp.mean(values, -1, keepdims=True)
    centered = values - middle
    spread = jnp.mean(centered * centered, -1, keepdims=True)
    inverse = lax.rsqrt(spread + 1e-05)
    return (centered * inverse, inverse)


def rotate(cos, sin, mixed):
    out = []
    for n in (0, 64):
        a, b = mixed[n : n + 16], mixed[n + 16 : n + 32]
        out += [a * cos - b * sin, b * cos + a * sin, mixed[n + 32 : n + 64]]
    return jnp.concatenate(out + [mixed[128:]], 0).astype(BF)


def project_kernel(ids, msg, cos, sin, x_ref, hidden, away, vec, b1, w_qkv, bias, w_away, raw, xs, sems):
    h, zc = ids[0], 2 * ids[1] + ids[2]
    start_rows_in(x_ref, xs, sems)
    for s in range(16):
        w_qkv[s * 64 : (s + 1) * 64, :] = msg[s, 0:64, :]
        w_away[s * 64 : (s + 1) * 64, :] = msg[s, 0:64, 192:384]
        v = msg[s, 64:80, 0:64].astype(F32)
        raw[s] = v
        vec[:, s * 64 : (s + 1) * 64] = v
    own, oth = h * 8 + zc, (1 - h) * 8 + zc
    v_own, v_oth = raw[own], raw[oth]
    bias[...] = jnp.concatenate(
        [v_own[t : t + 1, :] for t in range(3)] + [v_oth[t : t + 1, :] for t in range(3)], 1
    )
    for n, i in enumerate((own, oth)):
        for j in range(4):
            at = n * 256 + j * 64
            b1[:, at : at + 64] = raw[4 * lax.rem(i, 4) + j, pl.ds(4 + i // 4, 1), :]
    gain, shift = vec[9:10, :], vec[10:11, :]

    def pair(n, unused):
        for i in range(2):
            wait_piece(xs, sems, 2 * n + i)
        at = pl.ds(pl.multiple_of(n * 512, 512), 512)
        normed, unused_inverse = normalize(xs[at, :].astype(F32))
        hid = (normed * gain + shift).astype(BF)
        hidden[at, :] = hid
        mixed = (dot(hid, w_away[...]) + bias[:, 192:384]).T
        away[:, at] = rotate(cos[:, at], sin[:, at], mixed)
        return unused

    lax.fori_loop(0, 4, pair, 0)


def project(ids, msg, cos, sin, x_all, *ties):
    outs = [
        ((2048, 1024), BF),
        ((192, 2048), BF),
        ((16, 1024), F32),
        ((1, 512), F32),
        ((1024, 384), BF),
        ((1, 384), F32),
    ]
    scratch = [pltpu.VMEM((1024, 192), BF), pltpu.VMEM((16, 16, 64), F32), pltpu.VMEM((2048, 1024), BF), DMA((8,))]
    inputs = (ids, msg, cos, sin, x_all)
    return call(
        project_kernel, "project", inputs, [SM, VM, VM, VM, ANY], outs, scratch,
        4 * 2048 * 1024 * 384, 12 << 20, ties,
    )


def here_kernel(hid_ref, w_qkv, bias, cos, sin, here, hs, sems):
    start_rows_in(hid_ref, hs, sems)

    def pair(n, unused):
        for i in range(2):
            wait_piece(hs, sems, 2 * n + i)
        at = pl.ds(pl.multiple_of(n * 512, 512), 512)
        mixed = (dot(hs[at, :], w_qkv[:, 0:192]) + bias[:, 0:192]).T
        here[:, at] = rotate(cos[:, at], sin[:, at], mixed)
        return unused

    lax.fori_loop(0, 4, pair, 0)


def project_here(hidden, w_qkv, bias, cos, sin, *ties):
    scratch = [pltpu.VMEM((2048, 1024), BF), DMA((8,))]
    return call(
        here_kernel, "project_here", (hidden, w_qkv, bias, cos, sin), [ANY] + [VM] * 4,
        [((192, 2048), BF)], scratch, 2 * 2048 * 1024 * 192, 8 << 20, ties,
    )[0]


ROOT = 0.7978845608028654


def units_kernel(hid_ref, w1, b1, act_ref, slope_ref, hs, act, slope, sems, asems, ssems):
    start_rows_in(hid_ref, hs, sems)

    def block(n, unused):
        for i in range(2):
            wait_piece(hs, sems, 2 * n + i)
        at = pl.ds(pl.multiple_of(n * 512, 512), 512)
        u = dot(hs[at, :], w1[...]) + b1[...]
        square = u * u
        th = jnp.tanh(ROOT * u * (1.0 + 0.044715 * square))
        half = 0.5 * (1.0 + th)
        act[at, :] = (u * half).astype(BF)
        back = half + 0.5 * u * (1.0 - th * th) * (ROOT * (1.0 + 3.0 * 0.044715 * square))
        slope[at, :] = back.astype(BF)
        start_block(act, n, act_ref, asems)
        start_block(slope, n, slope_ref, ssems)
        return unused

    lax.fori_loop(0, 4, block, 0)
    wait_blocks(act, act_ref, asems)
    wait_blocks(slope, slope_ref, ssems)


def units(hidden, w1, b1, *ties):
    outs = [((2048, 512), BF), ((2048, 512), BF)]
    scratch = [pltpu.VMEM((2048, 1024), BF)] + [pltpu.VMEM((2048, 512), BF)] * 2
    scratch += [DMA((8,)), DMA((4,)), DMA((4,))]
    return call(
        units_kernel, "units", (hidden, w1, b1), [ANY, VM, VM], outs, scratch,
        2 * 2048 * 1024 * 512, 11 << 20, ties, (ANY, ANY),
    )


def along_rows(w, grad, bias):
    first = jnp.sum(w * grad, 1, keepdims=True)
    second = jnp.sum(w * bias, 1, keepdims=True)
    lane = lax.broadcasted_iota(jnp.int32, (1024, 128), 1)
    return jnp.where(lane == 0, first, second).T[0:2, :]


def units_back_kernel(ids, hid_ref, act_ref, slope_ref, rows, rows_x, w1, g_ref, *refs):
    part_out, part_in, msg, gb1, along, do_here, do_away = refs[:7]
    hs, gs, act, ss, out, back, w2, wd, acc1, acc2, sems, hsems, asems, ssems, osems, bsems = refs[7:]
    h = ids[0]
    start_rows_in(g_ref, gs, sems)
    start_rows_in(act_ref, act, asems)
    start_rows_in(slope_ref, ss, ssems)
    start_rows_in(hid_ref, hs, hsems)
    w2[0:256, :] = rows[0:256, :]
    w2[256:512, :] = rows_x[0:256, :]
    wd[0:64, :] = rows[256:320, :]
    wd[64:128, :] = rows_x[256:320, :]
    acc1[...] = jnp.zeros_like(acc1)
    acc2[...] = jnp.zeros_like(acc2)
    gb1[...] = jnp.zeros_like(gb1)

    def block(n, unused):
        for i in range(2):
            wait_piece(gs, sems, 2 * n + i)
            wait_piece(act, asems, 2 * n + i)
            wait_piece(ss, ssems, 2 * n + i)
            wait_piece(hs, hsems, 2 * n + i)
        at = pl.ds(pl.multiple_of(n * 512, 512), 512)
        hid, g = hs[at, :], gs[at, :]
        back_b = (dot(g, w2[...], NT) * ss[at, :].astype(F32)).astype(BF)
        back[at, :] = dot(back_b, w1[...], NT).astype(BF)
        start_block(back, n, part_in, bsems)
        out[at, :] = dot(act[at, :], w2[...]).astype(BF)
        start_block(out, n, part_out, osems)
        gb1[...] += jnp.sum(back_b.astype(F32), 0, keepdims=True)
        both = dot(g, wd[...], NT).T.astype(BF)
        do_here[:, at] = both[:64]
        do_away[:, at] = both[64:]
        acc2[...] += dot(act[at, :], g, TN)
        acc1[...] += dot(hid, back_b, TN)
        return unused

    lax.fori_loop(0, 4, block, 0)
    along[...] = along_rows(w1[...].astype(F32), acc1[...], gb1[...])
    for p in range(8):
        for hd in range(2):
            rows_at = slice(hd * 512 + p * 64, hd * 512 + p * 64 + 64)
            for part in range(2):
                hh = h if part == 0 else 1 - h
                msg[2 * p + hd, pl.ds(pl.multiple_of(hh * 64, 64), 64), :] = acc1[
                    rows_at, part * 256 : part * 256 + 256
                ].astype(BF)
        for part in range(2):
            hh = h if part == 0 else 1 - h
            for q in range(4):
                msg[2 * p + hh, 128 + q * 32 : 160 + q * 32, :] = acc2[
                    part * 256 + p * 32 : part * 256 + p * 32 + 32, q * 256 : q * 256 + 256
                ].astype(BF)
    wait_blocks(back, part_in, bsems)
    wait_blocks(out, part_out, osems)


def units_back(ids, hidden, act, slope, rows, rows_x, w1, g_all, *ties):
    outs = [((2048, 1024), BF)] * 2 + [((16, 256, 256), BF), ((1, 512), F32), ((2, 1024), F32)]
    outs += [((64, 2048), BF)] * 2
    scratch = [
        pltpu.VMEM((2048, 1024), BF),
        pltpu.VMEM((2048, 1024), BF),
        pltpu.VMEM((2048, 512), BF),
        pltpu.VMEM((2048, 512), BF),
        pltpu.VMEM((2048, 1024), BF),
        pltpu.VMEM((2048, 1024), BF),
        pltpu.VMEM((512, 1024), BF),
        pltpu.VMEM((128, 1024), BF),
        pltpu.VMEM((1024, 512), F32),
        pltpu.VMEM((512, 1024), F32),
        DMA((8,)),
        DMA((8,)),
        DMA((8,)),
        DMA((8,)),
        DMA((4,)),
        DMA((4,)),
    ]
    return call(
        units_back_kernel, "units_back", (ids, hidden, act, slope, rows, rows_x, w1, g_all),
        [SM, ANY, ANY, ANY, VM, VM, VM, ANY], outs, scratch, 10 * 2048 * 1024 * 512, 18 << 20, ties,
        (ANY, ANY) + (VM,) * 5,
    )


def start_rows_out(src, n, to, sems):
    at = pl.ds(n * 512, 512)
    copy = pltpu.make_async_copy(src.at[at], to.at[at], sems.at[n])
    copy.start()
    return copy


def out_kernel(ids, part_ref, rows, rows_x, o_here, o_came, g_ref, total, gd, gs, both, part, out, sems, psems, osems):
    h = ids[0]
    start_rows_in(part_ref, part, psems)
    start_rows_in(g_ref, gs, sems)
    both[0:64, :] = o_here[...]
    both[64:128, :] = o_came[...]
    wd = jnp.concatenate([rows[256:320, :], rows_x[256:320, :]], 0)
    copies = []
    for n in range(4):
        at = slice(n * 512, n * 512 + 512)
        more = dot(both[:, at], wd, TN)
        wait_piece(part, psems, 2 * n)
        wait_piece(part, psems, 2 * n + 1)
        out[at, :] = (part[at, :].astype(F32) + more).astype(BF)
        copies.append(start_rows_out(out, n, total, osems))
    for i in range(8):
        wait_piece(gs, sems, i)
    grad = dot(both[...], gs[...]).astype(BF)
    gd[h] = grad[:64]
    gd[1 - h] = grad[64:]
    for copy in copies:
        copy.wait()


def out_part(ids, part, rows, rows_x, o_here, o_came, g_all, *ties):
    outs = [((2048, 1024), BF), ((2, 64, 1024), BF)]
    scratch = [
        pltpu.VMEM((2048, 1024), BF),
        pltpu.VMEM((128, 2048), BF),
        pltpu.VMEM((2048, 1024), BF),
        pltpu.VMEM((2048, 1024), BF),
        DMA((8,)),
        DMA((8,)),
        DMA((4,)),
    ]
    return call(
        out_kernel, "out_part", (ids, part, rows, rows_x, o_here, o_came, g_all),
        [SM, ANY] + [VM] * 4 + [ANY], outs, scratch, 4 * 2048 * 1024 * 128, 12 << 20, ties,
        (ANY, VM),
    )


def last_kernel(
    ids, d_here, d_came, w_qkv, part_ref, hid_ref, g_own, gb1, gd, along, vin, total, msg,
    hs, part, out, both, gq, vec, sems, psems, osems,
):
    h, zc = ids[0], 2 * ids[1] + ids[2]
    start_rows_in(part_ref, part, psems)
    start_rows_in(hid_ref, hs, sems)
    both[0:192, :] = d_here[...]
    both[192:384, :] = d_came[...]
    copies = []
    for n in range(4):
        at = slice(n * 512, n * 512 + 512)
        more = dot(both[:, at].T, w_qkv[...], NT)
        wait_piece(part, psems, 2 * n)
        wait_piece(part, psems, 2 * n + 1)
        out[at, :] = (part[at, :].astype(F32) + more).astype(BF)
        copies.append(start_rows_out(out, n, total, osems))
    ones = jnp.ones((8, 2048), BF)
    bias = dot(ones, both[...], NT)[0:1]
    for i in range(8):
        wait_piece(hs, sems, i)
    grad = dot(both[...], hs[...])
    turned = grad.T
    sums = along[...] + along_rows(w_qkv[...].astype(F32), turned, bias)
    gq[pl.ds(pl.multiple_of(h * 192, 64), 192), :] = grad[:192]
    gq[pl.ds(pl.multiple_of((1 - h) * 192, 64), 192), :] = grad[192:]
    own, oth = h * 8 + zc, (1 - h) * 8 + zc
    lane = lax.broadcasted_iota(jnp.int32, (1, 1024), 1)
    out_sum = jnp.sum(g_own[...].astype(F32), 0, keepdims=True)
    rows = []
    for t in range(3):
        a = jnp.concatenate([bias[:, t * 64 : t * 64 + 64]] * 16, 1)
        b = jnp.concatenate([bias[:, 192 + t * 64 : 256 + t * 64]] * 16, 1)
        rows.append(jnp.where(lane // 64 == own, a, 0.0) + jnp.where(lane // 64 == oth, b, 0.0))
    rows.append(out_sum)
    a = jnp.concatenate([gb1[:, 0:256]] * 4, 1)
    b = jnp.concatenate([gb1[:, 256:512]] * 4, 1)
    for r in range(4):
        block = lane // 256 + 4 * r
        rows.append(jnp.where(block == own, a, 0.0) + jnp.where(block == oth, b, 0.0))
    shift_sum = sums[1:2, :]
    gain_sum = (sums[0:1, :] - vin[10:11, :] * shift_sum) / vin[9:10, :]
    rows += [out_sum, gain_sum, shift_sum]
    for r, row in enumerate(rows):
        vec[r : r + 1, :] = row
    flat = gq[...].T
    zeros = jnp.zeros((8, 64), F32)
    for p in range(8):
        for hd in range(2):
            at = hd * 512 + p * 64
            msg[2 * p + hd, 0:64, :] = flat[at : at + 64, :].astype(BF)
            cols = slice((hd * 8 + p) * 64, (hd * 8 + p) * 64 + 64)
            v0 = vec[0:8, cols]
            v1 = vec[8:16, cols]
            vrows = jnp.concatenate([v0, zeros, v1, zeros, zeros, zeros], 1)
            d = gd[hd, p * 8 : p * 8 + 8, :].astype(F32)
            d2 = jnp.concatenate([d[:, 768:1024], jnp.zeros((8, 128), F32)], 1)
            tail = jnp.concatenate([vrows, d[:, 0:384], d[:, 384:768], d2], 0)
            msg[2 * p + hd, 64:96, :] = tail.astype(BF)
    for copy in copies:
        copy.wait()


def last_part(ids, d_here, d_came, w_qkv, part, hidden, g_own, gb1, gd, along, vec, *ties):
    scratch = [
        pltpu.VMEM((2048, 1024), BF),
        pltpu.VMEM((2048, 1024), BF),
        pltpu.VMEM((2048, 1024), BF),
        pltpu.VMEM((384, 2048), BF),
        pltpu.VMEM((384, 1024), F32),
        pltpu.VMEM((16, 1024), F32),
        DMA((8,)),
        DMA((8,)),
        DMA((4,)),
    ]
    return call(
        last_kernel, "last_part",
        (ids, d_here, d_came, w_qkv, part, hidden, g_own, gb1, gd, along, vec),
        [SM] + [VM] * 3 + [ANY] * 2 + [VM] * 5, [((2048, 1024), BF), ((16, 96, 384), BF)], scratch,
        4 * 2048 * 1024 * 384, 16 << 20, ties, (ANY, VM),
    )


SWAP = [(0, 1), (1, 0)]
GROUP = ("z", "core")
MODEL = ("xhi", "z", "core")
BATCH = ("xlo", "y")
SUM = ("xlo", "y", "xhi")


def swap_core(v):
    return lax.ppermute(v, "core", SWAP)


def swap_x(v):
    return lax.ppermute(v, "xhi", SWAP)


def group_sum(v):
    return lax.psum_scatter(v, GROUP, scatter_dimension=0, tiled=True)


def sum_kernel(n, parts, lo, hi, ps, sems):
    for i in range(8):
        at = pl.ds(2 * i, 2)
        pltpu.make_async_copy(parts.at[at], ps.at[at], sems.at[i]).start()
    total = None
    for i in range(8):
        at = pl.ds(2 * i, 2)
        pltpu.make_async_copy(ps.at[at], ps.at[at], sems.at[i]).wait()
        pair = ps[2 * i].astype(F32) + ps[2 * i + 1].astype(F32)
        total = pair if total is None else total + pair
    lo[...] = total[:n].astype(BF)
    hi[...] = total[n:].astype(BF)


def sum_parts(parts, n, *ties):
    rows, columns = parts.shape[1:]
    outs = [((n, columns), BF), ((rows - n, columns), BF)]
    scratch = [pltpu.VMEM(parts.shape, BF), DMA((8,))]
    return call(functools.partial(sum_kernel, n), "sum_parts", (parts,), [ANY], outs, scratch, 0, 2 << 20, ties)


def fan_kernel(lo, hi, out):
    n = lo.shape[0]
    for p in range(8):
        out[p, 0:n, :] = lo[...]
        out[p, n:, :] = hi[...]


def fan(lo, hi, *ties):
    shape = (8, lo.shape[0] + hi.shape[0], lo.shape[1])
    return call(fan_kernel, "fan", (lo, hi), [VM] * 2, [(shape, BF)], [], 0, 2 << 20, ties)[0]


def turn(v):
    return lax.ppermute(v, ("xlo", "y", "z", "core"), [(p * 8 + m, m * 8 + p) for p in range(8) for m in range(8)])


def tables(positions):
    freqs = 10000.0 ** (-(jnp.arange(ROT // 2, dtype=F32) * 2.0) / ROT)
    angles = positions.astype(F32)[None, :] * freqs[:, None]
    return (jnp.cos(angles), jnp.sin(angles))


def adamw(master, grad, first, second, rate):
    first_new = 0.9 * first + 0.1 * grad
    second_new = 0.95 * second + 0.05 * grad * grad
    first_hat = first_new / (1.0 - 0.9**STEP)
    second_hat = second_new / (1.0 - 0.95**STEP)
    fresh = master - rate * (first_hat / (jnp.sqrt(second_hat) + 1e-08) + 0.1 * master)
    return (fresh, first_new, second_new)


RATE = 2.0 * D ** (-0.5)
RATE_DOWN = 2.0 * FF ** (-0.5)


def update_units_kernel(early, w1, m1, v1, w2, m2, v2, w1n, m1n, v1n, w2n, m2n, v2n):
    for p in range(8):
        for hh in range(2):
            at = slice((hh * 8 + p) * 256, (hh * 8 + p) * 256 + 256)
            grad = early[p, hh * 64 : hh * 64 + 64, :].astype(F32)
            w1n[:, at], m1n[:, at], v1n[:, at] = adamw(w1[:, at], grad, m1[:, at], v1[:, at], RATE)
        for q in range(4):
            at = (slice(p * 32, p * 32 + 32), slice(q * 256, q * 256 + 256))
            grad = early[p, 128 + q * 32 : 160 + q * 32, :].astype(F32)
            w2n[at], m2n[at], v2n[at] = adamw(w2[at], grad, m2[at], v2[at], RATE_DOWN)


def update_units(early, *state, ties=()):
    outs = [((64, 4096), F32)] * 3 + [((256, 1024), F32)] * 3
    return call(update_units_kernel, "update_units", (early,) + state, [VM] * 7, outs, [], 0, 13 << 20, ties)


def update_heads_kernel(late, w, m, v, wd, md, vd, vec, mv, vv, wn, mn, vn, wdn, mdn, vdn, vecn, mvn, vvn, gq, gd):
    for zc in range(8):
        for hh in range(2):
            for t in range(3):
                col = t * 1024 + (hh * 8 + zc) * 64
                at = hh * 192 + t * 64
                gq[:, col : col + 64] = late[zc, 0:64, at : at + 64].astype(F32)
        rows = late[zc, 64:96, :].astype(F32)
        gd[zc * 8 : zc * 8 + 8, 0:384] = rows[8:16]
        gd[zc * 8 : zc * 8 + 8, 384:768] = rows[16:24]
        gd[zc * 8 : zc * 8 + 8, 768:1024] = rows[24:32, 0:256]
        total = rows[0:8] if zc == 0 else total + rows[0:8]
    grad = jnp.concatenate([total[:, 0:64], total[0:3, 128:192]], 0)
    wn[...], mn[...], vn[...] = adamw(w[...], gq[...], m[...], v[...], RATE)
    wdn[...], mdn[...], vdn[...] = adamw(wd[...], gd[...], md[...], vd[...], RATE)
    vecn[...], mvn[...], vvn[...] = adamw(vec[...], grad, mv[...], vv[...], 0.3)


def update_heads(late, *state):
    outs = [((64, 3072), F32)] * 3 + [((64, 1024), F32)] * 3 + [((11, 64), F32)] * 3
    scratch = [pltpu.VMEM((64, 3072), F32), pltpu.VMEM((64, 1024), F32)]
    return call(update_heads_kernel, "update_heads", (late,) + state, [VM] * 10, outs, scratch, 0, 7 << 20)


def input_kernel(came, x, g, vec, out):
    total = came[...].astype(F32)
    normed, inverse = normalize(x[...].astype(F32))
    back = total * vec[9:10, :]
    mean = jnp.mean(back, -1, keepdims=True)
    along = jnp.mean(back * normed, -1, keepdims=True)
    out[...] = (g[...].astype(F32) + inverse * (back - mean - normed * along)).astype(BF)


def input_part(blocks, x, g, vec, *ties):
    inputs = (blocks, x, g, vec)
    return call(input_kernel, "input_part", inputs, [VM] * 4, [((256, 1024), BF)], [], 0, 4 << 20, ties)[0]


def output_kernel(came, x, vec, out):
    total = came[...].astype(F32)
    out[...] = (x[...].astype(F32) + total + (vec[3:4, :] + vec[8:9, :])).astype(BF)


def output_part(blocks, x, vec, *ties):
    inputs = (blocks, x, vec)
    return call(output_kernel, "output_part", inputs, [VM] * 3, [((256, 1024), BF)], [], 0, 4 << 20, ties)[0]


def local(
    tokens,
    cotangent,
    qkv_weight,
    dense_weight,
    fc1_weight,
    fc2_weight,
    vectors,
    qkv_first,
    dense_first,
    fc1_first,
    fc2_first,
    vectors_first,
    qkv_second,
    dense_second,
    fc1_second,
    fc2_second,
    vectors_second,
):
    h, z, c = lax.axis_index("xhi"), lax.axis_index("z"), lax.axis_index("core")
    ids = jnp.stack([h, z, c, lax.axis_index(BATCH)]).astype(jnp.int32)
    x_own = tokens[0]
    g_own = cotangent[0]

    cos_all, sin_all = tables(jnp.arange(S, dtype=jnp.int32))
    cos_here = lax.dynamic_slice_in_dim(cos_all, h * (S // 2), S // 2, 1)
    sin_here = lax.dynamic_slice_in_dim(sin_all, h * (S // 2), S // 2, 1)
    cos_away = lax.dynamic_slice_in_dim(cos_all, (1 - h) * (S // 2), S // 2, 1)
    sin_away = lax.dynamic_slice_in_dim(sin_all, (1 - h) * (S // 2), S // 2, 1)

    x_all = lax.all_gather(x_own, GROUP, axis=0, tiled=True)
    msg, rows = pack(qkv_weight, vectors, fc2_weight, dense_weight)
    msg = lax.all_to_all(msg, MODEL, 0, 0, tiled=True)
    rows_x = swap_x(rows)
    up_msg = pack_up(fc1_weight, cos_here, sin_here, cos_away, sin_away, ids)
    w1 = lax.all_to_all(hold(up_msg, msg), MODEL, 0, 0, tiled=True).reshape(1024, 512)
    g_all = lax.all_gather(hold(g_own, x_all, w1), GROUP, axis=0, tiled=True)
    hidden, away, vec, b1, w_qkv, bias = project(
        ids, msg, cos_here, sin_here, x_all
    )
    came = swap_x(away)
    here = project_here(hidden, w_qkv, bias, cos_here, sin_here, away)
    act, slope = units(hidden, w1, b1, here)
    o_full, lse, o_here, o_away = attend(ids, here, came, act)
    o_came = swap_x(o_away)
    part_out, part_in, early, gb1, along, do_here, do_away = units_back(
        ids, hidden, act, slope, rows, rows_x, w1, g_all, o_away
    )
    do_came = swap_x(do_away)
    total, gd = out_part(
        ids, part_out, rows, rows_x, o_here, o_came, g_all
    )
    out_sum = group_sum(hold(total, do_came))
    early = lax.all_to_all(hold(early, do_came, gd), SUM, 0, 0, tiled=True)
    d_away, *partial = attend_back_far(
        ids, here, came, do_here, do_came, o_full, lse, cos_away, sin_away, gd
    )
    d_came = swap_x(d_away)
    d_here = attend_back_near(
        ids, here, do_here, o_full, lse, cos_here, sin_here, partial, d_away
    )
    total, late = last_part(
        ids, d_here, d_came, w_qkv, part_in, hidden, g_own, gb1, gd, along, vec, early
    )
    hidden_sum = group_sum(total)
    early_turn, early_stay = sum_parts(early, 128, late)
    early_turn = turn(early_turn)
    early = fan(early_turn, early_stay)
    late = lax.all_to_all(late, SUM, 0, 0, tiled=True)
    early = lax.all_to_all(hold(early, late), BATCH, 0, 0, tiled=True)
    late_turn, late_stay = sum_parts(late, 72, early_stay)
    late = fan(turn(late_turn), late_stay)
    late = lax.all_to_all(hold(late, early), BATCH, 0, 0, tiled=True)
    new1 = update_units(
        early,
        *(fc1_weight, fc1_first, fc1_second, fc2_weight, fc2_first, fc2_second),
    )
    output = output_part(out_sum, x_own, vec, new1[0])
    input_grad = input_part(hidden_sum, x_own, g_own, vec, output)
    new2 = update_heads(
        hold(late, input_grad),
        *(qkv_weight, qkv_first, qkv_second),
        *(dense_weight, dense_first, dense_second),
        *(vectors, vectors_first, vectors_second),
    )
    news = [(new2[j], new2[3 + j], new1[j], new1[3 + j], new2[6 + j]) for j in range(3)]
    return (output[None], input_grad[None]) + news[0] + news[1] + news[2]


def solution(mesh):
    fine = Mesh(mesh.devices.reshape(2, 4, 2, 4, 2), ("xlo", "y", "xhi", "z", "core"))
    dp, fsdp = ("xlo", "y"), ("xhi", "z", "core")
    token = P(dp, fsdp, None)
    row = P(fsdp, None)
    column = P(None, fsdp)
    params = (row, row, row, row, column)
    return jax.shard_map(
        local,
        mesh=fine,
        in_specs=(token, token) + params * 3,
        out_specs=(token, token) + params * 3,
        check_vma=False,
    )
```
